32 devices in a mesh: tm: 32 (over z, y, x, core).
Axes of the slice: x: 2, y: 2, z: 4, core: 2. Of those that a mesh axis runs over, the one named last changes fastest.
Arguments:
- diag_blocks: float32 [128, 512, 512], P('tm'), as said below
- lower_blocks: float32 [128, 512, 512], P('tm')
- arrow_blocks: float32 [128, 64, 512], P('tm')
- tip_block: float32 [64, 64], replicated, as said below
Outputs:
- pair_fronts: float32 [17408, 1088], P('tm')
- tip_schur: float32 [64, 64], replicated
Inputs may be any that keep to these rules, and one draw needn't show every extreme that they name: `diag_blocks`: every block is symmetric, and the matrix that Q forms over all time blocks is positive definite. `tip_block`: symmetric.
All inputs are finite; a program needn't handle non-finite values.
Results may differ from the reference program's by a relative error of at most 0.0003.
Values sent between devices are 32-bit elements; how exact they have to be, the bound alone decides.
No kernel may reach another device: no remote copies, remote signals or barrier semaphores. Data moves between devices by JAX's collectives and lax.ppermute only.
A program may use at most 128 MiB of HBM per device.

```python
import math
import jax
import jax.numpy as jnp
from jax import lax

B = 512
A = 64
P_SIZE = 4
TIMES = 128
PAIRS = 16
FRONT = 1088


dense_share = 0.03


def coupled_fields(key, edge_low, edge_high, nugget_low, nugget_high, rate_low, rate_high):
    place_key, edge_key, dense_key, nugget_key, rate_key = jax.random.split(key, 5)
    cycle_place = jax.random.permutation(place_key, B)
    offset = (cycle_place[None, :] - cycle_place[:, None]) % B
    forward = (offset == 1).astype(jnp.float32)
    edges = jnp.exp(jax.random.uniform(edge_key, (TIMES, B), jnp.float32, math.log(edge_low), math.log(edge_high)))
    adjacency = forward[None, :, :] * edges[:, :, None] + jnp.swapaxes(forward, 0, 1)[None, :, :] * edges[:, None, :]
    identity = jnp.eye(B, dtype=jnp.float32)
    uniform_part = jax.random.uniform(dense_key, (TIMES, B, B), jnp.float32)
    dense_links = (uniform_part + jnp.swapaxes(uniform_part, 1, 2)) * (dense_share / B) * (1.0 - identity)
    nugget = jax.random.uniform(nugget_key, (TIMES, B), jnp.float32, nugget_low, nugget_high)
    degree = jnp.sum(adjacency, axis=2)
    center = nugget + degree + 2.0 * dense_share
    spatial = identity * center[:, None, :] - adjacency - dense_links
    rates = jax.random.uniform(rate_key, (TIMES,), jnp.float32, rate_low, rate_high)
    return (spatial, rates)


def draw_diag_blocks(key, part):
    spatial, rates = coupled_fields(key, 0.5, 1.5, 0.01, 0.05, 0.8, 0.9)
    damping_low, damping_high = (0.02, 0.06)
    key = jax.random.fold_in(key, 11)
    damping = jax.random.uniform(key, (TIMES, B), jnp.float32, damping_low, damping_high)
    previous = jnp.concatenate([jnp.zeros((1, B, B), jnp.float32), spatial[:-1]], axis=0)
    identity = jnp.eye(B, dtype=jnp.float32)
    return previous + (rates * rates)[:, None, None] * spatial + identity * damping[:, None, :]


def draw_lower_blocks(key, part):
    spatial, rates = coupled_fields(key, 0.5, 1.5, 0.01, 0.05, 0.8, 0.9)
    return -rates[:, None, None] * spatial


def draw_arrow_blocks(key, part):
    key = jax.random.fold_in(key, 23)
    first_key = jax.random.fold_in(key, 0)
    position = jnp.arange(TIMES, dtype=jnp.float32) / max(TIMES - 1, 1)
    rising = (1.0 + 2.0 * position)[:, None, None] * (0.12 / math.sqrt(B))
    values = jnp.clip(jax.random.normal(first_key, (TIMES, A, B), jnp.float32), -5.0, 5.0)
    return values * rising


def draw_tip_block(key, part):
    key = jax.random.fold_in(key, 37)
    first_key, second_key = jax.random.split(key)
    noise = jnp.clip(jax.random.normal(first_key, (A, A), jnp.float32), -4.0, 4.0)
    center = jax.random.uniform(second_key, (A,), jnp.float32, 3.0, 6.0)
    identity = jnp.eye(A, dtype=jnp.float32)
    return (noise + noise.T) * (0.3 / math.sqrt(A)) * (1.0 - identity) + identity * center[None, :]


def setup_inputs(seed: int = 0) -> dict:
    key_list = jax.random.split(jax.random.key(seed), 5)
    diag_blocks = draw_diag_blocks(jax.random.fold_in(key_list[4], 71), 0)
    lower_blocks = draw_lower_blocks(jax.random.fold_in(key_list[4], 71), 0)
    arrow_blocks = draw_arrow_blocks(jax.random.fold_in(key_list[4], 71), 0)
    tip_block = draw_tip_block(jax.random.fold_in(key_list[4], 71), 0)
    return {"diag_blocks": diag_blocks, "lower_blocks": lower_blocks, "arrow_blocks": arrow_blocks, "tip_block": tip_block}


highest = lax.Precision.HIGHEST

def eliminate(pivot_block, coupling, outer_block):
    factor = jnp.linalg.cholesky(pivot_block)
    scaled = lax.linalg.triangular_solve(factor, coupling, left_side=True, lower=True)
    return outer_block - jnp.dot(scaled.T.astype(jnp.float32), scaled.astype(jnp.float32), precision=highest, preferred_element_type=jnp.float32)

def partition_front(diag_part, lower_part, arrow_part):
    count = diag_part.shape[0]
    width = diag_part.shape[1]
    tip_width = arrow_part.shape[1]
    square_zero = jnp.zeros((width, width), jnp.float32)
    front = jnp.block([[diag_part[0], lower_part[0].T, arrow_part[0].T], [lower_part[0], diag_part[1], arrow_part[1].T], [arrow_part[0], arrow_part[1], jnp.zeros((tip_width, tip_width), jnp.float32)]])
    for index in range(1, count - 1):
        current = front[width:2 * width]
        coupling = jnp.concatenate([current[:, :width], lower_part[index].T, current[:, 2 * width:]], axis=1)
        outer_block = jnp.block([[front[:width, :width], square_zero, front[:width, 2 * width:]], [square_zero, diag_part[index + 1], arrow_part[index + 1].T], [front[2 * width:, :width], arrow_part[index + 1], front[2 * width:, 2 * width:]]])
        front = eliminate(current[:, width:2 * width], coupling, outer_block)
    return front

def condense(front, link):
    width = link.shape[0]
    tip_width = front.shape[0] - 2 * width
    square_zero = jnp.zeros((width, width), jnp.float32)
    side_zero = jnp.zeros((width, tip_width), jnp.float32)
    right_rows = front[width:2 * width]
    coupling = jnp.concatenate([right_rows[:, :width], link.T, right_rows[:, 2 * width:]], axis=1)
    outer_block = jnp.block([[front[:width, :width], square_zero, front[:width, 2 * width:]], [square_zero, square_zero, side_zero], [front[2 * width:, :width], side_zero.T, front[2 * width:, 2 * width:]]])
    return eliminate(right_rows[:, width:2 * width], coupling, outer_block)

def joined_system(condensed, right_front, width):
    double = 2 * width
    square_zero = jnp.zeros((width, width), jnp.float32)
    pivot_block = condensed[width:double, width:double] + right_front[:width, :width]
    coupling = jnp.concatenate([condensed[width:double, :width], right_front[:width, width:double], condensed[width:double, double:] + right_front[:width, double:]], axis=1)
    outer_block = jnp.block([[condensed[:width, :width], square_zero, condensed[:width, double:]], [square_zero, right_front[width:double, width:double], right_front[width:double, double:]], [condensed[double:, :width], right_front[double:, width:double], condensed[double:, double:] + right_front[double:, double:]]])
    return (pivot_block, coupling, outer_block)

def merge_front(condensed, right_front, width):
    pivot_block, coupling, outer_block = joined_system(condensed, right_front, width)
    return eliminate(pivot_block, coupling, outer_block)

def reference(diag_blocks, lower_blocks, arrow_blocks, tip_block):
    pair_diag = diag_blocks.reshape(PAIRS, 2, P_SIZE, B, B)
    pair_lower = lower_blocks.reshape(PAIRS, 2, P_SIZE, B, B)
    pair_arrow = arrow_blocks.reshape(PAIRS, 2, P_SIZE, A, B)

    def one_pair(items):
        diag_pair, lower_pair, arrow_pair = items
        left_front = partition_front(diag_pair[0], lower_pair[0], arrow_pair[0])
        right_front = partition_front(diag_pair[1], lower_pair[1], arrow_pair[1])
        return merge_front(condense(left_front, lower_pair[0][P_SIZE - 1]), right_front, B)
    merged = lax.map(one_pair, (pair_diag, pair_lower, pair_arrow))
    pair_fronts = merged.reshape(PAIRS * FRONT, FRONT)
    tip_schur = tip_block + jnp.sum(merged[:, 2 * B:, 2 * B:], axis=0)
    return (pair_fronts, tip_schur)
```

```python
import functools

import jax
import jax.numpy as jnp
from jax import lax
from jax.experimental import pallas as pl
from jax.experimental.pallas import tpu as pltpu
from jax.sharding import PartitionSpec as P

F32 = jnp.float32
BF16 = jnp.bfloat16
SUB = 8
LANES = 128
HALF = 256
NN = (((1,), (0,)), ((), ()))
NT = (((1,), (1,)), ((), ()))


def split(value):
    high = value.astype(BF16)
    return high, (value - high.astype(F32)).astype(BF16)


def dot3(left, right, dims=NN):
    one = functools.partial(lax.dot_general, dimension_numbers=dims, preferred_element_type=F32)
    return one(left[0], right[0]) + (one(left[0], right[1]) + one(left[1], right[0]))


def row_of(value, index):
    return jnp.broadcast_to(value[index : index + 1, :], (SUB, LANES))


def column_of(value, index):
    return jnp.broadcast_to(value[:, index : index + 1], (SUB, LANES))


def panel_step(state):
    rows, columns = list(state[:16]), list(state[16:])
    sub = lax.broadcasted_iota(jnp.int32, (SUB, LANES), 0)
    lane = lax.broadcasted_iota(jnp.int32, (SUB, LANES), 1)
    panel = lane < SUB
    top = jnp.where(panel, jnp.where(lane == sub, 1.0, 0.0).astype(F32), rows[0])
    for pivot in range(SUB):
        inverse = pl.reciprocal(row_of(columns[pivot], pivot))
        here = sub == pivot
        for index in range(pivot + 1, SUB):
            scaled = row_of(columns[index], pivot) * inverse
            columns[index] = jnp.where(here, scaled, columns[index] - columns[pivot] * scaled)
        scaled = row_of(top, pivot) * inverse
        top = jnp.where(here, scaled, top - columns[pivot] * scaled)
    top_rows = [row_of(top, index) for index in range(SUB)]
    fresh = []
    for index in range(1, 16):
        terms = [column_of(rows[index], k) * top_rows[k] for k in range(SUB)]
        while len(terms) > 1:
            terms = [terms[k] + terms[k + 1] for k in range(0, len(terms), 2)]
        fresh.append(jnp.where(panel, 0.0, rows[index]) - terms[0])
    columns = [column_of(fresh[0], SUB + k) for k in range(SUB)]
    fresh.append(top)
    rows = [pltpu.roll(value, LANES - SUB, 1) for value in fresh]
    return tuple(rows + columns)


def invert_128(blocks):
    states = []
    for block in blocks:
        rows = [block[SUB * k : SUB * (k + 1), :] for k in range(16)]
        states.append(tuple(rows + [column_of(rows[0], k) for k in range(SUB)]))
    states = lax.fori_loop(0, 16, lambda _, carry: tuple(panel_step(s) for s in carry), tuple(states))
    return [jnp.concatenate(state[:16], axis=0) for state in states]


def invert_256(blocks):
    firsts = invert_128([block[0] for block in blocks])
    seconds, sides = [], []
    for first, (_, right, below, last) in zip(firsts, blocks):
        first, right, below = split(first), split(right), split(below)
        low = split(dot3(below, first))
        seconds.append(last - dot3(low, right))
        sides.append((low, split(dot3(first, right))))
    results = []
    for first, second, (low, high) in zip(firsts, invert_128(seconds), sides):
        corner = split(second)
        below = dot3(corner, low)
        top = jnp.concatenate([first + dot3(high, split(below)), -dot3(high, corner)], axis=1)
        bottom = jnp.concatenate([-below, second], axis=1)
        results.append(jnp.concatenate([top, bottom], axis=0))
    return results


def quarters(value):
    return (
        value[:LANES, :LANES],
        value[:LANES, LANES:],
        value[LANES:, :LANES],
        value[LANES:, LANES:],
    )


def chunks(count):
    return [(start, min(HALF, count - start)) for start in range(0, count, HALF)]


def eliminate(systems):
    upper = [split(x) for x in invert_256([quarters(s[0][:HALF, :HALF]) for s in systems])]
    lower = []
    for (pivot, g, gh, gl, zh, zl), inverse in zip(systems, upper):
        right = split(pivot[:HALF, HALF:])
        low = split(dot3(split(pivot[HALF:, :HALF]), inverse))
        lower.append(pivot[HALF:, HALF:] - dot3(low, right))
        for start, size in chunks(g.shape[0]):
            rows = pl.ds(start, size)
            part = split(g[rows, :HALF])
            gh[rows, :HALF], gl[rows, :HALF] = part
            solved = split(dot3(part, inverse))
            zh[rows, :HALF], zl[rows, :HALF] = solved
            part = split(g[rows, HALF:] - dot3(solved, right))
            gh[rows, HALF:], gl[rows, HALF:] = part
    lower = [split(x) for x in invert_256([quarters(value) for value in lower])]
    for (pivot, g, gh, gl, zh, zl), inverse in zip(systems, lower):
        for start, size in chunks(g.shape[0]):
            rows = pl.ds(start, size)
            solved = split(dot3((gh[rows, HALF:], gl[rows, HALF:]), inverse))
            zh[rows, HALF:], zl[rows, HALF:] = solved


def update(system, row, rows, column, columns):
    _, _, gh, gl, zh, zl = system
    row, column = pl.ds(row, rows), pl.ds(column, columns)
    return dot3((zh[row, :], zl[row, :]), (gh[column, :], gl[column, :]), NT)


def transpose_into(target, row, source):
    width = source.shape[1]
    for i in range(0, width, LANES):
        for j in range(0, source.shape[0], LANES):
            target[row + i : row + i + LANES, j : j + LANES] = source[
                j : j + LANES, i : i + LANES
            ].T


def front_kernel(
    side, diag, lower, arrow, pivot_out, pack_out, outer_out,
    dv, lv, av, ga, gah, gal, zah, zal, gb, gbh, gbl, zbh, zbl, pivot, sems,
):
    width, tip = diag.shape[1], arrow.shape[1]
    two = 2 * width
    order = [
        (diag, dv, 1), (diag, dv, 3), (lower, lv, 0), (lower, lv, 1), (lower, lv, 2), (lower, lv, 3),
        (arrow, av, 1), (arrow, av, 3), (diag, dv, 2), (arrow, av, 2), (diag, dv, 0), (arrow, av, 0),
    ]
    copies = [
        pltpu.make_async_copy(source.at[k], target.at[k], sems.at[n])
        for n, (source, target, k) in enumerate(order)
    ]
    for copy in copies:
        copy.start()
    for copy in copies:
        copy.wait()
    is_left = side[0] == 0

    transpose_into(ga, 0, lv.at[0])
    ga[width:two, :] = lv[1]
    ga[two:, :] = av[1]
    gb[:width, :] = lv[3]
    transpose_into(gb, width, lv.at[2])
    gb[two:, :] = av[3]
    first = (dv.at[1], ga, gah, gal, zah, zal)
    third = (dv.at[3], gb, gbh, gbl, zbh, zbl)
    eliminate([first, third])

    def pick(left, right):
        return jnp.where(is_left, left, right)

    def drop(value):
        return jnp.where(is_left, value, jnp.zeros_like(value))

    for start, size in chunks(width):
        rows = pl.ds(start, size)
        shared = pl.ds(width + start, size)
        e = (width + start, size, width, width)
        pivot[rows, :] = dv[2, rows, :] - update(first, *e) - drop(update(third, *e))
        fe = (start, size, width, width)
        near = -update(first, *fe)
        far = -update(third, *fe)
        ga[rows, :] = pick(near, lv[2, rows, :])
        ga[shared, :] = pick(far, near)
        ff = (start, size, 0, width)
        near = dv[0, rows, :] - update(first, *ff)
        far = -update(third, *ff)
        pivot_out[rows, :] = pick(far, near)
        outer_out[rows, :] = pick(near, dv[3, rows, :])
    te = (two, tip, width, width)
    ga[two:, :] = av[2] - update(first, *te) - drop(update(third, *te))
    tf = (two, tip, 0, width)
    near = av[0] - update(first, *tf)
    far = -update(third, *tf)
    tip_pivot = pick(far, near)
    tip_outer = pick(near, av[3])
    tt = (two, tip, two, tip)
    tip_tip = -update(first, *tt) - drop(update(third, *tt))

    second = (pivot, ga, gah, gal, zah, zal)
    eliminate([second])
    for start, size in chunks(width):
        rows = pl.ds(start, size)
        pivot_out[rows, :] = pivot_out[rows, :] - update(second, width + start, size, width, width)
        pack_out[rows, :] = -update(second, start, size, width, width)
        outer_out[rows, :] = outer_out[rows, :] - update(second, start, size, 0, width)
    pack_out[width : width + tip, :] = tip_pivot - update(second, two, tip, width, width)
    pack_out[width + tip : width + 2 * tip, :] = tip_outer - update(second, two, tip, 0, width)
    base = width + 2 * tip
    pack_out[base : base + tip, :] = jnp.zeros((tip, width), F32)
    pack_out[base : base + tip, :tip] = tip_tip - update(second, *tt)
    spill = pack_out.shape[0] - base - tip
    pack_out[base + tip :, :] = outer_out[:spill, :]


def merge_kernel(
    side, pivot_mine, pivot_other, pack_mine, pack_other, outer_mine, merged, tip_out,
    g, gh, gl, zh, zl, pivot,
):
    width = pivot.shape[0]
    tip = tip_out.shape[0]
    two = 2 * width
    base = width + 2 * tip
    half = merged.shape[0]
    spill = half - width
    is_left = side[0] == 0
    pivot[...] = pivot_mine[...] + pivot_other[...]
    for start, size in chunks(width):
        rows = pl.ds(start, size)
        mine, other = pack_mine[rows, :], pack_other[rows, :]
        g[rows, :] = jnp.where(is_left, mine, other)
        g[pl.ds(width + start, size), :] = jnp.where(is_left, other, mine)
    at = pl.ds(width, tip)
    g[two:, :] = pack_mine[at, :] + pack_other[at, :]
    system = (pivot, g, gh, gl, zh, zl)
    eliminate([system])
    at = pl.ds(base, tip)
    tip_tip = pack_mine[at, :tip] + pack_other[at, :tip] - update(system, two, tip, two, tip)
    tip_out[...] = tip_tip
    outer_tip = pl.ds(width + tip, tip)

    @pl.when(is_left)
    def _():
        for start, size in chunks(width):
            rows = pl.ds(start, size)
            merged[rows, :width] = outer_mine[rows, :] - update(system, start, size, 0, width)
            merged[rows, width:two] = -update(system, start, size, width, width)
            mine = pack_mine[outer_tip, start : start + size].T
            merged[rows, two:] = mine - update(system, start, size, two, tip)
        merged[width:, :width] = -update(system, width, spill, 0, width)
        other = pack_other[base + tip :, :]
        merged[width:, width:two] = other - update(system, width, spill, width, width)
        other = pack_other[outer_tip, :LANES].T[:spill, :]
        merged[width:, two:] = other - update(system, width, spill, two, tip)

    @pl.when(jnp.logical_not(is_left))
    def _():
        for start, size in chunks(width):
            skip = spill if start == 0 else 0
            rows = pl.ds(start + skip - spill, size - skip)
            merged[rows, :width] = -update(system, width + start, size, 0, width)[skip:, :]
            mine = outer_mine[pl.ds(start, size), :]
            merged[rows, width:two] = (
                mine - update(system, width + start, size, width, width)
            )[skip:, :]
            mine = pack_mine[outer_tip, start : start + size].T
            merged[rows, two:] = (mine - update(system, width + start, size, two, tip))[skip:, :]
        rows = pl.ds(half - tip, tip)
        merged[rows, :width] = pack_other[outer_tip, :] - update(system, two, tip, 0, width)
        merged[rows, width:two] = pack_mine[outer_tip, :] - update(system, two, tip, width, width)
        merged[rows, two:] = tip_tip


def swapped(value, axis, mask):
    count = lax.axis_size(axis)
    return lax.ppermute(value, axis, [(k, k ^ mask) for k in range(count)])


def sum_over_pairs(value, axis):
    step = 2
    while step < lax.axis_size(axis):
        if 2 * step < lax.axis_size(axis):
            near, far, across = (swapped(value, axis, step * k) for k in (1, 2, 3))
            value = (value + near) + (far + across)
            step *= 4
        else:
            value = value + swapped(value, axis, step)
            step *= 2
    return value


def whole(*shape):
    return pl.BlockSpec(shape, lambda: (0,) * len(shape), memory_space=pltpu.VMEM)


def local(diag_blocks, lower_blocks, arrow_blocks, tip_block):
    count, width = diag_blocks.shape[:2]
    tip = arrow_blocks.shape[1]
    front = 2 * width + tip
    half = front // 2
    spill = half - width
    packed = width + 3 * tip + spill
    side = (lax.axis_index("tm") % 2).astype(jnp.int32).reshape(1)
    smem = pl.BlockSpec(memory_space=pltpu.SMEM)
    system = [pltpu.VMEM((front, width), F32)] + [pltpu.VMEM((front, width), BF16)] * 4
    params = pltpu.CompilerParams(vmem_limit_bytes=56 * 2**20)
    pivot, pack, outer = pl.pallas_call(
        front_kernel,
        out_shape=[
            jax.ShapeDtypeStruct((width, width), F32),
            jax.ShapeDtypeStruct((packed, width), F32),
            jax.ShapeDtypeStruct((width, width), F32),
        ],
        in_specs=[smem] + [pl.BlockSpec(memory_space=pl.ANY)] * 3,
        out_specs=[pl.BlockSpec(memory_space=pltpu.VMEM)] * 3,
        scratch_shapes=[
            pltpu.VMEM((count, width, width), F32),
            pltpu.VMEM((count, width, width), F32),
            pltpu.VMEM((count, tip, width), F32),
        ]
        + system
        + system
        + [pltpu.VMEM((width, width), F32), pltpu.SemaphoreType.DMA((3 * count,))],
        compiler_params=params,
        name="front",
    )(side, diag_blocks, lower_blocks, arrow_blocks)
    pivot_other = swapped(pivot, "tm", 1)
    pack_other = swapped(pack, "tm", 1)
    merged, tip_tip = pl.pallas_call(
        merge_kernel,
        out_shape=[
            jax.ShapeDtypeStruct((half, front), F32),
            jax.ShapeDtypeStruct((tip, tip), F32),
        ],
        in_specs=[smem] + [pl.BlockSpec(memory_space=pltpu.VMEM)] * 5,
        out_specs=[pl.BlockSpec(memory_space=pltpu.VMEM)] * 2,
        scratch_shapes=system + [pltpu.VMEM((width, width), F32)],
        compiler_params=params,
        name="merge",
    )(side, pivot, pivot_other, pack, pack_other, outer)
    return merged, tip_block + sum_over_pairs(tip_tip, "tm")


def solution(mesh):
    placed = (P("tm", None, None), P("tm", None, None), P("tm", None, None), P())
    return jax.shard_map(
        local, mesh=mesh, in_specs=placed, out_specs=(P("tm", None), P()), check_vma=False
    )
```

```python
import functools

import jax
import jax.numpy as jnp
from jax import lax
from jax.experimental import pallas as pl
from jax.experimental.pallas import tpu as pltpu
from jax.sharding import PartitionSpec as P

F32 = jnp.float32
BF16 = jnp.bfloat16
SUB = 8
LANES = 128
HALF = 256
NN = (((1,), (0,)), ((), ()))
NT = (((1,), (1,)), ((), ()))


def split(value):
    high = value.astype(BF16)
    return high, (value - high.astype(F32)).astype(BF16)


def dot3(left, right, dims=NN):
    one = functools.partial(lax.dot_general, dimension_numbers=dims, preferred_element_type=F32)
    return one(left[0], right[0]) + (one(left[0], right[1]) + one(left[1], right[0]))


def row_of(value, index):
    return jnp.broadcast_to(value[index : index + 1, :], (SUB, LANES))


def column_of(value, index):
    return jnp.broadcast_to(value[:, index : index + 1], (SUB, LANES))


def total(terms):
    while len(terms) > 1:
        terms = [terms[k] + terms[k + 1] for k in range(0, len(terms), 2)]
    return terms[0]


def cleared(value, start, top):
    lane = lax.broadcasted_iota(jnp.int32, (SUB, LANES), 1)
    panel = (lane >= start) & (lane < start + SUB)
    terms = [column_of(value, start + k) * top[k] for k in range(SUB)]
    return jnp.where(panel, 0.0, value) - total(terms)


def late_update(rows):
    top = [row_of(rows[15], k) for k in range(SUB)]
    return rows[:1] + [cleared(value, LANES - SUB, top) for value in rows[1:15]] + rows[15:]


def panel_step(state, late):
    rows, columns = list(state[:16]), list(state[16:])
    sub = lax.broadcasted_iota(jnp.int32, (SUB, LANES), 0)
    lane = lax.broadcasted_iota(jnp.int32, (SUB, LANES), 1)
    if late:
        rows = late_update(rows)
    top = jnp.where(lane < SUB, jnp.where(lane == sub, 1.0, 0.0).astype(F32), rows[0])
    for pivot in range(SUB):
        inverse = pltpu.reciprocal(row_of(columns[pivot], pivot))
        here = sub == pivot

        def eliminated(value):
            row = row_of(value, pivot)
            product = columns[pivot] * row
            return jnp.where(here, row * inverse, value - product * inverse)

        columns[pivot + 1 :] = [eliminated(value) for value in columns[pivot + 1 :]]
        top = eliminated(top)
    following = cleared(rows[1], 0, [row_of(top, k) for k in range(SUB)])
    columns = [column_of(following, SUB + k) for k in range(SUB)]
    rows = [pltpu.roll(value, LANES - SUB, 1) for value in [following] + rows[2:] + [top]]
    return tuple(rows + columns)


def invert_128(blocks):
    states = []
    for block in blocks:
        rows = [block[SUB * k : SUB * (k + 1), :] for k in range(16)]
        columns = [column_of(rows[0], k) for k in range(SUB)]
        states.append(panel_step(tuple(rows + columns), False))
    states = lax.fori_loop(
        1, 16, lambda _, carry: tuple(panel_step(s, True) for s in carry), tuple(states)
    )
    return [jnp.concatenate(late_update(list(state[:16])), axis=0) for state in states]


def invert_256(blocks):
    firsts = invert_128([block[0] for block in blocks])
    seconds, sides = [], []
    for first, (_, right, below, last) in zip(firsts, blocks):
        first, right, below = split(first), split(right), split(below)
        low = split(dot3(below, first))
        seconds.append(last - dot3(low, right))
        sides.append((low, split(dot3(first, right))))
    results = []
    for first, second, (low, high) in zip(firsts, invert_128(seconds), sides):
        corner = split(second)
        below = dot3(corner, low)
        top = jnp.concatenate([first + dot3(high, split(below)), -dot3(high, corner)], axis=1)
        bottom = jnp.concatenate([-below, second], axis=1)
        results.append(jnp.concatenate([top, bottom], axis=0))
    return results


def quarters(value):
    return (
        value[:LANES, :LANES],
        value[:LANES, LANES:],
        value[LANES:, :LANES],
        value[LANES:, LANES:],
    )


def chunks(count):
    return [(start, min(HALF, count - start)) for start in range(0, count, HALF)]


def equilibrate(pivot):
    width = pivot.shape[0]
    row = lax.broadcasted_iota(jnp.int32, (LANES, LANES), 0)
    lane = lax.broadcasted_iota(jnp.int32, (LANES, LANES), 1)
    scales = []
    for start in range(0, width, LANES):
        block = pivot[start : start + LANES, start : start + LANES]
        scales.append(lax.rsqrt(jnp.sum(jnp.where(row == lane, block, 0.0), axis=0, keepdims=True)))
    for index, scale in enumerate(scales):
        rows = pl.ds(index * LANES, LANES)
        down = jnp.broadcast_to(scale, (LANES, LANES)).T
        for other, across in enumerate(scales):
            lanes = pl.ds(other * LANES, LANES)
            pivot[rows, lanes] = pivot[rows, lanes] * down * across
    return jnp.concatenate(scales, axis=1)


def eliminate(systems):
    scales = [equilibrate(system[0]) for system in systems]
    upper = [split(x) for x in invert_256([quarters(s[0][:HALF, :HALF]) for s in systems])]
    lower = []
    for (pivot, g, gh, gl, zh, zl), inverse, scale in zip(systems, upper, scales):
        right = split(pivot[:HALF, HALF:])
        low = split(dot3(split(pivot[HALF:, :HALF]), inverse))
        lower.append(pivot[HALF:, HALF:] - dot3(low, right))
        for start, size in chunks(g.shape[0]):
            rows = pl.ds(start, size)
            part = split(g[rows, :HALF] * scale[:, :HALF])
            gh[rows, :HALF], gl[rows, :HALF] = part
            solved = split(dot3(part, inverse))
            zh[rows, :HALF], zl[rows, :HALF] = solved
            part = split(g[rows, HALF:] * scale[:, HALF:] - dot3(solved, right))
            gh[rows, HALF:], gl[rows, HALF:] = part
    lower = [split(x) for x in invert_256([quarters(value) for value in lower])]
    for (pivot, g, gh, gl, zh, zl), inverse in zip(systems, lower):
        for start, size in chunks(g.shape[0]):
            rows = pl.ds(start, size)
            solved = split(dot3((gh[rows, HALF:], gl[rows, HALF:]), inverse))
            zh[rows, HALF:], zl[rows, HALF:] = solved


def update(system, row, rows, column, columns):
    _, _, gh, gl, zh, zl = system
    row, column = pl.ds(row, rows), pl.ds(column, columns)
    return dot3((zh[row, :], zl[row, :]), (gh[column, :], gl[column, :]), NT)


def transpose_into(target, row, source):
    width = source.shape[1]
    for i in range(0, width, LANES):
        for j in range(0, source.shape[0], LANES):
            target[row + i : row + i + LANES, j : j + LANES] = source[
                j : j + LANES, i : i + LANES
            ].T


def front_kernel(
    side, diag, lower, arrow, pivot_out, pack_out, outer_out,
    dv, lv, av, ga, gah, gal, zah, zal, gb, gbh, gbl, zbh, zbl, pivot, sems,
):
    width, tip = diag.shape[1], arrow.shape[1]
    two = 2 * width
    order = [
        (diag, dv, 1), (diag, dv, 3), (lower, lv, 0), (lower, lv, 1), (lower, lv, 2), (lower, lv, 3),
        (arrow, av, 1), (arrow, av, 3), (diag, dv, 2), (arrow, av, 2), (diag, dv, 0), (arrow, av, 0),
    ]
    copies = [
        pltpu.make_async_copy(source.at[k], target.at[k], sems.at[n])
        for n, (source, target, k) in enumerate(order)
    ]
    for copy in copies:
        copy.start()
    for copy in copies:
        copy.wait()
    is_left = side[0] == 0

    transpose_into(ga, 0, lv.at[0])
    ga[width:two, :] = lv[1]
    ga[two:, :] = av[1]
    gb[:width, :] = lv[3]
    transpose_into(gb, width, lv.at[2])
    gb[two:, :] = av[3]
    first = (dv.at[1], ga, gah, gal, zah, zal)
    third = (dv.at[3], gb, gbh, gbl, zbh, zbl)
    outer_out[...] = dv[3]
    eliminate([first, third])

    def pick(left, right):
        return jnp.where(is_left, left, right)

    def drop(value):
        return jnp.where(is_left, value, jnp.zeros_like(value))

    for start, size in chunks(width):
        rows = pl.ds(start, size)
        shared = pl.ds(width + start, size)
        e = (width + start, size, width, width)
        pivot[rows, :] = dv[2, rows, :] - update(first, *e) - drop(update(third, *e))
        fe = (start, size, width, width)
        near = -update(first, *fe)
        far = -update(third, *fe)
        ga[rows, :] = pick(near, lv[2, rows, :])
        ga[shared, :] = pick(far, near)
        ff = (start, size, 0, width)
        near = dv[0, rows, :] - update(first, *ff)
        far = -update(third, *ff)
        pivot_out[rows, :] = pick(far, near)
        outer_out[rows, :] = pick(near, outer_out[rows, :])
    te = (two, tip, width, width)
    ga[two:, :] = av[2] - update(first, *te) - drop(update(third, *te))
    tf = (two, tip, 0, width)
    near = av[0] - update(first, *tf)
    far = -update(third, *tf)
    tip_pivot = pick(far, near)
    tip_outer = pick(near, av[3])
    tt = (two, tip, two, tip)
    tip_tip = -update(first, *tt) - drop(update(third, *tt))

    second = (pivot, ga, gah, gal, zah, zal)
    eliminate([second])
    for start, size in chunks(width):
        rows = pl.ds(start, size)
        pivot_out[rows, :] = pivot_out[rows, :] - update(second, width + start, size, width, width)
        pack_out[rows, :] = -update(second, start, size, width, width)
        outer_out[rows, :] = outer_out[rows, :] - update(second, start, size, 0, width)
    pack_out[width : width + tip, :] = tip_pivot - update(second, two, tip, width, width)
    pack_out[width + tip : width + 2 * tip, :] = tip_outer - update(second, two, tip, 0, width)
    base = width + 2 * tip
    pack_out[base : base + tip, :] = jnp.zeros((tip, width), F32)
    pack_out[base : base + tip, :tip] = tip_tip - update(second, *tt)
    spill = pack_out.shape[0] - base - tip
    pack_out[base + tip :, :] = outer_out[:spill, :]


def merge_kernel(
    side, pivot_mine, pivot_other, pack_mine, pack_other, outer_mine, merged, tip_out,
    g, gh, gl, zh, zl, pivot,
):
    width = pivot.shape[0]
    tip = tip_out.shape[0]
    two = 2 * width
    base = width + 2 * tip
    half = merged.shape[0]
    spill = half - width
    is_left = side[0] == 0
    pivot[...] = pivot_mine[...] + pivot_other[...]
    for start, size in chunks(width):
        rows = pl.ds(start, size)
        mine, other = pack_mine[rows, :], pack_other[rows, :]
        g[rows, :] = jnp.where(is_left, mine, other)
        g[pl.ds(width + start, size), :] = jnp.where(is_left, other, mine)
    at = pl.ds(width, tip)
    g[two:, :] = pack_mine[at, :] + pack_other[at, :]
    system = (pivot, g, gh, gl, zh, zl)
    eliminate([system])
    at = pl.ds(base, tip)
    tip_tip = pack_mine[at, :tip] + pack_other[at, :tip] - update(system, two, tip, two, tip)
    tip_out[...] = tip_tip
    outer_tip = pl.ds(width + tip, tip)

    @pl.when(is_left)
    def _():
        for start, size in chunks(width):
            rows = pl.ds(start, size)
            merged[rows, :width] = outer_mine[rows, :] - update(system, start, size, 0, width)
            merged[rows, width:two] = -update(system, start, size, width, width)
            mine = pack_mine[outer_tip, start : start + size].T
            merged[rows, two:] = mine - update(system, start, size, two, tip)
        merged[width:, :width] = -update(system, width, spill, 0, width)
        other = pack_other[base + tip :, :]
        merged[width:, width:two] = other - update(system, width, spill, width, width)
        other = pack_other[outer_tip, :LANES].T[:spill, :]
        merged[width:, two:] = other - update(system, width, spill, two, tip)

    @pl.when(jnp.logical_not(is_left))
    def _():
        for start, size in chunks(width):
            skip = spill if start == 0 else 0
            rows = pl.ds(start + skip - spill, size - skip)
            merged[rows, :width] = -update(system, width + start, size, 0, width)[skip:, :]
            mine = outer_mine[pl.ds(start, size), :]
            merged[rows, width:two] = (
                mine - update(system, width + start, size, width, width)
            )[skip:, :]
            mine = pack_mine[outer_tip, start : start + size].T
            merged[rows, two:] = (mine - update(system, width + start, size, two, tip))[skip:, :]
        rows = pl.ds(half - tip, tip)
        merged[rows, :width] = pack_other[outer_tip, :] - update(system, two, tip, 0, width)
        merged[rows, width:two] = pack_mine[outer_tip, :] - update(system, two, tip, width, width)
        merged[rows, two:] = tip_tip


def swapped(value, axis, mask):
    count = lax.axis_size(axis)
    return lax.ppermute(value, axis, [(k, k ^ mask) for k in range(count)])


def sum_over_pairs(value, axis):
    step = 2
    while step < lax.axis_size(axis):
        if 2 * step < lax.axis_size(axis):
            near, far, across = (swapped(value, axis, step * k) for k in (1, 2, 3))
            value = (value + near) + (far + across)
            step *= 4
        else:
            value = value + swapped(value, axis, step)
            step *= 2
    return value


def whole(*shape):
    return pl.BlockSpec(shape, lambda: (0,) * len(shape), memory_space=pltpu.VMEM)


def local(diag_blocks, lower_blocks, arrow_blocks, tip_block):
    count, width = diag_blocks.shape[:2]
    tip = arrow_blocks.shape[1]
    front = 2 * width + tip
    half = front // 2
    spill = half - width
    packed = width + 3 * tip + spill
    side = (lax.axis_index("tm") % 2).astype(jnp.int32).reshape(1)
    smem = pl.BlockSpec(memory_space=pltpu.SMEM)
    system = [pltpu.VMEM((front, width), F32)] + [pltpu.VMEM((front, width), BF16)] * 4
    params = pltpu.CompilerParams(vmem_limit_bytes=56 * 2**20)
    pivot, pack, outer = pl.pallas_call(
        front_kernel,
        out_shape=[
            jax.ShapeDtypeStruct((width, width), F32),
            jax.ShapeDtypeStruct((packed, width), F32),
            jax.ShapeDtypeStruct((width, width), F32),
        ],
        in_specs=[smem] + [pl.BlockSpec(memory_space=pl.ANY)] * 3,
        out_specs=[pl.BlockSpec(memory_space=pltpu.VMEM)] * 3,
        scratch_shapes=[
            pltpu.VMEM((count, width, width), F32),
            pltpu.VMEM((count, width, width), F32),
            pltpu.VMEM((count, tip, width), F32),
        ]
        + system
        + system
        + [pltpu.VMEM((width, width), F32), pltpu.SemaphoreType.DMA((3 * count,))],
        compiler_params=params,
        name="front",
    )(side, diag_blocks, lower_blocks, arrow_blocks)
    pivot_other = swapped(pivot, "tm", 1)
    pack_other = swapped(pack, "tm", 1)
    merged, tip_tip = pl.pallas_call(
        merge_kernel,
        out_shape=[
            jax.ShapeDtypeStruct((half, front), F32),
            jax.ShapeDtypeStruct((tip, tip), F32),
        ],
        in_specs=[smem] + [pl.BlockSpec(memory_space=pltpu.VMEM)] * 5,
        out_specs=[pl.BlockSpec(memory_space=pltpu.VMEM)] * 2,
        scratch_shapes=system + [pltpu.VMEM((width, width), F32)],
        compiler_params=params,
        name="merge",
    )(side, pivot, pivot_other, pack, pack_other, outer)
    return merged, tip_block + sum_over_pairs(tip_tip, "tm")


def solution(mesh):
    placed = (P("tm", None, None), P("tm", None, None), P("tm", None, None), P())
    return jax.shard_map(
        local, mesh=mesh, in_specs=placed, out_specs=(P("tm", None), P()), check_vma=False
    )
```

```python
import functools

import jax
import jax.numpy as jnp
from jax import lax
from jax.experimental import pallas as pl
from jax.experimental.pallas import tpu as pltpu
from jax.sharding import PartitionSpec as P

F32 = jnp.float32
BF16 = jnp.bfloat16
SUB = 8
LANES = 128
HALF = 256
NN = (((1,), (0,)), ((), ()))
NT = (((1,), (1,)), ((), ()))


def split(value):
    high = value.astype(BF16)
    return high, (value - high.astype(F32)).astype(BF16)


def dot3(left, right, dims=NN):
    one = functools.partial(lax.dot_general, dimension_numbers=dims, preferred_element_type=F32)
    return one(left[0], right[0]) + (one(left[0], right[1]) + one(left[1], right[0]))


def row_of(value, index):
    return jnp.broadcast_to(value[index : index + 1, :], (SUB, LANES))


def column_of(value, index):
    return jnp.broadcast_to(value[:, index : index + 1], (SUB, LANES))


def total(terms):
    while len(terms) > 1:
        terms = [terms[k] + terms[k + 1] for k in range(0, len(terms), 2)]
    return terms[0]


def cleared(value, start, top):
    lane = lax.broadcasted_iota(jnp.int32, (SUB, LANES), 1)
    panel = (lane >= start) & (lane < start + SUB)
    terms = [column_of(value, start + k) * top[k] for k in range(SUB)]
    return jnp.where(panel, 0.0, value) - total(terms)


def late_update(work, step, top):
    value = work[...]
    high, low = split(
        jnp.concatenate([jnp.where(step % 2 == k, top, jnp.zeros_like(top)) for k in (0, 1)], axis=0)
    )
    right = tuple(
        jnp.concatenate(
            [jnp.where(step // 2 == k, part, jnp.zeros_like(part)) for k in range(8)], axis=0
        )
        for part in (high, low)
    )
    lane = lax.broadcasted_iota(jnp.int32, (LANES, LANES), 1)
    panel = (lane >= SUB * step) & (lane < SUB * (step + 1))
    work[...] = jnp.where(panel, 0.0, value) - dot3(split(value), right)
    work[pl.ds(pl.multiple_of(SUB * step, SUB), SUB), :] = top


def panel_step(work, step, state, late):
    row, columns, last = state[0], list(state[1:9]), state[9]
    sub = lax.broadcasted_iota(jnp.int32, (SUB, LANES), 0)
    lane = lax.broadcasted_iota(jnp.int32, (SUB, LANES), 1)
    if late:
        late_update(work, step - 1, last)
    top = jnp.where(lane < SUB, jnp.where(lane == sub, 1.0, 0.0).astype(F32), row)
    for pivot in range(SUB):
        inverse = pltpu.reciprocal(row_of(columns[pivot], pivot))
        here = sub == pivot

        def eliminated(value):
            row = row_of(value, pivot)
            product = columns[pivot] * row
            return jnp.where(here, row * inverse, value - product * inverse)

        columns[pivot + 1 :] = [eliminated(value) for value in columns[pivot + 1 :]]
        top = eliminated(top)
    following = work[pl.ds(pl.multiple_of((step + 1) % 16 * SUB, SUB), SUB), :]
    following = pltpu.roll(following, (LANES - SUB * step) % LANES, 1)
    following = cleared(following, 0, [row_of(top, k) for k in range(SUB)])
    columns = [column_of(following, SUB + k) for k in range(SUB)]
    row = pltpu.roll(following, LANES - SUB, 1)
    return (row, *columns, pltpu.roll(top, SUB * step, 1))


def invert_128(blocks, works):
    states = []
    for block, work in zip(blocks, works):
        work[...] = block
        row = block[:SUB, :]
        columns = [column_of(row, k) for k in range(SUB)]
        states.append(panel_step(work, 0, (row, *columns, row), False))

    def step(index, carry):
        return tuple(panel_step(work, index, state, True) for work, state in zip(works, carry))

    states = lax.fori_loop(1, 16, step, tuple(states))
    for work, state in zip(works, states):
        late_update(work, 15, state[9])
    return [work[...] for work in works]


def invert_256(blocks, works):
    firsts = invert_128([block[0] for block in blocks], works)
    seconds, sides = [], []
    for first, (_, right, below, last) in zip(firsts, blocks):
        first, right, below = split(first), split(right), split(below)
        low = split(dot3(below, first))
        seconds.append(last - dot3(low, right))
        sides.append((low, split(dot3(first, right))))
    results = []
    for first, second, (low, high) in zip(firsts, invert_128(seconds, works), sides):
        corner = split(second)
        below = dot3(corner, low)
        top = jnp.concatenate([first + dot3(high, split(below)), -dot3(high, corner)], axis=1)
        bottom = jnp.concatenate([-below, second], axis=1)
        results.append(jnp.concatenate([top, bottom], axis=0))
    return results


def quarters(value):
    return (
        value[:LANES, :LANES],
        value[:LANES, LANES:],
        value[LANES:, :LANES],
        value[LANES:, LANES:],
    )


def chunks(count):
    return [(start, min(HALF, count - start)) for start in range(0, count, HALF)]


def equilibrate(pivot):
    width = pivot.shape[0]
    row = lax.broadcasted_iota(jnp.int32, (LANES, LANES), 0)
    lane = lax.broadcasted_iota(jnp.int32, (LANES, LANES), 1)
    scales = []
    for start in range(0, width, LANES):
        block = pivot[start : start + LANES, start : start + LANES]
        scales.append(lax.rsqrt(jnp.sum(jnp.where(row == lane, block, 0.0), axis=0, keepdims=True)))
    for index, scale in enumerate(scales):
        rows = pl.ds(index * LANES, LANES)
        down = jnp.broadcast_to(scale, (LANES, LANES)).T
        for other, across in enumerate(scales):
            lanes = pl.ds(other * LANES, LANES)
            pivot[rows, lanes] = pivot[rows, lanes] * down * across
    return jnp.concatenate(scales, axis=1)


def eliminate(systems, works):
    scales = [equilibrate(system[0]) for system in systems]
    upper = [quarters(system[0][:HALF, :HALF]) for system in systems]
    upper = [split(value) for value in invert_256(upper, works)]
    lower = []
    for (pivot, g, gh, gl, zh, zl), inverse, scale in zip(systems, upper, scales):
        right = split(pivot[:HALF, HALF:])
        low = split(dot3(split(pivot[HALF:, :HALF]), inverse))
        lower.append(pivot[HALF:, HALF:] - dot3(low, right))
        for start, size in chunks(g.shape[0]):
            rows = pl.ds(start, size)
            part = split(g[rows, :HALF] * scale[:, :HALF])
            gh[rows, :HALF], gl[rows, :HALF] = part
            solved = split(dot3(part, inverse))
            zh[rows, :HALF], zl[rows, :HALF] = solved
            part = split(g[rows, HALF:] * scale[:, HALF:] - dot3(solved, right))
            gh[rows, HALF:], gl[rows, HALF:] = part
    lower = [split(x) for x in invert_256([quarters(value) for value in lower], works)]
    for (pivot, g, gh, gl, zh, zl), inverse in zip(systems, lower):
        for start, size in chunks(g.shape[0]):
            rows = pl.ds(start, size)
            solved = split(dot3((gh[rows, HALF:], gl[rows, HALF:]), inverse))
            zh[rows, HALF:], zl[rows, HALF:] = solved


def update(system, row, rows, column, columns):
    _, _, gh, gl, zh, zl = system
    row, column = pl.ds(row, rows), pl.ds(column, columns)
    return dot3((zh[row, :], zl[row, :]), (gh[column, :], gl[column, :]), NT)


def transpose_into(target, row, source):
    width = source.shape[1]
    for i in range(0, width, LANES):
        for j in range(0, source.shape[0], LANES):
            target[row + i : row + i + LANES, j : j + LANES] = source[
                j : j + LANES, i : i + LANES
            ].T


def front_kernel(
    side, diag, lower, arrow, pivot_out, pack_out, outer_out,
    dv, lv, av, ga, gah, gal, zah, zal, gb, gbh, gbl, zbh, zbl, pivot, work, sems,
):
    width, tip = diag.shape[1], arrow.shape[1]
    two = 2 * width
    order = [
        (diag, dv, 1), (diag, dv, 3), (lower, lv, 0), (lower, lv, 1), (lower, lv, 2), (lower, lv, 3),
        (arrow, av, 1), (arrow, av, 3), (diag, dv, 2), (arrow, av, 2), (diag, dv, 0), (arrow, av, 0),
    ]
    copies = [
        pltpu.make_async_copy(source.at[k], target.at[k], sems.at[n])
        for n, (source, target, k) in enumerate(order)
    ]
    for copy in copies:
        copy.start()
    for copy in copies:
        copy.wait()
    is_left = side[0] == 0

    transpose_into(ga, 0, lv.at[0])
    ga[width:two, :] = lv[1]
    ga[two:, :] = av[1]
    gb[:width, :] = lv[3]
    transpose_into(gb, width, lv.at[2])
    gb[two:, :] = av[3]
    first = (dv.at[1], ga, gah, gal, zah, zal)
    third = (dv.at[3], gb, gbh, gbl, zbh, zbl)
    outer_out[...] = dv[3]
    eliminate([first, third], [work.at[0], work.at[1]])

    def pick(left, right):
        return jnp.where(is_left, left, right)

    def drop(value):
        return jnp.where(is_left, value, jnp.zeros_like(value))

    for start, size in chunks(width):
        rows = pl.ds(start, size)
        shared = pl.ds(width + start, size)
        e = (width + start, size, width, width)
        pivot[rows, :] = dv[2, rows, :] - update(first, *e) - drop(update(third, *e))
        fe = (start, size, width, width)
        near = -update(first, *fe)
        far = -update(third, *fe)
        ga[rows, :] = pick(near, lv[2, rows, :])
        ga[shared, :] = pick(far, near)
        ff = (start, size, 0, width)
        near = dv[0, rows, :] - update(first, *ff)
        far = -update(third, *ff)
        pivot_out[rows, :] = pick(far, near)
        outer_out[rows, :] = pick(near, outer_out[rows, :])
    te = (two, tip, width, width)
    ga[two:, :] = av[2] - update(first, *te) - drop(update(third, *te))
    tf = (two, tip, 0, width)
    near = av[0] - update(first, *tf)
    far = -update(third, *tf)
    tip_pivot = pick(far, near)
    tip_outer = pick(near, av[3])
    tt = (two, tip, two, tip)
    tip_tip = -update(first, *tt) - drop(update(third, *tt))

    second = (pivot, ga, gah, gal, zah, zal)
    eliminate([second], [work.at[0]])
    for start, size in chunks(width):
        rows = pl.ds(start, size)
        pivot_out[rows, :] = pivot_out[rows, :] - update(second, width + start, size, width, width)
        pack_out[rows, :] = -update(second, start, size, width, width)
        outer_out[rows, :] = outer_out[rows, :] - update(second, start, size, 0, width)
    pack_out[width : width + tip, :] = tip_pivot - update(second, two, tip, width, width)
    pack_out[width + tip : width + 2 * tip, :] = tip_outer - update(second, two, tip, 0, width)
    base = width + 2 * tip
    pack_out[base : base + tip, :] = jnp.zeros((tip, width), F32)
    pack_out[base : base + tip, :tip] = tip_tip - update(second, *tt)
    spill = pack_out.shape[0] - base - tip
    pack_out[base + tip :, :] = outer_out[:spill, :]


def merge_kernel(
    side, pivot_mine, pivot_other, pack_mine, pack_other, outer_mine, merged, tip_out,
    g, gh, gl, zh, zl, pivot, work,
):
    width = pivot.shape[0]
    tip = tip_out.shape[0]
    two = 2 * width
    base = width + 2 * tip
    half = merged.shape[0]
    spill = half - width
    is_left = side[0] == 0
    pivot[...] = pivot_mine[...] + pivot_other[...]
    for start, size in chunks(width):
        rows = pl.ds(start, size)
        mine, other = pack_mine[rows, :], pack_other[rows, :]
        g[rows, :] = jnp.where(is_left, mine, other)
        g[pl.ds(width + start, size), :] = jnp.where(is_left, other, mine)
    at = pl.ds(width, tip)
    g[two:, :] = pack_mine[at, :] + pack_other[at, :]
    system = (pivot, g, gh, gl, zh, zl)
    eliminate([system], [work])
    at = pl.ds(base, tip)
    tip_tip = pack_mine[at, :tip] + pack_other[at, :tip] - update(system, two, tip, two, tip)
    tip_out[...] = tip_tip
    outer_tip = pl.ds(width + tip, tip)

    @pl.when(is_left)
    def _():
        for start, size in chunks(width):
            rows = pl.ds(start, size)
            merged[rows, :width] = outer_mine[rows, :] - update(system, start, size, 0, width)
            merged[rows, width:two] = -update(system, start, size, width, width)
            mine = pack_mine[outer_tip, start : start + size].T
            merged[rows, two:] = mine - update(system, start, size, two, tip)
        merged[width:, :width] = -update(system, width, spill, 0, width)
        other = pack_other[base + tip :, :]
        merged[width:, width:two] = other - update(system, width, spill, width, width)
        other = pack_other[outer_tip, :LANES].T[:spill, :]
        merged[width:, two:] = other - update(system, width, spill, two, tip)

    @pl.when(jnp.logical_not(is_left))
    def _():
        for start, size in chunks(width):
            skip = spill if start == 0 else 0
            rows = pl.ds(start + skip - spill, size - skip)
            merged[rows, :width] = -update(system, width + start, size, 0, width)[skip:, :]
            mine = outer_mine[pl.ds(start, size), :]
            merged[rows, width:two] = (
                mine - update(system, width + start, size, width, width)
            )[skip:, :]
            mine = pack_mine[outer_tip, start : start + size].T
            merged[rows, two:] = (mine - update(system, width + start, size, two, tip))[skip:, :]
        rows = pl.ds(half - tip, tip)
        merged[rows, :width] = pack_other[outer_tip, :] - update(system, two, tip, 0, width)
        merged[rows, width:two] = pack_mine[outer_tip, :] - update(system, two, tip, width, width)
        merged[rows, two:] = tip_tip


def swapped(value, axis, mask):
    count = lax.axis_size(axis)
    return lax.ppermute(value, axis, [(k, k ^ mask) for k in range(count)])


def sum_over_pairs(value, axis):
    step = 2
    while step < lax.axis_size(axis):
        if 2 * step < lax.axis_size(axis):
            near, far, across = (swapped(value, axis, step * k) for k in (1, 2, 3))
            value = (value + near) + (far + across)
            step *= 4
        else:
            value = value + swapped(value, axis, step)
            step *= 2
    return value


def whole(*shape):
    return pl.BlockSpec(shape, lambda: (0,) * len(shape), memory_space=pltpu.VMEM)


def local(diag_blocks, lower_blocks, arrow_blocks, tip_block):
    count, width = diag_blocks.shape[:2]
    tip = arrow_blocks.shape[1]
    front = 2 * width + tip
    half = front // 2
    spill = half - width
    packed = width + 3 * tip + spill
    side = (lax.axis_index("tm") % 2).astype(jnp.int32).reshape(1)
    smem = pl.BlockSpec(memory_space=pltpu.SMEM)
    system = [pltpu.VMEM((front, width), F32)] + [pltpu.VMEM((front, width), BF16)] * 4
    params = pltpu.CompilerParams(vmem_limit_bytes=56 * 2**20)
    pivot, pack, outer = pl.pallas_call(
        front_kernel,
        out_shape=[
            jax.ShapeDtypeStruct((width, width), F32),
            jax.ShapeDtypeStruct((packed, width), F32),
            jax.ShapeDtypeStruct((width, width), F32),
        ],
        in_specs=[smem] + [pl.BlockSpec(memory_space=pl.ANY)] * 3,
        out_specs=[pl.BlockSpec(memory_space=pltpu.VMEM)] * 3,
        scratch_shapes=[
            pltpu.VMEM((count, width, width), F32),
            pltpu.VMEM((count, width, width), F32),
            pltpu.VMEM((count, tip, width), F32),
        ]
        + system
        + system
        + [pltpu.VMEM((width, width), F32), pltpu.VMEM((2, LANES, LANES), F32)]
        + [pltpu.SemaphoreType.DMA((3 * count,))],
        compiler_params=params,
        name="front",
    )(side, diag_blocks, lower_blocks, arrow_blocks)
    pivot_other = swapped(pivot, "tm", 1)
    pack_other = swapped(pack, "tm", 1)
    merged, tip_tip = pl.pallas_call(
        merge_kernel,
        out_shape=[
            jax.ShapeDtypeStruct((half, front), F32),
            jax.ShapeDtypeStruct((tip, tip), F32),
        ],
        in_specs=[smem] + [pl.BlockSpec(memory_space=pltpu.VMEM)] * 5,
        out_specs=[pl.BlockSpec(memory_space=pltpu.VMEM)] * 2,
        scratch_shapes=system + [pltpu.VMEM((width, width), F32), pltpu.VMEM((LANES, LANES), F32)],
        compiler_params=params,
        name="merge",
    )(side, pivot, pivot_other, pack, pack_other, outer)
    return merged, tip_block + sum_over_pairs(tip_tip, "tm")


def solution(mesh):
    placed = (P("tm", None, None), P("tm", None, None), P("tm", None, None), P())
    return jax.shard_map(
        local, mesh=mesh, in_specs=placed, out_specs=(P("tm", None), P()), check_vma=False
    )
```

```python
import functools

import jax
import jax.numpy as jnp
from jax import lax
from jax.experimental import pallas as pl
from jax.experimental.pallas import tpu as pltpu
from jax.sharding import PartitionSpec as P

F32 = jnp.float32
BF16 = jnp.bfloat16
SUB = 8
LANES = 128
HALF = 256
NN = (((1,), (0,)), ((), ()))
NT = (((1,), (1,)), ((), ()))


def split(value):
    high = value.astype(BF16)
    return high, (value - high.astype(F32)).astype(BF16)


def dot3(left, right, dims=NN):
    one = functools.partial(lax.dot_general, dimension_numbers=dims, preferred_element_type=F32)
    return one(left[0], right[0]) + (one(left[0], right[1]) + one(left[1], right[0]))


def row_of(value, index):
    return jnp.broadcast_to(value[index : index + 1, :], (SUB, LANES))


def column_of(value, index):
    return jnp.broadcast_to(value[:, index : index + 1], (SUB, LANES))


def total(terms):
    while len(terms) > 1:
        terms = [terms[k] + terms[k + 1] for k in range(0, len(terms), 2)]
    return terms[0]


def cleared(value, start, top):
    lane = lax.broadcasted_iota(jnp.int32, (SUB, LANES), 1)
    panel = (lane >= start) & (lane < start + SUB)
    terms = [column_of(value, start + k) * top[k] for k in range(SUB)]
    return jnp.where(panel, 0.0, value) - total(terms)


def late_update(work, step, top):
    value = work[...]
    high, low = split(
        jnp.concatenate([jnp.where(step % 2 == k, top, jnp.zeros_like(top)) for k in (0, 1)], axis=0)
    )
    right = tuple(
        jnp.concatenate(
            [jnp.where(step // 2 == k, part, jnp.zeros_like(part)) for k in range(8)], axis=0
        )
        for part in (high, low)
    )
    lane = lax.broadcasted_iota(jnp.int32, (LANES, LANES), 1)
    panel = (lane >= SUB * step) & (lane < SUB * (step + 1))
    work[...] = jnp.where(panel, 0.0, value) - dot3(split(value), right)
    work[pl.ds(pl.multiple_of(SUB * step, SUB), SUB), :] = top


def eliminated(value, pivot, first, second, corner, inverse):
    sub = lax.broadcasted_iota(jnp.int32, (SUB, LANES), 0)
    a, b, d = corner
    upper, lower = row_of(value, pivot), row_of(value, pivot + 1)
    upper, lower = d * upper - b * lower, a * lower - b * upper
    product = first * upper + second * lower
    rest = value - product * inverse
    return jnp.where(
        sub == pivot, upper * inverse, jnp.where(sub == pivot + 1, lower * inverse, rest)
    )


def panel_step(work, step, state, late):
    row, columns, last = state[0], list(state[1:9]), state[9]
    sub = lax.broadcasted_iota(jnp.int32, (SUB, LANES), 0)
    lane = lax.broadcasted_iota(jnp.int32, (SUB, LANES), 1)
    following = work[pl.ds(pl.multiple_of((step + 1) % 16 * SUB, SUB), SUB), :]
    if late:
        late_update(work, step - 1, last)
        before = pltpu.roll(last, (LANES + SUB - SUB * step) % LANES, 1)
        following = pltpu.roll(following, (LANES + SUB - SUB * step) % LANES, 1)
        following = cleared(following, 0, [row_of(before, k) for k in range(SUB)])
        following = pltpu.roll(following, LANES - SUB, 1)
    top = jnp.where(lane < SUB, jnp.where(lane == sub, 1.0, 0.0).astype(F32), row)
    for pivot in range(0, SUB, 2):
        a = row_of(columns[pivot], pivot)
        b = row_of(columns[pivot + 1], pivot)
        d = row_of(columns[pivot + 1], pivot + 1)
        inverse = pltpu.reciprocal(a * d - b * b)
        pair = (columns[pivot], columns[pivot + 1], (a, b, d), inverse)
        columns[pivot + 2 :] = [eliminated(value, pivot, *pair) for value in columns[pivot + 2 :]]
        top = eliminated(top, pivot, *pair)
    following = cleared(following, 0, [row_of(top, k) for k in range(SUB)])
    columns = [column_of(following, SUB + k) for k in range(SUB)]
    row = pltpu.roll(following, LANES - SUB, 1)
    return (row, *columns, pltpu.roll(top, SUB * step, 1))


def invert_128(blocks, works):
    states = []
    for block, work in zip(blocks, works):
        work[...] = block
        row = block[:SUB, :]
        columns = [column_of(row, k) for k in range(SUB)]
        states.append(panel_step(work, 0, (row, *columns, row), False))

    def step(index, carry):
        return tuple(panel_step(work, index, state, True) for work, state in zip(works, carry))

    states = lax.fori_loop(1, 16, step, tuple(states), unroll=3)
    for work, state in zip(works, states):
        late_update(work, 15, state[9])
    return [work[...] for work in works]


def invert_256(blocks, works):
    firsts = invert_128([block[0] for block in blocks], works)
    seconds, sides = [], []
    for first, (_, right, below, last) in zip(firsts, blocks):
        first, right, below = split(first), split(right), split(below)
        low = split(dot3(below, first))
        seconds.append(last - dot3(low, right))
        sides.append((low, split(dot3(first, right))))
    results = []
    for first, second, (low, high) in zip(firsts, invert_128(seconds, works), sides):
        corner = split(second)
        below = dot3(corner, low)
        top = jnp.concatenate([first + dot3(high, split(below)), -dot3(high, corner)], axis=1)
        bottom = jnp.concatenate([-below, second], axis=1)
        results.append(jnp.concatenate([top, bottom], axis=0))
    return results


def quarters(value):
    return (
        value[:LANES, :LANES],
        value[:LANES, LANES:],
        value[LANES:, :LANES],
        value[LANES:, LANES:],
    )


def chunks(count):
    return [(start, min(HALF, count - start)) for start in range(0, count, HALF)]


def equilibrate(pivot):
    width = pivot.shape[0]
    row = lax.broadcasted_iota(jnp.int32, (LANES, LANES), 0)
    lane = lax.broadcasted_iota(jnp.int32, (LANES, LANES), 1)
    scales = []
    for start in range(0, width, LANES):
        block = pivot[start : start + LANES, start : start + LANES]
        scales.append(lax.rsqrt(jnp.sum(jnp.where(row == lane, block, 0.0), axis=0, keepdims=True)))
    for index, scale in enumerate(scales):
        rows = pl.ds(index * LANES, LANES)
        down = jnp.broadcast_to(scale, (LANES, LANES)).T
        for other, across in enumerate(scales):
            lanes = pl.ds(other * LANES, LANES)
            pivot[rows, lanes] = pivot[rows, lanes] * down * across
    return jnp.concatenate(scales, axis=1)


def eliminate(systems, works):
    scales = [equilibrate(system[0]) for system in systems]
    upper = [quarters(system[0][:HALF, :HALF]) for system in systems]
    upper = [split(value) for value in invert_256(upper, works)]
    lower = []
    for (pivot, g, gh, gl, zh, zl), inverse, scale in zip(systems, upper, scales):
        right = split(pivot[:HALF, HALF:])
        low = split(dot3(split(pivot[HALF:, :HALF]), inverse))
        lower.append(pivot[HALF:, HALF:] - dot3(low, right))
        for start, size in chunks(g.shape[0]):
            rows = pl.ds(start, size)
            part = split(g[rows, :HALF] * scale[:, :HALF])
            gh[rows, :HALF], gl[rows, :HALF] = part
            solved = split(dot3(part, inverse))
            zh[rows, :HALF], zl[rows, :HALF] = solved
            part = split(g[rows, HALF:] * scale[:, HALF:] - dot3(solved, right))
            gh[rows, HALF:], gl[rows, HALF:] = part
    lower = [split(x) for x in invert_256([quarters(value) for value in lower], works)]
    for (pivot, g, gh, gl, zh, zl), inverse in zip(systems, lower):
        for start, size in chunks(g.shape[0]):
            rows = pl.ds(start, size)
            solved = split(dot3((gh[rows, HALF:], gl[rows, HALF:]), inverse))
            zh[rows, HALF:], zl[rows, HALF:] = solved


def update(system, row, rows, column, columns):
    _, _, gh, gl, zh, zl = system
    row, column = pl.ds(row, rows), pl.ds(column, columns)
    return dot3((zh[row, :], zl[row, :]), (gh[column, :], gl[column, :]), NT)


def transpose_into(target, row, source):
    width = source.shape[1]
    for i in range(0, width, LANES):
        for j in range(0, source.shape[0], LANES):
            target[row + i : row + i + LANES, j : j + LANES] = source[
                j : j + LANES, i : i + LANES
            ].T


def front_kernel(
    side, diag, lower, arrow, pivot_out, pack_out, outer_out,
    dv, lv, av, ga, gah, gal, zah, zal, gb, gbh, gbl, zbh, zbl, pivot, work, sems,
):
    width, tip = diag.shape[1], arrow.shape[1]
    two = 2 * width
    order = [
        (diag, dv, 1), (diag, dv, 3), (lower, lv, 0), (lower, lv, 1), (lower, lv, 2), (lower, lv, 3),
        (arrow, av, 1), (arrow, av, 3), (diag, dv, 2), (arrow, av, 2), (diag, dv, 0), (arrow, av, 0),
    ]
    copies = [
        pltpu.make_async_copy(source.at[k], target.at[k], sems.at[n])
        for n, (source, target, k) in enumerate(order)
    ]
    for copy in copies:
        copy.start()
    for copy in copies:
        copy.wait()
    is_left = side[0] == 0

    transpose_into(ga, 0, lv.at[0])
    ga[width:two, :] = lv[1]
    ga[two:, :] = av[1]
    gb[:width, :] = lv[3]
    transpose_into(gb, width, lv.at[2])
    gb[two:, :] = av[3]
    first = (dv.at[1], ga, gah, gal, zah, zal)
    third = (dv.at[3], gb, gbh, gbl, zbh, zbl)
    outer_out[...] = dv[3]
    eliminate([first, third], [work.at[0], work.at[1]])

    def pick(left, right):
        return jnp.where(is_left, left, right)

    def drop(value):
        return jnp.where(is_left, value, jnp.zeros_like(value))

    for start, size in chunks(width):
        rows = pl.ds(start, size)
        shared = pl.ds(width + start, size)
        e = (width + start, size, width, width)
        pivot[rows, :] = dv[2, rows, :] - update(first, *e) - drop(update(third, *e))
        fe = (start, size, width, width)
        near = -update(first, *fe)
        far = -update(third, *fe)
        ga[rows, :] = pick(near, lv[2, rows, :])
        ga[shared, :] = pick(far, near)
        ff = (start, size, 0, width)
        near = dv[0, rows, :] - update(first, *ff)
        far = -update(third, *ff)
        pivot_out[rows, :] = pick(far, near)
        outer_out[rows, :] = pick(near, outer_out[rows, :])
    te = (two, tip, width, width)
    ga[two:, :] = av[2] - update(first, *te) - drop(update(third, *te))
    tf = (two, tip, 0, width)
    near = av[0] - update(first, *tf)
    far = -update(third, *tf)
    tip_pivot = pick(far, near)
    tip_outer = pick(near, av[3])
    tt = (two, tip, two, tip)
    tip_tip = -update(first, *tt) - drop(update(third, *tt))

    second = (pivot, ga, gah, gal, zah, zal)
    eliminate([second], [work.at[0]])
    for start, size in chunks(width):
        rows = pl.ds(start, size)
        pivot_out[rows, :] = pivot_out[rows, :] - update(second, width + start, size, width, width)
        pack_out[rows, :] = -update(second, start, size, width, width)
        outer_out[rows, :] = outer_out[rows, :] - update(second, start, size, 0, width)
    pivot_out[width : width + tip, :] = tip_pivot - update(second, two, tip, width, width)
    pivot_out[width + tip :, :] = jnp.zeros((tip, width), F32)
    pivot_out[width + tip :, :tip] = tip_tip - update(second, *tt)
    pack_out[width : width + tip, :] = tip_outer - update(second, two, tip, 0, width)
    spill = pack_out.shape[0] - width - tip
    pack_out[width + tip :, :] = outer_out[:spill, :]


def invert_512(pivot, work):
    scale = equilibrate(pivot)
    (first,) = invert_256([quarters(pivot[:HALF, :HALF])], [work])
    right = split(pivot[:HALF, HALF:])
    below = split(pivot[HALF:, :HALF])
    upper = split(first)
    low = split(dot3(below, upper))
    high = split(dot3(upper, right))
    (second,) = invert_256([quarters(pivot[HALF:, HALF:] - dot3(low, right))], [work])
    corner = split(second)
    below = dot3(corner, low)
    pivot[:HALF, :HALF] = first + dot3(high, split(below))
    pivot[:HALF, HALF:] = -dot3(high, corner)
    pivot[HALF:, :HALF] = -below
    pivot[HALF:, HALF:] = second
    for start in range(0, pivot.shape[0], LANES):
        rows = pl.ds(start, LANES)
        down = jnp.broadcast_to(scale[:, start : start + LANES], (LANES, LANES)).T
        for lanes in range(0, pivot.shape[0], LANES):
            across = scale[:, lanes : lanes + LANES]
            lanes = pl.ds(lanes, LANES)
            pivot[rows, lanes] = pivot[rows, lanes] * down * across


def factor_kernel(mine, other, inverse, tip_out, work):
    width, tip = inverse.shape[0], tip_out.shape[0]
    inverse[...] = mine[:width, :] + other[:width, :]
    invert_512(inverse, work)
    at = pl.ds(width, tip)
    coupling = split(mine[at, :] + other[at, :])
    solved = split(dot3(coupling, split(inverse[...])))
    at = pl.ds(width + tip, tip)
    tip_out[...] = mine[at, :tip] + other[at, :tip] - dot3(solved, coupling, NT)


def merge_kernel(
    side, inverse, tip_tip, pivot_mine, pivot_other, pack_mine, pack_other, outer_mine, merged,
    gh, gl, zh, zl,
):
    width, tip = inverse.shape[0], tip_tip.shape[0]
    two = 2 * width
    half = merged.shape[0]
    spill = half - width
    is_left = side[0] == 0
    for start, size in chunks(width):
        rows = pl.ds(start, size)
        mine, other = split(pack_mine[rows, :]), split(pack_other[rows, :])
        gh[rows, :] = jnp.where(is_left, mine[0], other[0])
        gl[rows, :] = jnp.where(is_left, mine[1], other[1])
        rows = pl.ds(width + start, size)
        gh[rows, :] = jnp.where(is_left, other[0], mine[0])
        gl[rows, :] = jnp.where(is_left, other[1], mine[1])
    at = pl.ds(width, tip)
    gh[two:, :], gl[two:, :] = split(pivot_mine[at, :] + pivot_other[at, :])
    solver = split(inverse[...])
    system = (None, None, gh, gl, zh, zl)
    outer_tip = pl.ds(width, tip)

    def solve(start, size):
        rows = pl.ds(start, size)
        zh[rows, :], zl[rows, :] = split(dot3((gh[rows, :], gl[rows, :]), solver))

    @pl.when(is_left)
    def _():
        for start, size in chunks(half):
            solve(start, size)
        for start, size in chunks(width):
            rows = pl.ds(start, size)
            merged[rows, :width] = outer_mine[rows, :] - update(system, start, size, 0, width)
            merged[rows, width:two] = -update(system, start, size, width, width)
            mine = pack_mine[outer_tip, start : start + size].T
            merged[rows, two:] = mine - update(system, start, size, two, tip)
        merged[width:, :width] = -update(system, width, spill, 0, width)
        other = pack_other[width + tip :, :]
        merged[width:, width:two] = other - update(system, width, spill, width, width)
        other = pack_other[outer_tip, :LANES].T[:spill, :]
        merged[width:, two:] = other - update(system, width, spill, two, tip)

    @pl.when(jnp.logical_not(is_left))
    def _():
        for start, size in chunks(width + tip):
            solve(width + start, size)
        for start, size in chunks(width):
            skip = spill if start == 0 else 0
            rows = pl.ds(start + skip - spill, size - skip)
            merged[rows, :width] = -update(system, width + start, size, 0, width)[skip:, :]
            mine = outer_mine[pl.ds(start, size), :]
            merged[rows, width:two] = (
                mine - update(system, width + start, size, width, width)
            )[skip:, :]
            mine = pack_mine[outer_tip, start : start + size].T
            merged[rows, two:] = (mine - update(system, width + start, size, two, tip))[skip:, :]
        rows = pl.ds(half - tip, tip)
        merged[rows, :width] = pack_other[outer_tip, :] - update(system, two, tip, 0, width)
        merged[rows, width:two] = pack_mine[outer_tip, :] - update(system, two, tip, width, width)
        merged[rows, two:] = tip_tip[...]


def swapped(value, axis, mask):
    count = lax.axis_size(axis)
    return lax.ppermute(value, axis, [(k, k ^ mask) for k in range(count)])


def sum_over_pairs(value, axis):
    step = 2
    while step < lax.axis_size(axis):
        if 2 * step < lax.axis_size(axis):
            near, far, across = (swapped(value, axis, step * k) for k in (1, 2, 3))
            value = (value + near) + (far + across)
            step *= 4
        else:
            value = value + swapped(value, axis, step)
            step *= 2
    return value


def local(diag_blocks, lower_blocks, arrow_blocks, tip_block):
    count, width = diag_blocks.shape[:2]
    tip = arrow_blocks.shape[1]
    front = 2 * width + tip
    half = front // 2
    spill = half - width
    side = (lax.axis_index("tm") % 2).astype(jnp.int32).reshape(1)
    smem = pl.BlockSpec(memory_space=pltpu.SMEM)
    vmem = pl.BlockSpec(memory_space=pltpu.VMEM)
    parts = [pltpu.VMEM((front, width), BF16)] * 4
    system = [pltpu.VMEM((front, width), F32)] + parts
    params = pltpu.CompilerParams(vmem_limit_bytes=56 * 2**20)
    pivot, pack, outer = pl.pallas_call(
        front_kernel,
        out_shape=[
            jax.ShapeDtypeStruct((width + 2 * tip, width), F32),
            jax.ShapeDtypeStruct((width + tip + spill, width), F32),
            jax.ShapeDtypeStruct((width, width), F32),
        ],
        in_specs=[smem] + [pl.BlockSpec(memory_space=pl.ANY)] * 3,
        out_specs=[vmem] * 3,
        scratch_shapes=[
            pltpu.VMEM((count, width, width), F32),
            pltpu.VMEM((count, width, width), F32),
            pltpu.VMEM((count, tip, width), F32),
        ]
        + system
        + system
        + [pltpu.VMEM((width, width), F32), pltpu.VMEM((2, LANES, LANES), F32)]
        + [pltpu.SemaphoreType.DMA((3 * count,))],
        compiler_params=params,
        name="front",
    )(side, diag_blocks, lower_blocks, arrow_blocks)
    pivot_other = swapped(pivot, "tm", 1)
    pack_other = swapped(pack, "tm", 1)
    inverse, tip_tip = pl.pallas_call(
        factor_kernel,
        out_shape=[
            jax.ShapeDtypeStruct((width, width), F32),
            jax.ShapeDtypeStruct((tip, tip), F32),
        ],
        in_specs=[vmem] * 2,
        out_specs=[vmem] * 2,
        scratch_shapes=[pltpu.VMEM((LANES, LANES), F32)],
        compiler_params=pltpu.CompilerParams(vmem_limit_bytes=24 * 2**20),
        cost_estimate=pl.CostEstimate(flops=10**10, bytes_accessed=10**7, transcendentals=0),
        name="factor",
    )(pivot, pivot_other)
    merged = pl.pallas_call(
        merge_kernel,
        out_shape=jax.ShapeDtypeStruct((half, front), F32),
        in_specs=[smem] + [vmem] * 7,
        out_specs=vmem,
        scratch_shapes=parts,
        compiler_params=pltpu.CompilerParams(vmem_limit_bytes=40 * 2**20),
        cost_estimate=pl.CostEstimate(flops=5 * 10**9, bytes_accessed=10**7, transcendentals=0),
        name="merge",
    )(side, inverse, tip_tip, pivot, pivot_other, pack, pack_other, outer)
    return merged, tip_block + sum_over_pairs(tip_tip, "tm")


def solution(mesh):
    placed = (P("tm", None, None), P("tm", None, None), P("tm", None, None), P())
    return jax.shard_map(
        local, mesh=mesh, in_specs=placed, out_specs=(P("tm", None), P()), check_vma=False
    )
```

```python
import functools

import jax
import jax.numpy as jnp
from jax import lax
from jax.experimental import pallas as pl
from jax.experimental.pallas import tpu as pltpu
from jax.sharding import PartitionSpec as P

F32 = jnp.float32
BF16 = jnp.bfloat16
SUB = 8
PAIR = 16
LANES = 128
HALF = 256
NN = (((1,), (0,)), ((), ()))
NT = (((1,), (1,)), ((), ()))


def split(value):
    high = value.astype(BF16)
    return high, (value - high.astype(F32)).astype(BF16)


def dot3(left, right, dims=NN):
    one = functools.partial(lax.dot_general, dimension_numbers=dims, preferred_element_type=F32)
    return one(left[0], right[0]) + (one(left[0], right[1]) + one(left[1], right[0]))


def row_of(value, index):
    return jnp.broadcast_to(value[index : index + 1, :], (SUB, LANES))


def column_of(value, index):
    return jnp.broadcast_to(value[:, index : index + 1], (SUB, LANES))


def total(terms):
    while len(terms) > 1:
        terms = [terms[k] + terms[k + 1] for k in range(0, len(terms), 2)]
    return terms[0]


def cleared(value, start, top):
    lane = lax.broadcasted_iota(jnp.int32, (SUB, LANES), 1)
    panel = (lane >= start) & (lane < start + SUB)
    terms = [column_of(value, start + k) * top[k] for k in range(SUB)]
    return jnp.where(panel, 0.0, value) - total(terms)


def late_update(work, step, top):
    value = work[...]
    right = tuple(
        jnp.concatenate(
            [jnp.where(step == k, part, jnp.zeros_like(part)) for k in range(8)], axis=0
        )
        for part in split(top)
    )
    lane = lax.broadcasted_iota(jnp.int32, (LANES, LANES), 1)
    panel = (lane >= PAIR * step) & (lane < PAIR * (step + 1))
    work[...] = jnp.where(panel, 0.0, value) - dot3(split(value), right)
    work[pl.ds(pl.multiple_of(PAIR * step, PAIR), PAIR), :] = top


def eliminated(value, pivot, first, second, corner, inverse):
    sub = lax.broadcasted_iota(jnp.int32, (SUB, LANES), 0)
    a, b, d = corner
    upper, lower = row_of(value, pivot), row_of(value, pivot + 1)
    upper, lower = d * upper - b * lower, a * lower - b * upper
    product = first * upper + second * lower
    rest = value - product * inverse
    return jnp.where(
        sub == pivot, upper * inverse, jnp.where(sub == pivot + 1, lower * inverse, rest)
    )


def turned(value, count):
    return pltpu.roll(value, (LANES - count) % LANES, 1)


def rows_of(value):
    return [row_of(value, k) for k in range(SUB)]


def columns_of(value, start):
    return [column_of(value, start + k) for k in range(SUB)]


def panel(row, columns):
    columns = list(columns)
    sub = lax.broadcasted_iota(jnp.int32, (SUB, LANES), 0)
    lane = lax.broadcasted_iota(jnp.int32, (SUB, LANES), 1)
    top = jnp.where(lane < SUB, jnp.where(lane == sub, 1.0, 0.0).astype(F32), row)
    for pivot in range(0, SUB, 2):
        a = row_of(columns[pivot], pivot)
        b = row_of(columns[pivot + 1], pivot)
        d = row_of(columns[pivot + 1], pivot + 1)
        inverse = pltpu.reciprocal(a * d - b * b)
        pair = (columns[pivot], columns[pivot + 1], (a, b, d), inverse)
        columns[pivot + 2 :] = [eliminated(value, pivot, *pair) for value in columns[pivot + 2 :]]
        top = eliminated(top, pivot, *pair)
    return top


def pair_step(work, step, state, late):
    first, second, columns, last = state[0], state[1], state[2:10], state[10]
    if late:
        late_update(work, step - 1, last)
    following = work[pl.ds(pl.multiple_of((step + 1) % 8 * PAIR, PAIR), PAIR), :]
    following = [turned(following[k : k + SUB, :], PAIR * step) for k in (0, SUB)]
    top = panel(first, columns)
    rows = rows_of(top)
    second = cleared(second, 0, rows)
    columns = columns_of(second, SUB)
    following = [turned(cleared(value, 0, rows), SUB) for value in following]
    bottom = panel(turned(second, SUB), columns)
    rows = rows_of(bottom)
    following = [cleared(value, 0, rows) for value in following]
    columns = columns_of(following[0], SUB)
    top = cleared(turned(top, SUB), 0, rows)
    last = jnp.concatenate([top, bottom], axis=0)
    last = pltpu.roll(last, (PAIR * step + SUB) % LANES, 1)
    return (*(turned(value, SUB) for value in following), *columns, last)


def invert_128(blocks, works):
    states = []
    for block, work in zip(blocks, works):
        work[...] = block
        rows = [block[:SUB, :], block[SUB:PAIR, :]]
        state = (*rows, *columns_of(rows[0], 0), block[:PAIR, :])
        states.append(pair_step(work, 0, state, False))

    def step(index, carry):
        return tuple(pair_step(work, index, state, True) for work, state in zip(works, carry))

    states = lax.fori_loop(1, 8, step, tuple(states))
    for work, state in zip(works, states):
        late_update(work, 7, state[10])
    return [work[...] for work in works]


def invert_256(blocks, works):
    firsts = invert_128([block[0] for block in blocks], works)
    seconds, sides = [], []
    for first, (_, right, below, last) in zip(firsts, blocks):
        first, right, below = split(first), split(right), split(below)
        low = split(dot3(below, first))
        seconds.append(last - dot3(low, right))
        sides.append((low, split(dot3(first, right))))
    results = []
    for first, second, (low, high) in zip(firsts, invert_128(seconds, works), sides):
        corner = split(second)
        below = dot3(corner, low)
        top = jnp.concatenate([first + dot3(high, split(below)), -dot3(high, corner)], axis=1)
        bottom = jnp.concatenate([-below, second], axis=1)
        results.append(jnp.concatenate([top, bottom], axis=0))
    return results


def quarters(value):
    return (
        value[:LANES, :LANES],
        value[:LANES, LANES:],
        value[LANES:, :LANES],
        value[LANES:, LANES:],
    )


def chunks(count):
    return [(start, min(HALF, count - start)) for start in range(0, count, HALF)]


def equilibrate(pivot):
    width = pivot.shape[0]
    row = lax.broadcasted_iota(jnp.int32, (LANES, LANES), 0)
    lane = lax.broadcasted_iota(jnp.int32, (LANES, LANES), 1)
    scales = []
    for start in range(0, width, LANES):
        block = pivot[start : start + LANES, start : start + LANES]
        scales.append(lax.rsqrt(jnp.sum(jnp.where(row == lane, block, 0.0), axis=0, keepdims=True)))
    for index, scale in enumerate(scales):
        rows = pl.ds(index * LANES, LANES)
        down = jnp.broadcast_to(scale, (LANES, LANES)).T
        for other, across in enumerate(scales):
            lanes = pl.ds(other * LANES, LANES)
            pivot[rows, lanes] = pivot[rows, lanes] * down * across
    return jnp.concatenate(scales, axis=1)


def eliminate(systems, works):
    scales = [equilibrate(system[0]) for system in systems]
    upper = [quarters(system[0][:HALF, :HALF]) for system in systems]
    upper = [split(value) for value in invert_256(upper, works)]
    lower = []
    for (pivot, g, gh, gl, zh, zl), inverse, scale in zip(systems, upper, scales):
        right = split(pivot[:HALF, HALF:])
        low = split(dot3(split(pivot[HALF:, :HALF]), inverse))
        lower.append(pivot[HALF:, HALF:] - dot3(low, right))
        for start, size in chunks(g.shape[0]):
            rows = pl.ds(start, size)
            part = split(g[rows, :HALF] * scale[:, :HALF])
            gh[rows, :HALF], gl[rows, :HALF] = part
            solved = split(dot3(part, inverse))
            zh[rows, :HALF], zl[rows, :HALF] = solved
            part = split(g[rows, HALF:] * scale[:, HALF:] - dot3(solved, right))
            gh[rows, HALF:], gl[rows, HALF:] = part
    lower = [split(x) for x in invert_256([quarters(value) for value in lower], works)]
    for (pivot, g, gh, gl, zh, zl), inverse in zip(systems, lower):
        for start, size in chunks(g.shape[0]):
            rows = pl.ds(start, size)
            solved = split(dot3((gh[rows, HALF:], gl[rows, HALF:]), inverse))
            zh[rows, HALF:], zl[rows, HALF:] = solved


def update(system, row, rows, column, columns):
    _, _, gh, gl, zh, zl = system
    row, column = pl.ds(row, rows), pl.ds(column, columns)
    return dot3((zh[row, :], zl[row, :]), (gh[column, :], gl[column, :]), NT)


def transpose_into(target, row, source):
    width = source.shape[1]
    for i in range(0, width, LANES):
        for j in range(0, source.shape[0], LANES):
            target[row + i : row + i + LANES, j : j + LANES] = source[
                j : j + LANES, i : i + LANES
            ].T


def front_kernel(
    side, diag, lower, arrow, pivot_out, pack_out, outer_out,
    dv, lv, av, ga, gah, gal, zah, zal, gb, gbh, gbl, zbh, zbl, pivot, work, work_b, sems,
):
    width, tip = diag.shape[1], arrow.shape[1]
    two = 2 * width
    order = [
        (diag, dv, 1), (diag, dv, 3), (lower, lv, 0), (lower, lv, 1), (lower, lv, 2), (lower, lv, 3),
        (arrow, av, 1), (arrow, av, 3), (diag, dv, 2), (arrow, av, 2), (diag, dv, 0), (arrow, av, 0),
    ]
    copies = [
        pltpu.make_async_copy(source.at[k], target.at[k], sems.at[n])
        for n, (source, target, k) in enumerate(order)
    ]
    for copy in copies:
        copy.start()
    for copy in copies:
        copy.wait()
    is_left = side[0] == 0

    transpose_into(ga, 0, lv.at[0])
    ga[width:two, :] = lv[1]
    ga[two:, :] = av[1]
    gb[:width, :] = lv[3]
    transpose_into(gb, width, lv.at[2])
    gb[two:, :] = av[3]
    first = (dv.at[1], ga, gah, gal, zah, zal)
    third = (dv.at[3], gb, gbh, gbl, zbh, zbl)
    outer_out[...] = dv[3]
    eliminate([first, third], [work, work_b])

    def pick(left, right):
        return jnp.where(is_left, left, right)

    def drop(value):
        return jnp.where(is_left, value, jnp.zeros_like(value))

    for start, size in chunks(width):
        rows = pl.ds(start, size)
        shared = pl.ds(width + start, size)
        e = (width + start, size, width, width)
        pivot[rows, :] = dv[2, rows, :] - update(first, *e) - drop(update(third, *e))
        fe = (start, size, width, width)
        near = -update(first, *fe)
        far = -update(third, *fe)
        ga[rows, :] = pick(near, lv[2, rows, :])
        ga[shared, :] = pick(far, near)
        ff = (start, size, 0, width)
        near = dv[0, rows, :] - update(first, *ff)
        far = -update(third, *ff)
        pivot_out[rows, :] = pick(far, near)
        outer_out[rows, :] = pick(near, outer_out[rows, :])
    te = (two, tip, width, width)
    ga[two:, :] = av[2] - update(first, *te) - drop(update(third, *te))
    tf = (two, tip, 0, width)
    near = av[0] - update(first, *tf)
    far = -update(third, *tf)
    tip_pivot = pick(far, near)
    tip_outer = pick(near, av[3])
    tt = (two, tip, two, tip)
    tip_tip = -update(first, *tt) - drop(update(third, *tt))

    second = (pivot, ga, gah, gal, zah, zal)
    eliminate([second], [work])
    for start, size in chunks(width):
        rows = pl.ds(start, size)
        pivot_out[rows, :] = pivot_out[rows, :] - update(second, width + start, size, width, width)
        pack_out[rows, :] = -update(second, start, size, width, width)
        outer_out[rows, :] = outer_out[rows, :] - update(second, start, size, 0, width)
    pivot_out[width : width + tip, :] = tip_pivot - update(second, two, tip, width, width)
    pivot_out[width + tip :, :] = jnp.zeros((tip, width), F32)
    pivot_out[width + tip :, :tip] = tip_tip - update(second, *tt)
    pack_out[width : width + tip, :] = tip_outer - update(second, two, tip, 0, width)
    spill = pack_out.shape[0] - width - tip
    pack_out[width + tip :, :] = outer_out[:spill, :]


def invert_512(pivot, work):
    scale = equilibrate(pivot)
    (first,) = invert_256([quarters(pivot[:HALF, :HALF])], [work])
    right = split(pivot[:HALF, HALF:])
    below = split(pivot[HALF:, :HALF])
    upper = split(first)
    low = split(dot3(below, upper))
    high = split(dot3(upper, right))
    (second,) = invert_256([quarters(pivot[HALF:, HALF:] - dot3(low, right))], [work])
    corner = split(second)
    below = dot3(corner, low)
    pivot[:HALF, :HALF] = first + dot3(high, split(below))
    pivot[:HALF, HALF:] = -dot3(high, corner)
    pivot[HALF:, :HALF] = -below
    pivot[HALF:, HALF:] = second
    for start in range(0, pivot.shape[0], LANES):
        rows = pl.ds(start, LANES)
        down = jnp.broadcast_to(scale[:, start : start + LANES], (LANES, LANES)).T
        for lanes in range(0, pivot.shape[0], LANES):
            across = scale[:, lanes : lanes + LANES]
            lanes = pl.ds(lanes, LANES)
            pivot[rows, lanes] = pivot[rows, lanes] * down * across


def factor_kernel(mine, other, inverse, tip_out, work):
    width, tip = inverse.shape[0], tip_out.shape[0]
    inverse[...] = mine[:width, :] + other[:width, :]
    invert_512(inverse, work)
    at = pl.ds(width, tip)
    coupling = split(mine[at, :] + other[at, :])
    solved = split(dot3(coupling, split(inverse[...])))
    at = pl.ds(width + tip, tip)
    tip_out[...] = mine[at, :tip] + other[at, :tip] - dot3(solved, coupling, NT)


def merge_kernel(
    side, inverse, tip_tip, pivot_mine, pivot_other, pack_mine, pack_other, outer_mine, merged,
    gh, gl, zh, zl,
):
    width, tip = inverse.shape[0], tip_tip.shape[0]
    two = 2 * width
    half = merged.shape[0]
    spill = half - width
    is_left = side[0] == 0
    for start, size in chunks(width):
        rows = pl.ds(start, size)
        mine, other = split(pack_mine[rows, :]), split(pack_other[rows, :])
        gh[rows, :] = jnp.where(is_left, mine[0], other[0])
        gl[rows, :] = jnp.where(is_left, mine[1], other[1])
        rows = pl.ds(width + start, size)
        gh[rows, :] = jnp.where(is_left, other[0], mine[0])
        gl[rows, :] = jnp.where(is_left, other[1], mine[1])
    at = pl.ds(width, tip)
    gh[two:, :], gl[two:, :] = split(pivot_mine[at, :] + pivot_other[at, :])
    solver = split(inverse[...])
    system = (None, None, gh, gl, zh, zl)
    outer_tip = pl.ds(width, tip)

    def solve(start, size):
        rows = pl.ds(start, size)
        zh[rows, :], zl[rows, :] = split(dot3((gh[rows, :], gl[rows, :]), solver))

    @pl.when(is_left)
    def _():
        for start, size in chunks(half):
            solve(start, size)
        for start, size in chunks(width):
            rows = pl.ds(start, size)
            merged[rows, :width] = outer_mine[rows, :] - update(system, start, size, 0, width)
            merged[rows, width:two] = -update(system, start, size, width, width)
            mine = pack_mine[outer_tip, start : start + size].T
            merged[rows, two:] = mine - update(system, start, size, two, tip)
        merged[width:, :width] = -update(system, width, spill, 0, width)
        other = pack_other[width + tip :, :]
        merged[width:, width:two] = other - update(system, width, spill, width, width)
        other = pack_other[outer_tip, :LANES].T[:spill, :]
        merged[width:, two:] = other - update(system, width, spill, two, tip)

    @pl.when(jnp.logical_not(is_left))
    def _():
        for start, size in chunks(width + tip):
            solve(width + start, size)
        for start, size in chunks(width):
            skip = spill if start == 0 else 0
            rows = pl.ds(start + skip - spill, size - skip)
            merged[rows, :width] = -update(system, width + start, size, 0, width)[skip:, :]
            mine = outer_mine[pl.ds(start, size), :]
            merged[rows, width:two] = (
                mine - update(system, width + start, size, width, width)
            )[skip:, :]
            mine = pack_mine[outer_tip, start : start + size].T
            merged[rows, two:] = (mine - update(system, width + start, size, two, tip))[skip:, :]
        rows = pl.ds(half - tip, tip)
        merged[rows, :width] = pack_other[outer_tip, :] - update(system, two, tip, 0, width)
        merged[rows, width:two] = pack_mine[outer_tip, :] - update(system, two, tip, width, width)
        merged[rows, two:] = tip_tip[...]


def swapped(value, axis, mask):
    count = lax.axis_size(axis)
    return lax.ppermute(value, axis, [(k, k ^ mask) for k in range(count)])


def sum_over_pairs(value, axis):
    step = 2
    while step < lax.axis_size(axis):
        if 2 * step < lax.axis_size(axis):
            near, far, across = (swapped(value, axis, step * k) for k in (1, 2, 3))
            value = (value + near) + (far + across)
            step *= 4
        else:
            value = value + swapped(value, axis, step)
            step *= 2
    return value


def local(diag_blocks, lower_blocks, arrow_blocks, tip_block):
    count, width = diag_blocks.shape[:2]
    tip = arrow_blocks.shape[1]
    front = 2 * width + tip
    half = front // 2
    spill = half - width
    side = (lax.axis_index("tm") % 2).astype(jnp.int32).reshape(1)
    smem = pl.BlockSpec(memory_space=pltpu.SMEM)
    vmem = pl.BlockSpec(memory_space=pltpu.VMEM)
    parts = [pltpu.VMEM((front, width), BF16)] * 4
    system = [pltpu.VMEM((front, width), F32)] + parts
    params = pltpu.CompilerParams(vmem_limit_bytes=56 * 2**20)
    pivot, pack, outer = pl.pallas_call(
        front_kernel,
        out_shape=[
            jax.ShapeDtypeStruct((width + 2 * tip, width), F32),
            jax.ShapeDtypeStruct((width + tip + spill, width), F32),
            jax.ShapeDtypeStruct((width, width), F32),
        ],
        in_specs=[smem] + [pl.BlockSpec(memory_space=pl.ANY)] * 3,
        out_specs=[vmem] * 3,
        scratch_shapes=[
            pltpu.VMEM((count, width, width), F32),
            pltpu.VMEM((count, width, width), F32),
            pltpu.VMEM((count, tip, width), F32),
        ]
        + system
        + system
        + [pltpu.VMEM((width, width), F32)]
        + [pltpu.VMEM((LANES, LANES), F32)] * 2
        + [pltpu.SemaphoreType.DMA((3 * count,))],
        compiler_params=params,
        name="front",
    )(side, diag_blocks, lower_blocks, arrow_blocks)
    pivot_other = swapped(pivot, "tm", 1)
    pack_other = swapped(pack, "tm", 1)
    inverse, tip_tip = pl.pallas_call(
        factor_kernel,
        out_shape=[
            jax.ShapeDtypeStruct((width, width), F32),
            jax.ShapeDtypeStruct((tip, tip), F32),
        ],
        in_specs=[vmem] * 2,
        out_specs=[vmem] * 2,
        scratch_shapes=[pltpu.VMEM((LANES, LANES), F32)],
        compiler_params=pltpu.CompilerParams(vmem_limit_bytes=24 * 2**20),
        cost_estimate=pl.CostEstimate(flops=10**10, bytes_accessed=10**7, transcendentals=0),
        name="factor",
    )(pivot, pivot_other)
    merged = pl.pallas_call(
        merge_kernel,
        out_shape=jax.ShapeDtypeStruct((half, front), F32),
        in_specs=[smem] + [vmem] * 7,
        out_specs=vmem,
        scratch_shapes=parts,
        compiler_params=pltpu.CompilerParams(vmem_limit_bytes=40 * 2**20),
        cost_estimate=pl.CostEstimate(flops=5 * 10**9, bytes_accessed=10**7, transcendentals=0),
        name="merge",
    )(side, inverse, tip_tip, pivot, pivot_other, pack, pack_other, outer)
    return merged, tip_block + sum_over_pairs(tip_tip, "tm")


def solution(mesh):
    placed = (P("tm", None, None), P("tm", None, None), P("tm", None, None), P())
    return jax.shard_map(
        local, mesh=mesh, in_specs=placed, out_specs=(P("tm", None), P()), check_vma=False
    )
```

```python
import functools

import jax
import jax.numpy as jnp
from jax import lax
from jax.experimental import pallas as pl
from jax.experimental.pallas import tpu as pltpu
from jax.sharding import PartitionSpec as P

F32 = jnp.float32
BF16 = jnp.bfloat16
SUB = 8
PAIR = 16
LANES = 128
HALF = 256
NN = (((1,), (0,)), ((), ()))
NT = (((1,), (1,)), ((), ()))


def split(value):
    high = value.astype(BF16)
    return high, (value - high.astype(F32)).astype(BF16)


def dot3(left, right, dims=NN):
    one = functools.partial(lax.dot_general, dimension_numbers=dims, preferred_element_type=F32)
    return one(left[0], right[0]) + (one(left[0], right[1]) + one(left[1], right[0]))


def row_of(value, index):
    return jnp.broadcast_to(value[index : index + 1, :], (SUB, LANES))


def column_of(value, index):
    return jnp.broadcast_to(value[:, index : index + 1], (SUB, LANES))


def total(terms):
    while len(terms) > 1:
        terms = [terms[k] + terms[k + 1] for k in range(0, len(terms), 2)]
    return terms[0]


def cleared(value, start, top):
    lane = lax.broadcasted_iota(jnp.int32, (SUB, LANES), 1)
    panel = (lane >= start) & (lane < start + len(top))
    terms = [column_of(value, start + k) * row for k, row in enumerate(top)]
    return jnp.where(panel, 0.0, value) - total(terms)


def late_update(work, step, top):
    value = work[...]
    right = tuple(
        jnp.concatenate(
            [jnp.where(step == k, part, jnp.zeros_like(part)) for k in range(8)], axis=0
        )
        for part in split(top)
    )
    lane = lax.broadcasted_iota(jnp.int32, (LANES, LANES), 1)
    panel = (lane >= PAIR * step) & (lane < PAIR * (step + 1))
    work[...] = jnp.where(panel, 0.0, value) - dot3(split(value), right)
    work[pl.ds(pl.multiple_of(PAIR * step, PAIR), PAIR), :] = top


def eliminated(value, pivot, first, second, corner, inverse):
    sub = lax.broadcasted_iota(jnp.int32, (SUB, LANES), 0)
    a, b, d = corner
    upper, lower = row_of(value, pivot), row_of(value, pivot + 1)
    upper, lower = d * upper - b * lower, a * lower - b * upper
    product = first * upper + second * lower
    rest = value - product * inverse
    return jnp.where(
        sub == pivot, upper * inverse, jnp.where(sub == pivot + 1, lower * inverse, rest)
    )


def turned(value, count):
    return pltpu.roll(value, (LANES - count) % LANES, 1)


def rows_of(value):
    return [row_of(value, k) for k in range(SUB)]


def columns_of(value, start):
    return [column_of(value, start + k) for k in range(SUB)]


def panel(row, columns, start):
    columns = list(columns)
    sub = lax.broadcasted_iota(jnp.int32, (SUB, LANES), 0)
    lane = lax.broadcasted_iota(jnp.int32, (SUB, LANES), 1) - start
    inside = (lane >= 0) & (lane < SUB)
    top = jnp.where(inside, jnp.where(lane == sub, 1.0, 0.0).astype(F32), row)
    for pivot in range(0, SUB, 2):
        a = row_of(columns[pivot], pivot)
        b = row_of(columns[pivot + 1], pivot)
        d = row_of(columns[pivot + 1], pivot + 1)
        inverse = pltpu.reciprocal(a * d - b * b)
        pair = (columns[pivot], columns[pivot + 1], (a, b, d), inverse)
        columns[pivot + 2 :] = [eliminated(value, pivot, *pair) for value in columns[pivot + 2 :]]
        top = eliminated(top, pivot, *pair)
    return top


def pair_step(work, step, state, late):
    first, second, columns, last = state[0], state[1], state[2:10], list(state[10:])
    following = work[pl.ds(pl.multiple_of((step + 1) % 8 * PAIR, PAIR), PAIR), :]
    following = [following[:SUB, :], following[SUB:, :]]
    if late:
        late_update(work, step - 1, pltpu.roll(jnp.concatenate(last, axis=0), PAIR * (step - 1), 1))
        rows = rows_of(last[0]) + rows_of(last[1])
        following = [turned(value, PAIR * (step - 1)) for value in following]
        following = [turned(cleared(value, 0, rows), PAIR) for value in following]
    top = panel(first, columns, 0)
    rows = rows_of(top)
    second = cleared(second, 0, rows)
    following = [cleared(value, 0, rows) for value in following]
    bottom = panel(second, columns_of(second, SUB), SUB)
    rows = rows_of(bottom)
    following = [cleared(value, SUB, rows) for value in following]
    top = cleared(top, SUB, rows)
    columns = columns_of(following[0], PAIR)
    return (*(turned(value, PAIR) for value in following), *columns, top, bottom)


def invert_128(blocks, works):
    states = []
    for block, work in zip(blocks, works):
        work[...] = block
        rows = [block[:SUB, :], block[SUB:PAIR, :]]
        state = (*rows, *columns_of(rows[0], 0), *rows)
        states.append(pair_step(work, 0, state, False))

    def step(index, carry):
        return tuple(pair_step(work, index, state, True) for work, state in zip(works, carry))

    states = lax.fori_loop(1, 8, step, tuple(states))
    for work, state in zip(works, states):
        late_update(work, 7, pltpu.roll(jnp.concatenate(state[10:], axis=0), 7 * PAIR, 1))
    return [work[...] for work in works]


def invert_256(blocks, works):
    firsts = invert_128([block[0] for block in blocks], works)
    seconds, sides = [], []
    for first, (_, right, below, last) in zip(firsts, blocks):
        first, right, below = split(first), split(right), split(below)
        low = split(dot3(below, first))
        seconds.append(last - dot3(low, right))
        sides.append((low, split(dot3(first, right))))
    results = []
    for first, second, (low, high) in zip(firsts, invert_128(seconds, works), sides):
        corner = split(second)
        below = dot3(corner, low)
        top = jnp.concatenate([first + dot3(high, split(below)), -dot3(high, corner)], axis=1)
        bottom = jnp.concatenate([-below, second], axis=1)
        results.append(jnp.concatenate([top, bottom], axis=0))
    return results


def quarters(value):
    return (
        value[:LANES, :LANES],
        value[:LANES, LANES:],
        value[LANES:, :LANES],
        value[LANES:, LANES:],
    )


def chunks(count):
    return [(start, min(HALF, count - start)) for start in range(0, count, HALF)]


def equilibrate(pivot):
    width = pivot.shape[0]
    row = lax.broadcasted_iota(jnp.int32, (LANES, LANES), 0)
    lane = lax.broadcasted_iota(jnp.int32, (LANES, LANES), 1)
    scales = []
    for start in range(0, width, LANES):
        block = pivot[start : start + LANES, start : start + LANES]
        scales.append(lax.rsqrt(jnp.sum(jnp.where(row == lane, block, 0.0), axis=0, keepdims=True)))
    for index, scale in enumerate(scales):
        rows = pl.ds(index * LANES, LANES)
        down = jnp.broadcast_to(scale, (LANES, LANES)).T
        for other, across in enumerate(scales):
            lanes = pl.ds(other * LANES, LANES)
            pivot[rows, lanes] = pivot[rows, lanes] * down * across
    return jnp.concatenate(scales, axis=1)


def eliminate(systems, works):
    scales = [equilibrate(system[0]) for system in systems]
    upper = [quarters(system[0][:HALF, :HALF]) for system in systems]
    upper = [split(value) for value in invert_256(upper, works)]
    lower = []
    for (pivot, g, gh, gl, zh, zl), inverse, scale in zip(systems, upper, scales):
        right = split(pivot[:HALF, HALF:])
        low = split(dot3(split(pivot[HALF:, :HALF]), inverse))
        lower.append(pivot[HALF:, HALF:] - dot3(low, right))
        for start, size in chunks(g.shape[0]):
            rows = pl.ds(start, size)
            part = split(g[rows, :HALF] * scale[:, :HALF])
            gh[rows, :HALF], gl[rows, :HALF] = part
            solved = split(dot3(part, inverse))
            zh[rows, :HALF], zl[rows, :HALF] = solved
            part = split(g[rows, HALF:] * scale[:, HALF:] - dot3(solved, right))
            gh[rows, HALF:], gl[rows, HALF:] = part
    lower = [split(x) for x in invert_256([quarters(value) for value in lower], works)]
    for (pivot, g, gh, gl, zh, zl), inverse in zip(systems, lower):
        for start, size in chunks(g.shape[0]):
            rows = pl.ds(start, size)
            solved = split(dot3((gh[rows, HALF:], gl[rows, HALF:]), inverse))
            zh[rows, HALF:], zl[rows, HALF:] = solved


def update(system, row, rows, column, columns):
    _, _, gh, gl, zh, zl = system
    row, column = pl.ds(row, rows), pl.ds(column, columns)
    return dot3((zh[row, :], zl[row, :]), (gh[column, :], gl[column, :]), NT)


def transpose_into(target, row, source):
    width = source.shape[1]
    for i in range(0, width, LANES):
        for j in range(0, source.shape[0], LANES):
            target[row + i : row + i + LANES, j : j + LANES] = source[
                j : j + LANES, i : i + LANES
            ].T


def front_kernel(
    side, diag, lower, arrow, pivot_out, pack_out, outer_out,
    dv, lv, av, ga, gah, gal, zah, zal, gb, gbh, gbl, zbh, zbl, pivot, work, work_b, sems,
):
    width, tip = diag.shape[1], arrow.shape[1]
    two = 2 * width
    order = [
        (diag, dv, 1), (diag, dv, 3), (lower, lv, 0), (lower, lv, 1), (lower, lv, 2), (lower, lv, 3),
        (arrow, av, 1), (arrow, av, 3), (diag, dv, 2), (arrow, av, 2), (diag, dv, 0), (arrow, av, 0),
    ]
    copies = [
        pltpu.make_async_copy(source.at[k], target.at[k], sems.at[n])
        for n, (source, target, k) in enumerate(order)
    ]
    for copy in copies:
        copy.start()
    for copy in copies:
        copy.wait()
    is_left = side[0] == 0

    transpose_into(ga, 0, lv.at[0])
    ga[width:two, :] = lv[1]
    ga[two:, :] = av[1]
    gb[:width, :] = lv[3]
    transpose_into(gb, width, lv.at[2])
    gb[two:, :] = av[3]
    first = (dv.at[1], ga, gah, gal, zah, zal)
    third = (dv.at[3], gb, gbh, gbl, zbh, zbl)
    outer_out[...] = dv[3]
    eliminate([first, third], [work, work_b])

    def pick(left, right):
        return jnp.where(is_left, left, right)

    def drop(value):
        return jnp.where(is_left, value, jnp.zeros_like(value))

    for start, size in chunks(width):
        rows = pl.ds(start, size)
        shared = pl.ds(width + start, size)
        e = (width + start, size, width, width)
        pivot[rows, :] = dv[2, rows, :] - update(first, *e) - drop(update(third, *e))
        fe = (start, size, width, width)
        near = -update(first, *fe)
        far = -update(third, *fe)
        ga[rows, :] = pick(near, lv[2, rows, :])
        ga[shared, :] = pick(far, near)
        ff = (start, size, 0, width)
        near = dv[0, rows, :] - update(first, *ff)
        far = -update(third, *ff)
        pivot_out[rows, :] = pick(far, near)
        outer_out[rows, :] = pick(near, outer_out[rows, :])
    te = (two, tip, width, width)
    ga[two:, :] = av[2] - update(first, *te) - drop(update(third, *te))
    tf = (two, tip, 0, width)
    near = av[0] - update(first, *tf)
    far = -update(third, *tf)
    tip_pivot = pick(far, near)
    tip_outer = pick(near, av[3])
    tt = (two, tip, two, tip)
    tip_tip = -update(first, *tt) - drop(update(third, *tt))

    second = (pivot, ga, gah, gal, zah, zal)
    eliminate([second], [work])
    for start, size in chunks(width):
        rows = pl.ds(start, size)
        pivot_out[rows, :] = pivot_out[rows, :] - update(second, width + start, size, width, width)
        pack_out[rows, :] = -update(second, start, size, width, width)
        outer_out[rows, :] = outer_out[rows, :] - update(second, start, size, 0, width)
    pivot_out[width : width + tip, :] = tip_pivot - update(second, two, tip, width, width)
    pivot_out[width + tip :, :] = jnp.zeros((tip, width), F32)
    pivot_out[width + tip :, :tip] = tip_tip - update(second, *tt)
    pack_out[width : width + tip, :] = tip_outer - update(second, two, tip, 0, width)
    spill = pack_out.shape[0] - width - tip
    pack_out[width + tip :, :] = outer_out[:spill, :]


def invert_512(pivot, work):
    scale = equilibrate(pivot)
    (first,) = invert_256([quarters(pivot[:HALF, :HALF])], [work])
    right = split(pivot[:HALF, HALF:])
    below = split(pivot[HALF:, :HALF])
    upper = split(first)
    low = split(dot3(below, upper))
    high = split(dot3(upper, right))
    (second,) = invert_256([quarters(pivot[HALF:, HALF:] - dot3(low, right))], [work])
    corner = split(second)
    below = dot3(corner, low)
    pivot[:HALF, :HALF] = first + dot3(high, split(below))
    pivot[:HALF, HALF:] = -dot3(high, corner)
    pivot[HALF:, :HALF] = -below
    pivot[HALF:, HALF:] = second
    for start in range(0, pivot.shape[0], LANES):
        rows = pl.ds(start, LANES)
        down = jnp.broadcast_to(scale[:, start : start + LANES], (LANES, LANES)).T
        for lanes in range(0, pivot.shape[0], LANES):
            across = scale[:, lanes : lanes + LANES]
            lanes = pl.ds(lanes, LANES)
            pivot[rows, lanes] = pivot[rows, lanes] * down * across


def factor_kernel(mine, other, inverse, tip_out, work):
    width, tip = inverse.shape[0], tip_out.shape[0]
    inverse[...] = mine[:width, :] + other[:width, :]
    invert_512(inverse, work)
    at = pl.ds(width, tip)
    coupling = split(mine[at, :] + other[at, :])
    solved = split(dot3(coupling, split(inverse[...])))
    at = pl.ds(width + tip, tip)
    tip_out[...] = mine[at, :tip] + other[at, :tip] - dot3(solved, coupling, NT)


def merge_kernel(
    side, inverse, tip_tip, pivot_mine, pivot_other, pack_mine, pack_other, outer_mine, merged,
    gh, gl, zh, zl,
):
    width, tip = inverse.shape[0], tip_tip.shape[0]
    two = 2 * width
    half = merged.shape[0]
    spill = half - width
    is_left = side[0] == 0
    for start, size in chunks(width):
        rows = pl.ds(start, size)
        mine, other = split(pack_mine[rows, :]), split(pack_other[rows, :])
        gh[rows, :] = jnp.where(is_left, mine[0], other[0])
        gl[rows, :] = jnp.where(is_left, mine[1], other[1])
        rows = pl.ds(width + start, size)
        gh[rows, :] = jnp.where(is_left, other[0], mine[0])
        gl[rows, :] = jnp.where(is_left, other[1], mine[1])
    at = pl.ds(width, tip)
    gh[two:, :], gl[two:, :] = split(pivot_mine[at, :] + pivot_other[at, :])
    solver = split(inverse[...])
    system = (None, None, gh, gl, zh, zl)
    outer_tip = pl.ds(width, tip)

    def solve(start, size):
        rows = pl.ds(start, size)
        zh[rows, :], zl[rows, :] = split(dot3((gh[rows, :], gl[rows, :]), solver))

    @pl.when(is_left)
    def _():
        for start, size in chunks(half):
            solve(start, size)
        for start, size in chunks(width):
            rows = pl.ds(start, size)
            merged[rows, :width] = outer_mine[rows, :] - update(system, start, size, 0, width)
            merged[rows, width:two] = -update(system, start, size, width, width)
            mine = pack_mine[outer_tip, start : start + size].T
            merged[rows, two:] = mine - update(system, start, size, two, tip)
        merged[width:, :width] = -update(system, width, spill, 0, width)
        other = pack_other[width + tip :, :]
        merged[width:, width:two] = other - update(system, width, spill, width, width)
        other = pack_other[outer_tip, :LANES].T[:spill, :]
        merged[width:, two:] = other - update(system, width, spill, two, tip)

    @pl.when(jnp.logical_not(is_left))
    def _():
        for start, size in chunks(width + tip):
            solve(width + start, size)
        for start, size in chunks(width):
            skip = spill if start == 0 else 0
            rows = pl.ds(start + skip - spill, size - skip)
            merged[rows, :width] = -update(system, width + start, size, 0, width)[skip:, :]
            mine = outer_mine[pl.ds(start, size), :]
            merged[rows, width:two] = (
                mine - update(system, width + start, size, width, width)
            )[skip:, :]
            mine = pack_mine[outer_tip, start : start + size].T
            merged[rows, two:] = (mine - update(system, width + start, size, two, tip))[skip:, :]
        rows = pl.ds(half - tip, tip)
        merged[rows, :width] = pack_other[outer_tip, :] - update(system, two, tip, 0, width)
        merged[rows, width:two] = pack_mine[outer_tip, :] - update(system, two, tip, width, width)
        merged[rows, two:] = tip_tip[...]


def swapped(value, axis, mask):
    count = lax.axis_size(axis)
    return lax.ppermute(value, axis, [(k, k ^ mask) for k in range(count)])


def sum_over_pairs(value, axis):
    step = 2
    while step < lax.axis_size(axis):
        if 2 * step < lax.axis_size(axis):
            near, far, across = (swapped(value, axis, step * k) for k in (1, 2, 3))
            value = (value + near) + (far + across)
            step *= 4
        else:
            value = value + swapped(value, axis, step)
            step *= 2
    return value


def local(diag_blocks, lower_blocks, arrow_blocks, tip_block):
    count, width = diag_blocks.shape[:2]
    tip = arrow_blocks.shape[1]
    front = 2 * width + tip
    half = front // 2
    spill = half - width
    side = (lax.axis_index("tm") % 2).astype(jnp.int32).reshape(1)
    smem = pl.BlockSpec(memory_space=pltpu.SMEM)
    vmem = pl.BlockSpec(memory_space=pltpu.VMEM)
    parts = [pltpu.VMEM((front, width), BF16)] * 4
    system = [pltpu.VMEM((front, width), F32)] + parts
    params = pltpu.CompilerParams(vmem_limit_bytes=56 * 2**20)
    pivot, pack, outer = pl.pallas_call(
        front_kernel,
        out_shape=[
            jax.ShapeDtypeStruct((width + 2 * tip, width), F32),
            jax.ShapeDtypeStruct((width + tip + spill, width), F32),
            jax.ShapeDtypeStruct((width, width), F32),
        ],
        in_specs=[smem] + [pl.BlockSpec(memory_space=pl.ANY)] * 3,
        out_specs=[vmem] * 3,
        scratch_shapes=[
            pltpu.VMEM((count, width, width), F32),
            pltpu.VMEM((count, width, width), F32),
            pltpu.VMEM((count, tip, width), F32),
        ]
        + system
        + system
        + [pltpu.VMEM((width, width), F32)]
        + [pltpu.VMEM((LANES, LANES), F32)] * 2
        + [pltpu.SemaphoreType.DMA((3 * count,))],
        compiler_params=params,
        name="front",
    )(side, diag_blocks, lower_blocks, arrow_blocks)
    pivot_other = swapped(pivot, "tm", 1)
    pack_other = swapped(pack, "tm", 1)
    inverse, tip_tip = pl.pallas_call(
        factor_kernel,
        out_shape=[
            jax.ShapeDtypeStruct((width, width), F32),
            jax.ShapeDtypeStruct((tip, tip), F32),
        ],
        in_specs=[vmem] * 2,
        out_specs=[vmem] * 2,
        scratch_shapes=[pltpu.VMEM((LANES, LANES), F32)],
        compiler_params=pltpu.CompilerParams(vmem_limit_bytes=24 * 2**20),
        cost_estimate=pl.CostEstimate(flops=10**10, bytes_accessed=10**7, transcendentals=0),
        name="factor",
    )(pivot, pivot_other)
    merged = pl.pallas_call(
        merge_kernel,
        out_shape=jax.ShapeDtypeStruct((half, front), F32),
        in_specs=[smem] + [vmem] * 7,
        out_specs=vmem,
        scratch_shapes=parts,
        compiler_params=pltpu.CompilerParams(vmem_limit_bytes=40 * 2**20),
        cost_estimate=pl.CostEstimate(flops=5 * 10**9, bytes_accessed=10**7, transcendentals=0),
        name="merge",
    )(side, inverse, tip_tip, pivot, pivot_other, pack, pack_other, outer)
    return merged, tip_block + sum_over_pairs(tip_tip, "tm")


def solution(mesh):
    placed = (P("tm", None, None), P("tm", None, None), P("tm", None, None), P())
    return jax.shard_map(
        local, mesh=mesh, in_specs=placed, out_specs=(P("tm", None), P()), check_vma=False
    )
```

```python
import functools

import jax
import jax.numpy as jnp
from jax import lax
from jax.experimental import pallas as pl
from jax.experimental.pallas import tpu as pltpu
from jax.sharding import PartitionSpec as P

F32 = jnp.float32
BF16 = jnp.bfloat16
SUB = 8
PAIR = 16
LANES = 128
HALF = 256
NN = (((1,), (0,)), ((), ()))
NT = (((1,), (1,)), ((), ()))


def split(value):
    high = value.astype(BF16)
    return high, (value - high.astype(F32)).astype(BF16)


def dot3(left, right, dims=NN):
    one = functools.partial(lax.dot_general, dimension_numbers=dims, preferred_element_type=F32)
    return one(left[0], right[0]) + (one(left[0], right[1]) + one(left[1], right[0]))


def row_of(value, index):
    return jnp.broadcast_to(value[index : index + 1, :], (SUB, LANES))


def column_of(value, index):
    return jnp.broadcast_to(value[:, index : index + 1], (SUB, LANES))


def total(terms):
    while len(terms) > 1:
        terms = [terms[k] + terms[k + 1] for k in range(0, len(terms), 2)]
    return terms[0]


def cleared(value, start, top):
    lane = lax.broadcasted_iota(jnp.int32, (SUB, LANES), 1)
    panel = (lane >= start) & (lane < start + len(top))
    terms = [column_of(value, start + k) * row for k, row in enumerate(top)]
    return jnp.where(panel, 0.0, value) - total(terms)


def late_update(work, step, top):
    value = work[...]
    right = tuple(
        jnp.concatenate(
            [jnp.where(step == k, part, jnp.zeros_like(part)) for k in range(8)], axis=0
        )
        for part in split(top)
    )
    lane = lax.broadcasted_iota(jnp.int32, (LANES, LANES), 1)
    panel = (lane >= PAIR * step) & (lane < PAIR * (step + 1))
    work[...] = jnp.where(panel, 0.0, value) - dot3(split(value), right)
    work[pl.ds(pl.multiple_of(PAIR * step, PAIR), PAIR), :] = top


def turned(value, count):
    return pltpu.roll(value, (LANES - count) % LANES, 1)


def rows_of(value):
    return [row_of(value, k) for k in range(SUB)]


def columns_of(value, start):
    return [column_of(value, start + k) for k in range(SUB)]


def panel(row, columns, start):
    sub = lax.broadcasted_iota(jnp.int32, (SUB, LANES), 0)
    lane = lax.broadcasted_iota(jnp.int32, (SUB, LANES), 1) - start
    inside = (lane >= 0) & (lane < SUB)
    rows = rows_of(jnp.where(inside, jnp.where(lane == sub, 1.0, 0.0).astype(F32), row))
    entry = {(i, k): row_of(columns[k], i) for k in range(SUB) for i in range(k, SUB)}
    factors = {}
    for k in range(0, SUB, 2):
        a, b, d = entry[k, k], entry[k + 1, k], entry[k + 1, k + 1]
        inverse = pltpu.reciprocal(a * d - b * b)
        below = range(k + 2, SUB)
        raw = {
            i: (d * entry[i, k] - b * entry[i, k + 1], a * entry[i, k + 1] - b * entry[i, k])
            for i in below
        }
        for i in below:
            factors[i, k], factors[i, k + 1] = raw[i][0] * inverse, raw[i][1] * inverse
        for j in below:
            for i in range(j, SUB):
                left = raw[i] if i < k + 4 else (factors[i, k], factors[i, k + 1])
                product = left[0] * entry[j, k] + left[1] * entry[j, k + 1]
                entry[i, j] = entry[i, j] - (product * inverse if i < k + 4 else product)
        for i in below:
            rows[i] = rows[i] - (factors[i, k] * rows[k] + factors[i, k + 1] * rows[k + 1])
        rows[k], rows[k + 1] = (
            (d * rows[k] - b * rows[k + 1]) * inverse,
            (a * rows[k + 1] - b * rows[k]) * inverse,
        )
    for k in range(SUB - 2, 0, -2):
        for i in range(k):
            rows[i] = rows[i] - (factors[k, i] * rows[k] + factors[k + 1, i] * rows[k + 1])
    return rows


def joined(rows):
    sub = lax.broadcasted_iota(jnp.int32, (SUB, LANES), 0)
    for half in (1, 2, 4):
        rows = [
            jnp.where(sub & half == 0, rows[k], rows[k + 1]) for k in range(0, len(rows), 2)
        ]
    return rows[0]


def pair_step(work, step, state, late):
    first, second, columns, last = state[0], state[1], state[2:10], list(state[10:])
    following = work[pl.ds(pl.multiple_of((step + 1) % 8 * PAIR, PAIR), PAIR), :]
    following = [following[:SUB, :], following[SUB:, :]]
    if late:
        late_update(work, step - 1, pltpu.roll(jnp.concatenate(last, axis=0), PAIR * (step - 1), 1))
        rows = rows_of(last[0]) + rows_of(last[1])
        following = [turned(value, PAIR * (step - 1)) for value in following]
        following = [turned(cleared(value, 0, rows), PAIR) for value in following]
    rows = panel(first, columns, 0)
    top = joined(rows)
    second = cleared(second, 0, rows)
    following = [cleared(value, 0, rows) for value in following]
    rows = panel(second, columns_of(second, SUB), SUB)
    bottom = joined(rows)
    following = [cleared(value, SUB, rows) for value in following]
    top = cleared(top, SUB, rows)
    columns = columns_of(following[0], PAIR)
    return (*(turned(value, PAIR) for value in following), *columns, top, bottom)


def invert_128(blocks, works):
    states = []
    for block, work in zip(blocks, works):
        work[...] = block
        rows = [block[:SUB, :], block[SUB:PAIR, :]]
        state = (*rows, *columns_of(rows[0], 0), *rows)
        states.append(pair_step(work, 0, state, False))

    def step(index, carry):
        return tuple(pair_step(work, index, state, True) for work, state in zip(works, carry))

    states = lax.fori_loop(1, 8, step, tuple(states))
    for work, state in zip(works, states):
        late_update(work, 7, pltpu.roll(jnp.concatenate(state[10:], axis=0), 7 * PAIR, 1))
    return [work[...] for work in works]


def invert_256(blocks, works):
    firsts = invert_128([block[0] for block in blocks], works)
    seconds, sides = [], []
    for first, (_, right, below, last) in zip(firsts, blocks):
        first, right, below = split(first), split(right), split(below)
        low = split(dot3(below, first))
        seconds.append(last - dot3(low, right))
        sides.append((low, split(dot3(first, right))))
    results = []
    for first, second, (low, high) in zip(firsts, invert_128(seconds, works), sides):
        corner = split(second)
        below = dot3(corner, low)
        top = jnp.concatenate([first + dot3(high, split(below)), -dot3(high, corner)], axis=1)
        bottom = jnp.concatenate([-below, second], axis=1)
        results.append(jnp.concatenate([top, bottom], axis=0))
    return results


def quarters(value):
    return (
        value[:LANES, :LANES],
        value[:LANES, LANES:],
        value[LANES:, :LANES],
        value[LANES:, LANES:],
    )


def chunks(count):
    return [(start, min(HALF, count - start)) for start in range(0, count, HALF)]


def equilibrate(pivot):
    width = pivot.shape[0]
    row = lax.broadcasted_iota(jnp.int32, (LANES, LANES), 0)
    lane = lax.broadcasted_iota(jnp.int32, (LANES, LANES), 1)
    scales = []
    for start in range(0, width, LANES):
        block = pivot[start : start + LANES, start : start + LANES]
        scales.append(lax.rsqrt(jnp.sum(jnp.where(row == lane, block, 0.0), axis=0, keepdims=True)))
    for index, scale in enumerate(scales):
        rows = pl.ds(index * LANES, LANES)
        down = jnp.broadcast_to(scale, (LANES, LANES)).T
        for other, across in enumerate(scales):
            lanes = pl.ds(other * LANES, LANES)
            pivot[rows, lanes] = pivot[rows, lanes] * down * across
    return jnp.concatenate(scales, axis=1)


def eliminate(systems, works):
    scales = [equilibrate(system[0]) for system in systems]
    upper = [quarters(system[0][:HALF, :HALF]) for system in systems]
    upper = [split(value) for value in invert_256(upper, works)]
    lower = []
    for (pivot, g, gh, gl, zh, zl), inverse, scale in zip(systems, upper, scales):
        right = split(pivot[:HALF, HALF:])
        low = split(dot3(split(pivot[HALF:, :HALF]), inverse))
        lower.append(pivot[HALF:, HALF:] - dot3(low, right))
        for start, size in chunks(g.shape[0]):
            rows = pl.ds(start, size)
            part = split(g[rows, :HALF] * scale[:, :HALF])
            gh[rows, :HALF], gl[rows, :HALF] = part
            solved = split(dot3(part, inverse))
            zh[rows, :HALF], zl[rows, :HALF] = solved
            part = split(g[rows, HALF:] * scale[:, HALF:] - dot3(solved, right))
            gh[rows, HALF:], gl[rows, HALF:] = part
    lower = [split(x) for x in invert_256([quarters(value) for value in lower], works)]
    for (pivot, g, gh, gl, zh, zl), inverse in zip(systems, lower):
        for start, size in chunks(g.shape[0]):
            rows = pl.ds(start, size)
            solved = split(dot3((gh[rows, HALF:], gl[rows, HALF:]), inverse))
            zh[rows, HALF:], zl[rows, HALF:] = solved


def update(system, row, rows, column, columns):
    _, _, gh, gl, zh, zl = system
    row, column = pl.ds(row, rows), pl.ds(column, columns)
    return dot3((zh[row, :], zl[row, :]), (gh[column, :], gl[column, :]), NT)


def transpose_into(target, row, source):
    width = source.shape[1]
    for i in range(0, width, LANES):
        for j in range(0, source.shape[0], LANES):
            target[row + i : row + i + LANES, j : j + LANES] = source[
                j : j + LANES, i : i + LANES
            ].T


def front_kernel(
    side, diag, lower, arrow, pivot_out, pack_out, outer_out,
    dv, lv, av, ga, gah, gal, zah, zal, gb, gbh, gbl, zbh, zbl, pivot, work, work_b, sems,
):
    width, tip = diag.shape[1], arrow.shape[1]
    two = 2 * width
    order = [
        (diag, dv, 1), (diag, dv, 3), (lower, lv, 0), (lower, lv, 1), (lower, lv, 2), (lower, lv, 3),
        (arrow, av, 1), (arrow, av, 3), (diag, dv, 2), (arrow, av, 2), (diag, dv, 0), (arrow, av, 0),
    ]
    copies = [
        pltpu.make_async_copy(source.at[k], target.at[k], sems.at[n])
        for n, (source, target, k) in enumerate(order)
    ]
    for copy in copies:
        copy.start()
    for copy in copies:
        copy.wait()
    is_left = side[0] == 0

    transpose_into(ga, 0, lv.at[0])
    ga[width:two, :] = lv[1]
    ga[two:, :] = av[1]
    gb[:width, :] = lv[3]
    transpose_into(gb, width, lv.at[2])
    gb[two:, :] = av[3]
    first = (dv.at[1], ga, gah, gal, zah, zal)
    third = (dv.at[3], gb, gbh, gbl, zbh, zbl)
    outer_out[...] = dv[3]
    eliminate([first, third], [work, work_b])

    def pick(left, right):
        return jnp.where(is_left, left, right)

    def drop(value):
        return jnp.where(is_left, value, jnp.zeros_like(value))

    for start, size in chunks(width):
        rows = pl.ds(start, size)
        shared = pl.ds(width + start, size)
        e = (width + start, size, width, width)
        pivot[rows, :] = dv[2, rows, :] - update(first, *e) - drop(update(third, *e))
        fe = (start, size, width, width)
        near = -update(first, *fe)
        far = -update(third, *fe)
        ga[rows, :] = pick(near, lv[2, rows, :])
        ga[shared, :] = pick(far, near)
        ff = (start, size, 0, width)
        near = dv[0, rows, :] - update(first, *ff)
        far = -update(third, *ff)
        pivot_out[rows, :] = pick(far, near)
        outer_out[rows, :] = pick(near, outer_out[rows, :])
    te = (two, tip, width, width)
    ga[two:, :] = av[2] - update(first, *te) - drop(update(third, *te))
    tf = (two, tip, 0, width)
    near = av[0] - update(first, *tf)
    far = -update(third, *tf)
    tip_pivot = pick(far, near)
    tip_outer = pick(near, av[3])
    tt = (two, tip, two, tip)
    tip_tip = -update(first, *tt) - drop(update(third, *tt))

    second = (pivot, ga, gah, gal, zah, zal)
    eliminate([second], [work])
    for start, size in chunks(width):
        rows = pl.ds(start, size)
        pivot_out[rows, :] = pivot_out[rows, :] - update(second, width + start, size, width, width)
        pack_out[rows, :] = -update(second, start, size, width, width)
        outer_out[rows, :] = outer_out[rows, :] - update(second, start, size, 0, width)
    pivot_out[width : width + tip, :] = tip_pivot - update(second, two, tip, width, width)
    pivot_out[width + tip :, :] = jnp.zeros((tip, width), F32)
    pivot_out[width + tip :, :tip] = tip_tip - update(second, *tt)
    pack_out[width : width + tip, :] = tip_outer - update(second, two, tip, 0, width)
    spill = pack_out.shape[0] - width - tip
    pack_out[width + tip :, :] = outer_out[:spill, :]


def invert_512(pivot, work):
    scale = equilibrate(pivot)
    (first,) = invert_256([quarters(pivot[:HALF, :HALF])], [work])
    right = split(pivot[:HALF, HALF:])
    below = split(pivot[HALF:, :HALF])
    upper = split(first)
    low = split(dot3(below, upper))
    high = split(dot3(upper, right))
    (second,) = invert_256([quarters(pivot[HALF:, HALF:] - dot3(low, right))], [work])
    corner = split(second)
    below = dot3(corner, low)
    pivot[:HALF, :HALF] = first + dot3(high, split(below))
    pivot[:HALF, HALF:] = -dot3(high, corner)
    pivot[HALF:, :HALF] = -below
    pivot[HALF:, HALF:] = second
    for start in range(0, pivot.shape[0], LANES):
        rows = pl.ds(start, LANES)
        down = jnp.broadcast_to(scale[:, start : start + LANES], (LANES, LANES)).T
        for lanes in range(0, pivot.shape[0], LANES):
            across = scale[:, lanes : lanes + LANES]
            lanes = pl.ds(lanes, LANES)
            pivot[rows, lanes] = pivot[rows, lanes] * down * across


def factor_kernel(mine, other, inverse, tip_out, work):
    width, tip = inverse.shape[0], tip_out.shape[0]
    inverse[...] = mine[:width, :] + other[:width, :]
    invert_512(inverse, work)
    at = pl.ds(width, tip)
    coupling = split(mine[at, :] + other[at, :])
    solved = split(dot3(coupling, split(inverse[...])))
    at = pl.ds(width + tip, tip)
    tip_out[...] = mine[at, :tip] + other[at, :tip] - dot3(solved, coupling, NT)


def merge_kernel(
    side, inverse, tip_tip, pivot_mine, pivot_other, pack_mine, pack_other, outer_mine, merged,
    gh, gl, zh, zl,
):
    width, tip = inverse.shape[0], tip_tip.shape[0]
    two = 2 * width
    half = merged.shape[0]
    spill = half - width
    is_left = side[0] == 0
    for start, size in chunks(width):
        rows = pl.ds(start, size)
        mine, other = split(pack_mine[rows, :]), split(pack_other[rows, :])
        gh[rows, :] = jnp.where(is_left, mine[0], other[0])
        gl[rows, :] = jnp.where(is_left, mine[1], other[1])
        rows = pl.ds(width + start, size)
        gh[rows, :] = jnp.where(is_left, other[0], mine[0])
        gl[rows, :] = jnp.where(is_left, other[1], mine[1])
    at = pl.ds(width, tip)
    gh[two:, :], gl[two:, :] = split(pivot_mine[at, :] + pivot_other[at, :])
    solver = split(inverse[...])
    system = (None, None, gh, gl, zh, zl)
    outer_tip = pl.ds(width, tip)

    def solve(start, size):
        rows = pl.ds(start, size)
        zh[rows, :], zl[rows, :] = split(dot3((gh[rows, :], gl[rows, :]), solver))

    @pl.when(is_left)
    def _():
        for start, size in chunks(half):
            solve(start, size)
        for start, size in chunks(width):
            rows = pl.ds(start, size)
            merged[rows, :width] = outer_mine[rows, :] - update(system, start, size, 0, width)
            merged[rows, width:two] = -update(system, start, size, width, width)
            mine = pack_mine[outer_tip, start : start + size].T
            merged[rows, two:] = mine - update(system, start, size, two, tip)
        merged[width:, :width] = -update(system, width, spill, 0, width)
        other = pack_other[width + tip :, :]
        merged[width:, width:two] = other - update(system, width, spill, width, width)
        other = pack_other[outer_tip, :LANES].T[:spill, :]
        merged[width:, two:] = other - update(system, width, spill, two, tip)

    @pl.when(jnp.logical_not(is_left))
    def _():
        for start, size in chunks(width + tip):
            solve(width + start, size)
        for start, size in chunks(width):
            skip = spill if start == 0 else 0
            rows = pl.ds(start + skip - spill, size - skip)
            merged[rows, :width] = -update(system, width + start, size, 0, width)[skip:, :]
            mine = outer_mine[pl.ds(start, size), :]
            merged[rows, width:two] = (
                mine - update(system, width + start, size, width, width)
            )[skip:, :]
            mine = pack_mine[outer_tip, start : start + size].T
            merged[rows, two:] = (mine - update(system, width + start, size, two, tip))[skip:, :]
        rows = pl.ds(half - tip, tip)
        merged[rows, :width] = pack_other[outer_tip, :] - update(system, two, tip, 0, width)
        merged[rows, width:two] = pack_mine[outer_tip, :] - update(system, two, tip, width, width)
        merged[rows, two:] = tip_tip[...]


def swapped(value, axis, mask):
    count = lax.axis_size(axis)
    return lax.ppermute(value, axis, [(k, k ^ mask) for k in range(count)])


def sum_over_pairs(value, axis):
    step = 2
    while step < lax.axis_size(axis):
        if 2 * step < lax.axis_size(axis):
            near, far, across = (swapped(value, axis, step * k) for k in (1, 2, 3))
            value = (value + near) + (far + across)
            step *= 4
        else:
            value = value + swapped(value, axis, step)
            step *= 2
    return value


def local(diag_blocks, lower_blocks, arrow_blocks, tip_block):
    count, width = diag_blocks.shape[:2]
    tip = arrow_blocks.shape[1]
    front = 2 * width + tip
    half = front // 2
    spill = half - width
    side = (lax.axis_index("tm") % 2).astype(jnp.int32).reshape(1)
    smem = pl.BlockSpec(memory_space=pltpu.SMEM)
    vmem = pl.BlockSpec(memory_space=pltpu.VMEM)
    parts = [pltpu.VMEM((front, width), BF16)] * 4
    system = [pltpu.VMEM((front, width), F32)] + parts
    params = pltpu.CompilerParams(vmem_limit_bytes=56 * 2**20)
    pivot, pack, outer = pl.pallas_call(
        front_kernel,
        out_shape=[
            jax.ShapeDtypeStruct((width + 2 * tip, width), F32),
            jax.ShapeDtypeStruct((width + tip + spill, width), F32),
            jax.ShapeDtypeStruct((width, width), F32),
        ],
        in_specs=[smem] + [pl.BlockSpec(memory_space=pl.ANY)] * 3,
        out_specs=[vmem] * 3,
        scratch_shapes=[
            pltpu.VMEM((count, width, width), F32),
            pltpu.VMEM((count, width, width), F32),
            pltpu.VMEM((count, tip, width), F32),
        ]
        + system
        + system
        + [pltpu.VMEM((width, width), F32)]
        + [pltpu.VMEM((LANES, LANES), F32)] * 2
        + [pltpu.SemaphoreType.DMA((3 * count,))],
        compiler_params=params,
        name="front",
    )(side, diag_blocks, lower_blocks, arrow_blocks)
    pivot_other = swapped(pivot, "tm", 1)
    pack_other = swapped(pack, "tm", 1)
    inverse, tip_tip = pl.pallas_call(
        factor_kernel,
        out_shape=[
            jax.ShapeDtypeStruct((width, width), F32),
            jax.ShapeDtypeStruct((tip, tip), F32),
        ],
        in_specs=[vmem] * 2,
        out_specs=[vmem] * 2,
        scratch_shapes=[pltpu.VMEM((LANES, LANES), F32)],
        compiler_params=pltpu.CompilerParams(vmem_limit_bytes=24 * 2**20),
        cost_estimate=pl.CostEstimate(flops=10**10, bytes_accessed=10**7, transcendentals=0),
        name="factor",
    )(pivot, pivot_other)
    merged = pl.pallas_call(
        merge_kernel,
        out_shape=jax.ShapeDtypeStruct((half, front), F32),
        in_specs=[smem] + [vmem] * 7,
        out_specs=vmem,
        scratch_shapes=parts,
        compiler_params=pltpu.CompilerParams(vmem_limit_bytes=40 * 2**20),
        cost_estimate=pl.CostEstimate(flops=5 * 10**9, bytes_accessed=10**7, transcendentals=0),
        name="merge",
    )(side, inverse, tip_tip, pivot, pivot_other, pack, pack_other, outer)
    return merged, tip_block + sum_over_pairs(tip_tip, "tm")


def solution(mesh):
    placed = (P("tm", None, None), P("tm", None, None), P("tm", None, None), P())
    return jax.shard_map(
        local, mesh=mesh, in_specs=placed, out_specs=(P("tm", None), P()), check_vma=False
    )
```

```python
import functools

import jax
import jax.numpy as jnp
from jax import lax
from jax.experimental import pallas as pl
from jax.experimental.pallas import tpu as pltpu
from jax.sharding import PartitionSpec as P

F32 = jnp.float32
BF16 = jnp.bfloat16
SUB = 8
PAIR = 16
LANES = 128
HALF = 256
CHUNK = 576
SLICE = 80
NN = (((1,), (0,)), ((), ()))
NT = (((1,), (1,)), ((), ()))


def split(value):
    high = value.astype(BF16)
    return high, (value - high.astype(F32)).astype(BF16)


def dot3(left, right, dims=NN):
    one = functools.partial(lax.dot_general, dimension_numbers=dims, preferred_element_type=F32)
    count = left[0].shape[0]
    both = one(jnp.concatenate(left, axis=0), right[0])
    return both[:count] + (both[count:] + one(left[0], right[1]))


def row_of(value, index):
    return jnp.broadcast_to(value[index : index + 1, :], (SUB, LANES))


def column_of(value, index):
    return jnp.broadcast_to(value[:, index : index + 1], (SUB, LANES))


def total(terms):
    while len(terms) > 1:
        terms = [terms[k] + terms[k + 1] for k in range(0, len(terms), 2)]
    return terms[0]


def cleared(value, start, top):
    lane = lax.broadcasted_iota(jnp.int32, (SUB, LANES), 1)
    panel = (lane >= start) & (lane < start + len(top))
    terms = [column_of(value, start + k) * row for k, row in enumerate(top)]
    return jnp.where(panel, 0.0, value) - total(terms)


def late_update(work, step, top):
    value = work[...]
    right = tuple(
        jnp.concatenate(
            [jnp.where(step == k, part, jnp.zeros_like(part)) for k in range(8)], axis=0
        )
        for part in split(top)
    )
    lane = lax.broadcasted_iota(jnp.int32, (LANES, LANES), 1)
    panel = (lane >= PAIR * step) & (lane < PAIR * (step + 1))
    work[...] = jnp.where(panel, 0.0, value) - dot3(split(value), right)
    work[pl.ds(pl.multiple_of(PAIR * step, PAIR), PAIR), :] = top


def eliminated(value, pivot, first, second, corner, inverse):
    sub = lax.broadcasted_iota(jnp.int32, (SUB, LANES), 0)
    a, b, d = corner
    upper, lower = row_of(value, pivot), row_of(value, pivot + 1)
    upper, lower = d * upper - b * lower, a * lower - b * upper
    product = first * upper + second * lower
    rest = value - product * inverse
    return jnp.where(
        sub == pivot, upper * inverse, jnp.where(sub == pivot + 1, lower * inverse, rest)
    )


def turned(value, count):
    return pltpu.roll(value, (LANES - count) % LANES, 1)


def rows_of(value):
    return [row_of(value, k) for k in range(SUB)]


def columns_of(value, start):
    return [column_of(value, start + k) for k in range(SUB)]


def panel(row, columns, start):
    columns = list(columns)
    sub = lax.broadcasted_iota(jnp.int32, (SUB, LANES), 0)
    lane = lax.broadcasted_iota(jnp.int32, (SUB, LANES), 1) - start
    inside = (lane >= 0) & (lane < SUB)
    top = jnp.where(inside, jnp.where(lane == sub, 1.0, 0.0).astype(F32), row)
    for pivot in range(0, SUB, 2):
        a = row_of(columns[pivot], pivot)
        b = row_of(columns[pivot + 1], pivot)
        d = row_of(columns[pivot + 1], pivot + 1)
        inverse = pltpu.reciprocal(a * d - b * b)
        pair = (columns[pivot], columns[pivot + 1], (a, b, d), inverse)
        columns[pivot + 2 :] = [eliminated(value, pivot, *pair) for value in columns[pivot + 2 :]]
        top = eliminated(top, pivot, *pair)
    return top


def pair_step(work, step, state, late):
    first, second, columns, last = state[0], state[1], state[2:10], list(state[10:])
    following = work[pl.ds(pl.multiple_of((step + 1) % 8 * PAIR, PAIR), PAIR), :]
    following = [following[:SUB, :], following[SUB:, :]]
    if late:
        late_update(work, step - 1, pltpu.roll(jnp.concatenate(last, axis=0), PAIR * (step - 1), 1))
        rows = rows_of(last[0]) + rows_of(last[1])
        following = [turned(value, PAIR * (step - 1)) for value in following]
        following = [turned(cleared(value, 0, rows), PAIR) for value in following]
    top = panel(first, columns, 0)
    rows = rows_of(top)
    second = cleared(second, 0, rows)
    following = [cleared(value, 0, rows) for value in following]
    bottom = panel(second, columns_of(second, SUB), SUB)
    rows = rows_of(bottom)
    following = [cleared(value, SUB, rows) for value in following]
    top = cleared(top, SUB, rows)
    columns = columns_of(following[0], PAIR)
    return (*(turned(value, PAIR) for value in following), *columns, top, bottom)


def invert_128(blocks, works, beside, slot):
    beside(slot)
    states = []
    for block, work in zip(blocks, works):
        work[...] = block
        rows = [block[:SUB, :], block[SUB:PAIR, :]]
        state = (*rows, *columns_of(rows[0], 0), *rows)
        states.append(pair_step(work, 0, state, False))

    def step(index, carry):
        beside(slot + index)
        return tuple(pair_step(work, index, state, True) for work, state in zip(works, carry))

    states = lax.fori_loop(1, 8, step, tuple(states))
    for work, state in zip(works, states):
        late_update(work, 7, pltpu.roll(jnp.concatenate(state[10:], axis=0), 7 * PAIR, 1))
    return [work[...] for work in works]


def invert_256(blocks, works, beside=lambda slot: None):
    firsts = invert_128([block[0] for block in blocks], works, beside, 0)
    seconds, sides = [], []
    for first, (_, right, below, last) in zip(firsts, blocks):
        first, right, below = split(first), split(right), split(below)
        low = split(dot3(below, first))
        seconds.append(last - dot3(low, right))
        sides.append((low, split(dot3(first, right))))
    results = []
    for first, second, (low, high) in zip(firsts, invert_128(seconds, works, beside, 8), sides):
        corner = split(second)
        below = dot3(corner, low)
        top = jnp.concatenate([first + dot3(high, split(below)), -dot3(high, corner)], axis=1)
        bottom = jnp.concatenate([-below, second], axis=1)
        results.append(jnp.concatenate([top, bottom], axis=0))
    return results


def quarters(value):
    return (
        value[:LANES, :LANES],
        value[:LANES, LANES:],
        value[LANES:, :LANES],
        value[LANES:, LANES:],
    )


def chunks(count):
    parts = -(-count // CHUNK)
    return [(k * count // parts, count // parts) for k in range(parts)]


def equilibrate(pivot):
    width = pivot.shape[0]
    row = lax.broadcasted_iota(jnp.int32, (LANES, LANES), 0)
    lane = lax.broadcasted_iota(jnp.int32, (LANES, LANES), 1)
    scales = []
    for start in range(0, width, LANES):
        block = pivot[start : start + LANES, start : start + LANES]
        scales.append(lax.rsqrt(jnp.sum(jnp.where(row == lane, block, 0.0), axis=0, keepdims=True)))
    for index, scale in enumerate(scales):
        rows = pl.ds(index * LANES, LANES)
        down = jnp.broadcast_to(scale, (LANES, LANES)).T
        for other, across in enumerate(scales):
            lanes = pl.ds(other * LANES, LANES)
            pivot[rows, lanes] = pivot[rows, lanes] * down * across
    return jnp.concatenate(scales, axis=1)


def eliminate(systems, works):
    scales = [equilibrate(system[0]) for system in systems]
    upper = invert_256([quarters(system[0][:HALF, :HALF]) for system in systems], works)
    lower = []
    for system, inverse, scale in zip(systems, upper, scales):
        pivot, parts, row = system[0], system[6], system[7]
        inverse, right = split(inverse), split(pivot[:HALF, HALF:])
        parts[0], parts[1], parts[2], parts[3] = (*inverse, *right)
        row[...] = scale
        low = split(dot3(split(pivot[HALF:, :HALF]), inverse))
        lower.append(pivot[HALF:, HALF:] - dot3(low, right))

    def forward(slot):
        for _, g, gh, gl, zh, zl, parts, row in systems:
            start = jnp.minimum(slot * (SLICE // PAIR), (g.shape[0] - SLICE) // PAIR) * PAIR
            rows = pl.ds(pl.multiple_of(start, PAIR), SLICE)
            part = split(g[rows, :HALF] * row[:, :HALF])
            gh[rows, :HALF], gl[rows, :HALF] = part
            solved = split(dot3(part, (parts[0], parts[1])))
            zh[rows, :HALF], zl[rows, :HALF] = solved
            part = split(g[rows, HALF:] * row[:, HALF:] - dot3(solved, (parts[2], parts[3])))
            gh[rows, HALF:], gl[rows, HALF:] = part

    lower = [split(x) for x in invert_256([quarters(x) for x in lower], works, forward)]
    for (_, g, gh, gl, zh, zl, *_), inverse in zip(systems, lower):
        for start, size in chunks(g.shape[0]):
            rows = pl.ds(start, size)
            solved = split(dot3((gh[rows, HALF:], gl[rows, HALF:]), inverse))
            zh[rows, HALF:], zl[rows, HALF:] = solved


def update(system, row, rows, column, columns):
    gh, gl, zh, zl = system[2:6]
    row, column = pl.ds(row, rows), pl.ds(column, columns)
    return dot3((zh[row, :], zl[row, :]), (gh[column, :], gl[column, :]), NT)


def transpose_into(target, row, source):
    width = source.shape[1]
    for i in range(0, width, LANES):
        for j in range(0, source.shape[0], LANES):
            target[row + i : row + i + LANES, j : j + LANES] = source[
                j : j + LANES, i : i + LANES
            ].T


def front_kernel(
    side, diag, lower, arrow, pivot_out, pack_out, outer_out,
    dv, lv, av, ga, gah, gal, zah, zal, pa, ra, gb, gbh, gbl, zbh, zbl, pb, rb, pivot, work, work_b, sems,
):
    width, tip = diag.shape[1], arrow.shape[1]
    two = 2 * width
    order = [
        (diag, dv, 1), (diag, dv, 3), (lower, lv, 0), (lower, lv, 1), (lower, lv, 2), (lower, lv, 3),
        (arrow, av, 1), (arrow, av, 3), (diag, dv, 2), (arrow, av, 2), (diag, dv, 0), (arrow, av, 0),
    ]
    copies = [
        pltpu.make_async_copy(source.at[k], target.at[k], sems.at[n])
        for n, (source, target, k) in enumerate(order)
    ]
    for copy in copies:
        copy.start()
    for copy in copies:
        copy.wait()
    is_left = side[0] == 0

    transpose_into(ga, 0, lv.at[0])
    ga[width:two, :] = lv[1]
    ga[two:, :] = av[1]
    gb[:width, :] = lv[3]
    transpose_into(gb, width, lv.at[2])
    gb[two:, :] = av[3]
    first = (dv.at[1], ga, gah, gal, zah, zal, pa, ra)
    third = (dv.at[3], gb, gbh, gbl, zbh, zbl, pb, rb)
    outer_out[...] = dv[3]
    eliminate([first, third], [work, work_b])

    def pick(left, right):
        return jnp.where(is_left, left, right)

    def drop(value):
        return jnp.where(is_left, value, jnp.zeros_like(value))

    for start, size in chunks(width):
        rows = pl.ds(start, size)
        shared = pl.ds(width + start, size)
        e = (width + start, size, width, width)
        pivot[rows, :] = dv[2, rows, :] - update(first, *e) - drop(update(third, *e))
        fe = (start, size, width, width)
        near = -update(first, *fe)
        far = -update(third, *fe)
        ga[rows, :] = pick(near, lv[2, rows, :])
        ga[shared, :] = pick(far, near)
        ff = (start, size, 0, width)
        near = dv[0, rows, :] - update(first, *ff)
        far = -update(third, *ff)
        pivot_out[rows, :] = pick(far, near)
        outer_out[rows, :] = pick(near, outer_out[rows, :])
    te = (two, tip, width, width)
    ga[two:, :] = av[2] - update(first, *te) - drop(update(third, *te))
    tf = (two, tip, 0, width)
    near = av[0] - update(first, *tf)
    far = -update(third, *tf)
    tip_pivot = pick(far, near)
    tip_outer = pick(near, av[3])
    tt = (two, tip, two, tip)
    tip_tip = -update(first, *tt) - drop(update(third, *tt))

    second = (pivot, ga, gah, gal, zah, zal, pa, ra)
    eliminate([second], [work])
    for start, size in chunks(width):
        rows = pl.ds(start, size)
        pivot_out[rows, :] = pivot_out[rows, :] - update(second, width + start, size, width, width)
        pack_out[rows, :] = -update(second, start, size, width, width)
        outer_out[rows, :] = outer_out[rows, :] - update(second, start, size, 0, width)
    pivot_out[width : width + tip, :] = tip_pivot - update(second, two, tip, width, width)
    pivot_out[width + tip :, :] = jnp.zeros((tip, width), F32)
    pivot_out[width + tip :, :tip] = tip_tip - update(second, *tt)
    pack_out[width : width + tip, :] = tip_outer - update(second, two, tip, 0, width)
    spill = pack_out.shape[0] - width - tip
    pack_out[width + tip :, :] = outer_out[:spill, :]


def invert_512(pivot, work):
    scale = equilibrate(pivot)
    (first,) = invert_256([quarters(pivot[:HALF, :HALF])], [work])
    right = split(pivot[:HALF, HALF:])
    below = split(pivot[HALF:, :HALF])
    upper = split(first)
    low = split(dot3(below, upper))
    high = split(dot3(upper, right))
    (second,) = invert_256([quarters(pivot[HALF:, HALF:] - dot3(low, right))], [work])
    corner = split(second)
    below = dot3(corner, low)
    pivot[:HALF, :HALF] = first + dot3(high, split(below))
    pivot[:HALF, HALF:] = -dot3(high, corner)
    pivot[HALF:, :HALF] = -below
    pivot[HALF:, HALF:] = second
    for start in range(0, pivot.shape[0], LANES):
        rows = pl.ds(start, LANES)
        down = jnp.broadcast_to(scale[:, start : start + LANES], (LANES, LANES)).T
        for lanes in range(0, pivot.shape[0], LANES):
            across = scale[:, lanes : lanes + LANES]
            lanes = pl.ds(lanes, LANES)
            pivot[rows, lanes] = pivot[rows, lanes] * down * across


def factor_kernel(mine, other, inverse, tip_out, work):
    width, tip = inverse.shape[0], tip_out.shape[0]
    inverse[...] = mine[:width, :] + other[:width, :]
    invert_512(inverse, work)
    at = pl.ds(width, tip)
    coupling = split(mine[at, :] + other[at, :])
    solved = split(dot3(coupling, split(inverse[...])))
    at = pl.ds(width + tip, tip)
    tip_out[...] = mine[at, :tip] + other[at, :tip] - dot3(solved, coupling, NT)


def merge_kernel(
    side, inverse, tip_tip, pivot_mine, pivot_other, pack_mine, pack_other, outer_mine, merged,
    gh, gl, zh, zl,
):
    width, tip = inverse.shape[0], tip_tip.shape[0]
    two = 2 * width
    half = merged.shape[0]
    spill = half - width
    is_left = side[0] == 0
    for start, size in chunks(width):
        rows = pl.ds(start, size)
        mine, other = split(pack_mine[rows, :]), split(pack_other[rows, :])
        gh[rows, :] = jnp.where(is_left, mine[0], other[0])
        gl[rows, :] = jnp.where(is_left, mine[1], other[1])
        rows = pl.ds(width + start, size)
        gh[rows, :] = jnp.where(is_left, other[0], mine[0])
        gl[rows, :] = jnp.where(is_left, other[1], mine[1])
    at = pl.ds(width, tip)
    gh[two:, :], gl[two:, :] = split(pivot_mine[at, :] + pivot_other[at, :])
    solver = split(inverse[...])
    system = (None, None, gh, gl, zh, zl)
    outer_tip = pl.ds(width, tip)

    def solve(start, size):
        rows = pl.ds(start, size)
        zh[rows, :], zl[rows, :] = split(dot3((gh[rows, :], gl[rows, :]), solver))

    @pl.when(is_left)
    def _():
        for start, size in chunks(half):
            solve(start, size)
        for start, size in chunks(width):
            rows = pl.ds(start, size)
            merged[rows, :width] = outer_mine[rows, :] - update(system, start, size, 0, width)
            merged[rows, width:two] = -update(system, start, size, width, width)
            mine = pack_mine[outer_tip, start : start + size].T
            merged[rows, two:] = mine - update(system, start, size, two, tip)
        merged[width:, :width] = -update(system, width, spill, 0, width)
        other = pack_other[width + tip :, :]
        merged[width:, width:two] = other - update(system, width, spill, width, width)
        other = pack_other[outer_tip, :LANES].T[:spill, :]
        merged[width:, two:] = other - update(system, width, spill, two, tip)

    @pl.when(jnp.logical_not(is_left))
    def _():
        for start, size in chunks(width + tip):
            solve(width + start, size)
        for start, size in chunks(width):
            skip = spill if start == 0 else 0
            rows = pl.ds(start + skip - spill, size - skip)
            merged[rows, :width] = -update(system, width + start, size, 0, width)[skip:, :]
            mine = outer_mine[pl.ds(start, size), :]
            merged[rows, width:two] = (
                mine - update(system, width + start, size, width, width)
            )[skip:, :]
            mine = pack_mine[outer_tip, start : start + size].T
            merged[rows, two:] = (mine - update(system, width + start, size, two, tip))[skip:, :]
        rows = pl.ds(half - tip, tip)
        merged[rows, :width] = pack_other[outer_tip, :] - update(system, two, tip, 0, width)
        merged[rows, width:two] = pack_mine[outer_tip, :] - update(system, two, tip, width, width)
        merged[rows, two:] = tip_tip[...]


def swapped(value, axis, mask):
    count = lax.axis_size(axis)
    return lax.ppermute(value, axis, [(k, k ^ mask) for k in range(count)])


def sum_over_pairs(value, axis):
    step = 2
    while step < lax.axis_size(axis):
        if 2 * step < lax.axis_size(axis):
            near, far, across = (swapped(value, axis, step * k) for k in (1, 2, 3))
            value = (value + near) + (far + across)
            step *= 4
        else:
            value = value + swapped(value, axis, step)
            step *= 2
    return value


def local(diag_blocks, lower_blocks, arrow_blocks, tip_block):
    count, width = diag_blocks.shape[:2]
    tip = arrow_blocks.shape[1]
    front = 2 * width + tip
    half = front // 2
    spill = half - width
    side = (lax.axis_index("tm") % 2).astype(jnp.int32).reshape(1)
    smem = pl.BlockSpec(memory_space=pltpu.SMEM)
    vmem = pl.BlockSpec(memory_space=pltpu.VMEM)
    parts = [pltpu.VMEM((front, width), BF16)] * 4
    system = [pltpu.VMEM((front, width), F32)] + parts
    system += [pltpu.VMEM((4, HALF, HALF), BF16), pltpu.VMEM((1, width), F32)]
    params = pltpu.CompilerParams(vmem_limit_bytes=56 * 2**20)
    pivot, pack, outer = pl.pallas_call(
        front_kernel,
        out_shape=[
            jax.ShapeDtypeStruct((width + 2 * tip, width), F32),
            jax.ShapeDtypeStruct((width + tip + spill, width), F32),
            jax.ShapeDtypeStruct((width, width), F32),
        ],
        in_specs=[smem] + [pl.BlockSpec(memory_space=pl.ANY)] * 3,
        out_specs=[vmem] * 3,
        scratch_shapes=[
            pltpu.VMEM((count, width, width), F32),
            pltpu.VMEM((count, width, width), F32),
            pltpu.VMEM((count, tip, width), F32),
        ]
        + system
        + system
        + [pltpu.VMEM((width, width), F32)]
        + [pltpu.VMEM((LANES, LANES), F32)] * 2
        + [pltpu.SemaphoreType.DMA((3 * count,))],
        compiler_params=params,
        name="front",
    )(side, diag_blocks, lower_blocks, arrow_blocks)
    pivot_other = swapped(pivot, "tm", 1)
    pack_other = swapped(pack, "tm", 1)
    inverse, tip_tip = pl.pallas_call(
        factor_kernel,
        out_shape=[
            jax.ShapeDtypeStruct((width, width), F32),
            jax.ShapeDtypeStruct((tip, tip), F32),
        ],
        in_specs=[vmem] * 2,
        out_specs=[vmem] * 2,
        scratch_shapes=[pltpu.VMEM((LANES, LANES), F32)],
        compiler_params=pltpu.CompilerParams(vmem_limit_bytes=24 * 2**20),
        cost_estimate=pl.CostEstimate(flops=10**10, bytes_accessed=10**7, transcendentals=0),
        name="factor",
    )(pivot, pivot_other)
    merged = pl.pallas_call(
        merge_kernel,
        out_shape=jax.ShapeDtypeStruct((half, front), F32),
        in_specs=[smem] + [vmem] * 7,
        out_specs=vmem,
        scratch_shapes=parts,
        compiler_params=pltpu.CompilerParams(vmem_limit_bytes=40 * 2**20),
        cost_estimate=pl.CostEstimate(flops=5 * 10**9, bytes_accessed=10**7, transcendentals=0),
        name="merge",
    )(side, inverse, tip_tip, pivot, pivot_other, pack, pack_other, outer)
    return merged, tip_block + sum_over_pairs(tip_tip, "tm")


def solution(mesh):
    placed = (P("tm", None, None), P("tm", None, None), P("tm", None, None), P())
    return jax.shard_map(
        local, mesh=mesh, in_specs=placed, out_specs=(P("tm", None), P()), check_vma=False
    )
```

```python
import functools

import jax
import jax.numpy as jnp
from jax import lax
from jax.experimental import pallas as pl
from jax.experimental.pallas import tpu as pltpu
from jax.sharding import PartitionSpec as P

F32 = jnp.float32
BF16 = jnp.bfloat16
SUB = 8
PAIR = 16
LANES = 128
HALF = 256
CHUNK = 576
SLICE = 80
NN = (((1,), (0,)), ((), ()))
NT = (((1,), (1,)), ((), ()))


def split(value):
    high = value.astype(BF16)
    return high, (value - high.astype(F32)).astype(BF16)


def dot3(left, right, dims=NN):
    one = functools.partial(lax.dot_general, dimension_numbers=dims, preferred_element_type=F32)
    count = left[0].shape[0]
    both = one(jnp.concatenate(left, axis=0), right[0])
    return both[:count] + (both[count:] + one(left[0], right[1]))


def row_of(value, index):
    return jnp.broadcast_to(value[index : index + 1, :], (SUB, LANES))


def column_of(value, index):
    return jnp.broadcast_to(value[:, index : index + 1], (SUB, LANES))


def total(terms):
    while len(terms) > 1:
        terms = [terms[k] + terms[k + 1] for k in range(0, len(terms), 2)]
    return terms[0]


def cleared(value, start, top):
    lane = lax.broadcasted_iota(jnp.int32, (SUB, LANES), 1)
    panel = (lane >= start) & (lane < start + len(top))
    terms = [column_of(value, start + k) * row for k, row in enumerate(top)]
    return jnp.where(panel, 0.0, value) - total(terms)


def late_update(work, step, top):
    value = work[...]
    right = tuple(
        jnp.concatenate(
            [jnp.where(step == k, part, jnp.zeros_like(part)) for k in range(8)], axis=0
        )
        for part in split(top)
    )
    lane = lax.broadcasted_iota(jnp.int32, (LANES, LANES), 1)
    panel = (lane >= PAIR * step) & (lane < PAIR * (step + 1))
    work[...] = jnp.where(panel, 0.0, value) - dot3(split(value), right)
    work[pl.ds(pl.multiple_of(PAIR * step, PAIR), PAIR), :] = top


def eliminated(value, pivot, first, second, corner, inverse):
    sub = lax.broadcasted_iota(jnp.int32, (SUB, LANES), 0)
    a, b, d = corner
    upper, lower = row_of(value, pivot), row_of(value, pivot + 1)
    upper, lower = d * upper - b * lower, a * lower - b * upper
    product = first * upper + second * lower
    rest = value - product * inverse
    return jnp.where(
        sub == pivot, upper * inverse, jnp.where(sub == pivot + 1, lower * inverse, rest)
    )


def turned(value, count):
    return pltpu.roll(value, (LANES - count) % LANES, 1)


def rows_of(value):
    return [row_of(value, k) for k in range(SUB)]


def columns_of(value, start):
    return [column_of(value, start + k) for k in range(SUB)]


def panel(row, columns, start):
    columns = list(columns)
    sub = lax.broadcasted_iota(jnp.int32, (SUB, LANES), 0)
    lane = lax.broadcasted_iota(jnp.int32, (SUB, LANES), 1) - start
    inside = (lane >= 0) & (lane < SUB)
    top = jnp.where(inside, jnp.where(lane == sub, 1.0, 0.0).astype(F32), row)
    for pivot in range(0, SUB, 2):
        a = row_of(columns[pivot], pivot)
        b = row_of(columns[pivot + 1], pivot)
        d = row_of(columns[pivot + 1], pivot + 1)
        inverse = pltpu.reciprocal(a * d - b * b)
        pair = (columns[pivot], columns[pivot + 1], (a, b, d), inverse)
        columns[pivot + 2 :] = [eliminated(value, pivot, *pair) for value in columns[pivot + 2 :]]
        top = eliminated(top, pivot, *pair)
    return top


def pair_step(work, step, state, late):
    first, second, columns, last = state[0], state[1], state[2:10], list(state[10:])
    following = work[pl.ds(pl.multiple_of((step + 1) % 8 * PAIR, PAIR), PAIR), :]
    following = [following[:SUB, :], following[SUB:, :]]
    if late:
        late_update(work, step - 1, pltpu.roll(jnp.concatenate(last, axis=0), PAIR * (step - 1), 1))
        rows = rows_of(last[0]) + rows_of(last[1])
        following = [turned(value, PAIR * (step - 1)) for value in following]
        following = [turned(cleared(value, 0, rows), PAIR) for value in following]
    top = panel(first, columns, 0)
    rows = rows_of(top)
    second = cleared(second, 0, rows)
    following = [cleared(value, 0, rows) for value in following]
    bottom = panel(second, columns_of(second, SUB), SUB)
    rows = rows_of(bottom)
    following = [cleared(value, SUB, rows) for value in following]
    top = cleared(top, SUB, rows)
    columns = columns_of(following[0], PAIR)
    return (*(turned(value, PAIR) for value in following), *columns, top, bottom)


def invert_128(blocks, works, beside, slot, unroll):
    beside(slot)
    states = []
    for block, work in zip(blocks, works):
        work[...] = block
        rows = [block[:SUB, :], block[SUB:PAIR, :]]
        state = (*rows, *columns_of(rows[0], 0), *rows)
        states.append(pair_step(work, 0, state, False))

    def step(index, carry):
        beside(slot + index)
        return tuple(pair_step(work, index, state, True) for work, state in zip(works, carry))

    states = lax.fori_loop(1, 8, step, tuple(states), unroll=unroll)
    for work, state in zip(works, states):
        late_update(work, 7, pltpu.roll(jnp.concatenate(state[10:], axis=0), 7 * PAIR, 1))
    return [work[...] for work in works]


def invert_256(blocks, works, beside=lambda slot: None, unroll=1):
    firsts = invert_128([block[0] for block in blocks], works, beside, 0, unroll)
    seconds, sides = [], []
    for first, (_, right, below, last) in zip(firsts, blocks):
        first, right, below = split(first), split(right), split(below)
        low = split(dot3(below, first))
        seconds.append(last - dot3(low, right))
        sides.append((low, split(dot3(first, right))))
    results = []
    for first, second, (low, high) in zip(firsts, invert_128(seconds, works, beside, 8, unroll), sides):
        corner = split(second)
        below = dot3(corner, low)
        top = jnp.concatenate([first + dot3(high, split(below)), -dot3(high, corner)], axis=1)
        bottom = jnp.concatenate([-below, second], axis=1)
        results.append(jnp.concatenate([top, bottom], axis=0))
    return results


def quarters(value):
    return (
        value[:LANES, :LANES],
        value[:LANES, LANES:],
        value[LANES:, :LANES],
        value[LANES:, LANES:],
    )


def chunks(count):
    parts = -(-count // CHUNK)
    return [(k * count // parts, count // parts) for k in range(parts)]


def equilibrate(pivot):
    width = pivot.shape[0]
    row = lax.broadcasted_iota(jnp.int32, (LANES, LANES), 0)
    lane = lax.broadcasted_iota(jnp.int32, (LANES, LANES), 1)
    scales = []
    for start in range(0, width, LANES):
        block = pivot[start : start + LANES, start : start + LANES]
        scales.append(lax.rsqrt(jnp.sum(jnp.where(row == lane, block, 0.0), axis=0, keepdims=True)))
    for index, scale in enumerate(scales):
        rows = pl.ds(index * LANES, LANES)
        down = jnp.broadcast_to(scale, (LANES, LANES)).T
        for other, across in enumerate(scales):
            lanes = pl.ds(other * LANES, LANES)
            pivot[rows, lanes] = pivot[rows, lanes] * down * across
    return jnp.concatenate(scales, axis=1)


def eliminate(systems, works, beside, prepare):
    scales = [equilibrate(system[0]) for system in systems]
    upper = invert_256([quarters(system[0][:HALF, :HALF]) for system in systems], works, beside)
    prepare()
    lower = []
    for system, inverse, scale in zip(systems, upper, scales):
        pivot, parts, row = system[0], system[6], system[7]
        inverse, right = split(inverse), split(pivot[:HALF, HALF:])
        parts[0], parts[1], parts[2], parts[3] = (*inverse, *right)
        row[...] = scale
        low = split(dot3(split(pivot[HALF:, :HALF]), inverse))
        lower.append(pivot[HALF:, HALF:] - dot3(low, right))

    def forward(slot):
        for _, g, gh, gl, zh, zl, parts, row in systems:
            start = jnp.minimum(slot * (SLICE // PAIR), (g.shape[0] - SLICE) // PAIR) * PAIR
            rows = pl.ds(pl.multiple_of(start, PAIR), SLICE)
            part = split(g[rows, :HALF] * row[:, :HALF])
            gh[rows, :HALF], gl[rows, :HALF] = part
            solved = split(dot3(part, (parts[0], parts[1])))
            zh[rows, :HALF], zl[rows, :HALF] = solved
            part = split(g[rows, HALF:] * row[:, HALF:] - dot3(solved, (parts[2], parts[3])))
            gh[rows, HALF:], gl[rows, HALF:] = part

    lower = [split(x) for x in invert_256([quarters(x) for x in lower], works, forward)]
    for (_, g, gh, gl, zh, zl, *_), inverse in zip(systems, lower):
        for start, size in chunks(g.shape[0]):
            rows = pl.ds(start, size)
            solved = split(dot3((gh[rows, HALF:], gl[rows, HALF:]), inverse))
            zh[rows, HALF:], zl[rows, HALF:] = solved


def update(system, row, rows, column, columns):
    gh, gl, zh, zl = system[2:6]
    row, column = pl.ds(row, rows), pl.ds(column, columns)
    return dot3((zh[row, :], zl[row, :]), (gh[column, :], gl[column, :]), NT)


def transpose_into(target, row, source):
    width = source.shape[1]
    for i in range(0, width, LANES):
        for j in range(0, source.shape[0], LANES):
            target[row + i : row + i + LANES, j : j + LANES] = source[
                j : j + LANES, i : i + LANES
            ].T


def front_kernel(
    side, diag, lower, arrow, pivot_out, pack_out, outer_out,
    dv, lv, av, ga, gb, gh, gl, zh, zl, pa, pb, ra, rb, pivot, terms, work, work_b, sems,
):
    width, tip = diag.shape[1], arrow.shape[1]
    two = 2 * width
    order = [
        (diag, dv, 1), (diag, dv, 3), (lower, lv, 0), (lower, lv, 1), (lower, lv, 2), (lower, lv, 3),
        (arrow, av, 1), (arrow, av, 3), (diag, dv, 2), (arrow, av, 2), (diag, dv, 0), (arrow, av, 0),
    ]
    copies = [
        pltpu.make_async_copy(source.at[k], target.at[k], sems.at[n])
        for n, (source, target, k) in enumerate(order)
    ]
    for copy in copies:
        copy.start()
    is_left = side[0] == 0
    first = (dv.at[1], ga, gh.at[0], gl.at[0], zh.at[0], zl.at[0], pa, ra)
    third = (dv.at[3], gb, gh.at[1], gl.at[1], zh.at[1], zl.at[1], pb, rb)
    for copy in copies[:2]:
        copy.wait()
    outer_out[...] = dv[3]

    def nothing(slot):
        pass

    def couplings():
        for copy in copies[2:]:
            copy.wait()
        transpose_into(ga, 0, lv.at[0])
        ga[width:two, :] = lv[1]
        ga[two:, :] = av[1]
        gb[:width, :] = lv[3]
        transpose_into(gb, width, lv.at[2])
        gb[two:, :] = av[3]

    eliminate([first, third], [work, work_b], nothing, couplings)

    def pick(left, right):
        return jnp.where(is_left, left, right)

    def drop(value):
        return jnp.where(is_left, value, jnp.zeros_like(value))

    e = (width, width, width, width)
    pivot[...] = dv[2] - update(first, *e) - drop(update(third, *e))

    def rest(slot):
        chain, piece, half = slot // 8, slot // 2 % 4, slot % 2
        lanes = pl.ds(pl.multiple_of(half * HALF, HALF), HALF)
        across = pl.ds(pl.multiple_of(piece * HALF, HALF), HALF)
        column = pl.ds(pl.multiple_of((width + piece * HALF) % two, HALF), HALF)
        right = (gh[chain, column, lanes], gl[chain, column, lanes])
        for row, size, target in ((0, width, 0), (two, tip, width)):
            rows, down = pl.ds(row, size), pl.ds(target, size)
            term = dot3((zh[chain, rows, lanes], zl[chain, rows, lanes]), right, NT)
            held = terms[chain, down, across]
            terms[chain, down, across] = jnp.where(half == 0, 0.0, held) + term

    tt = (two, tip, two, tip)

    def fronts():
        near, far = -terms[0, :width, :width], -terms[1, :width, :width]
        ga[:width, :] = pick(near, lv[2])
        ga[width:two, :] = pick(far, near)
        ga[two:, :] = av[2] - terms[0, width:, :width] - drop(terms[1, width:, :width])
        near, far = dv[0] - terms[0, :width, width:], -terms[1, :width, width:]
        pivot_out[:width, :] = pick(far, near)
        outer_out[...] = pick(near, outer_out[...])
        near, far = av[0] - terms[0, width:, width:], -terms[1, width:, width:]
        pivot_out[width : width + tip, :] = pick(far, near)
        pack_out[width : width + tip, :] = pick(near, av[3])
        pivot_out[width + tip :, :] = jnp.zeros((tip, width), F32)
        pivot_out[width + tip :, :tip] = -update(first, *tt) - drop(update(third, *tt))

    second = (pivot, ga, gh.at[0], gl.at[0], zh.at[0], zl.at[0], pa, ra)
    eliminate([second], [work], rest, fronts)
    pivot_out[:width, :] = pivot_out[:width, :] - update(second, width, width, width, width)
    pack_out[:width, :] = -update(second, 0, width, width, width)
    outer_out[...] = outer_out[...] - update(second, 0, width, 0, width)
    at = pl.ds(width, tip)
    pivot_out[at, :] = pivot_out[at, :] - update(second, two, tip, width, width)
    pack_out[at, :] = pack_out[at, :] - update(second, two, tip, 0, width)
    at = pl.ds(width + tip, tip)
    pivot_out[at, :tip] = pivot_out[at, :tip] - update(second, *tt)
    spill = pack_out.shape[0] - width - tip
    pack_out[width + tip :, :] = outer_out[:spill, :]


def invert_512(pivot, work):
    scale = equilibrate(pivot)
    (first,) = invert_256([quarters(pivot[:HALF, :HALF])], [work], unroll=7)
    right = split(pivot[:HALF, HALF:])
    below = split(pivot[HALF:, :HALF])
    upper = split(first)
    low = split(dot3(below, upper))
    high = split(dot3(upper, right))
    last = pivot[HALF:, HALF:] - dot3(low, right)
    (second,) = invert_256([quarters(last)], [work], unroll=7)
    corner = split(second)
    below = dot3(corner, low)
    pivot[:HALF, :HALF] = first + dot3(high, split(below))
    pivot[:HALF, HALF:] = -dot3(high, corner)
    pivot[HALF:, :HALF] = -below
    pivot[HALF:, HALF:] = second
    for start in range(0, pivot.shape[0], LANES):
        rows = pl.ds(start, LANES)
        down = jnp.broadcast_to(scale[:, start : start + LANES], (LANES, LANES)).T
        for lanes in range(0, pivot.shape[0], LANES):
            across = scale[:, lanes : lanes + LANES]
            lanes = pl.ds(lanes, LANES)
            pivot[rows, lanes] = pivot[rows, lanes] * down * across


def factor_kernel(mine, other, inverse, tip_out, work):
    width, tip = inverse.shape[0], tip_out.shape[0]
    inverse[...] = mine[:width, :] + other[:width, :]
    invert_512(inverse, work)
    at = pl.ds(width, tip)
    coupling = split(mine[at, :] + other[at, :])
    solved = split(dot3(coupling, split(inverse[...])))
    at = pl.ds(width + tip, tip)
    tip_out[...] = mine[at, :tip] + other[at, :tip] - dot3(solved, coupling, NT)


def merge_kernel(
    side, inverse, tip_tip, pivot_mine, pivot_other, pack_mine, pack_other, outer_mine, merged,
    gh, gl, zh, zl,
):
    width, tip = inverse.shape[0], tip_tip.shape[0]
    two = 2 * width
    half = merged.shape[0]
    spill = half - width
    is_left = side[0] == 0
    for start, size in chunks(width):
        rows = pl.ds(start, size)
        mine, other = split(pack_mine[rows, :]), split(pack_other[rows, :])
        gh[rows, :] = jnp.where(is_left, mine[0], other[0])
        gl[rows, :] = jnp.where(is_left, mine[1], other[1])
        rows = pl.ds(width + start, size)
        gh[rows, :] = jnp.where(is_left, other[0], mine[0])
        gl[rows, :] = jnp.where(is_left, other[1], mine[1])
    at = pl.ds(width, tip)
    gh[two:, :], gl[two:, :] = split(pivot_mine[at, :] + pivot_other[at, :])
    solver = split(inverse[...])
    system = (None, None, gh, gl, zh, zl)
    outer_tip = pl.ds(width, tip)

    def solve(start, size):
        rows = pl.ds(start, size)
        zh[rows, :], zl[rows, :] = split(dot3((gh[rows, :], gl[rows, :]), solver))

    @pl.when(is_left)
    def _():
        for start, size in chunks(half):
            solve(start, size)
        for start, size in chunks(width):
            rows = pl.ds(start, size)
            merged[rows, :width] = outer_mine[rows, :] - update(system, start, size, 0, width)
            merged[rows, width:two] = -update(system, start, size, width, width)
            mine = pack_mine[outer_tip, start : start + size].T
            merged[rows, two:] = mine - update(system, start, size, two, tip)
        merged[width:, :width] = -update(system, width, spill, 0, width)
        other = pack_other[width + tip :, :]
        merged[width:, width:two] = other - update(system, width, spill, width, width)
        other = pack_other[outer_tip, :LANES].T[:spill, :]
        merged[width:, two:] = other - update(system, width, spill, two, tip)

    @pl.when(jnp.logical_not(is_left))
    def _():
        for start, size in chunks(width + tip):
            solve(width + start, size)
        for start, size in chunks(width):
            skip = spill if start == 0 else 0
            rows = pl.ds(start + skip - spill, size - skip)
            merged[rows, :width] = -update(system, width + start, size, 0, width)[skip:, :]
            mine = outer_mine[pl.ds(start, size), :]
            merged[rows, width:two] = (
                mine - update(system, width + start, size, width, width)
            )[skip:, :]
            mine = pack_mine[outer_tip, start : start + size].T
            merged[rows, two:] = (mine - update(system, width + start, size, two, tip))[skip:, :]
        rows = pl.ds(half - tip, tip)
        merged[rows, :width] = pack_other[outer_tip, :] - update(system, two, tip, 0, width)
        merged[rows, width:two] = pack_mine[outer_tip, :] - update(system, two, tip, width, width)
        merged[rows, two:] = tip_tip[...]


def swapped(value, axis, mask):
    count = lax.axis_size(axis)
    return lax.ppermute(value, axis, [(k, k ^ mask) for k in range(count)])


def sum_over_pairs(value, axis):
    step = 2
    while step < lax.axis_size(axis):
        if 2 * step < lax.axis_size(axis):
            near, far, across = (swapped(value, axis, step * k) for k in (1, 2, 3))
            value = (value + near) + (far + across)
            step *= 4
        else:
            value = value + swapped(value, axis, step)
            step *= 2
    return value


def local(diag_blocks, lower_blocks, arrow_blocks, tip_block):
    count, width = diag_blocks.shape[:2]
    tip = arrow_blocks.shape[1]
    front = 2 * width + tip
    half = front // 2
    spill = half - width
    side = (lax.axis_index("tm") % 2).astype(jnp.int32).reshape(1)
    smem = pl.BlockSpec(memory_space=pltpu.SMEM)
    vmem = pl.BlockSpec(memory_space=pltpu.VMEM)
    parts = [pltpu.VMEM((front, width), BF16)] * 4
    params = pltpu.CompilerParams(vmem_limit_bytes=56 * 2**20)
    pivot, pack, outer = pl.pallas_call(
        front_kernel,
        out_shape=[
            jax.ShapeDtypeStruct((width + 2 * tip, width), F32),
            jax.ShapeDtypeStruct((width + tip + spill, width), F32),
            jax.ShapeDtypeStruct((width, width), F32),
        ],
        in_specs=[smem] + [pl.BlockSpec(memory_space=pl.ANY)] * 3,
        out_specs=[vmem] * 3,
        scratch_shapes=[
            pltpu.VMEM((count, width, width), F32),
            pltpu.VMEM((count, width, width), F32),
            pltpu.VMEM((count, tip, width), F32),
        ]
        + [pltpu.VMEM((front, width), F32)] * 2
        + [pltpu.VMEM((2, front, width), BF16)] * 4
        + [pltpu.VMEM((4, HALF, HALF), BF16)] * 2
        + [pltpu.VMEM((1, width), F32)] * 2
        + [pltpu.VMEM((width, width), F32), pltpu.VMEM((2, width + tip, 2 * width), F32)]
        + [pltpu.VMEM((LANES, LANES), F32)] * 2
        + [pltpu.SemaphoreType.DMA((3 * count,))],
        compiler_params=params,
        name="front",
    )(side, diag_blocks, lower_blocks, arrow_blocks)
    pivot_other = swapped(pivot, "tm", 1)
    pack_other = swapped(pack, "tm", 1)
    inverse, tip_tip = pl.pallas_call(
        factor_kernel,
        out_shape=[
            jax.ShapeDtypeStruct((width, width), F32),
            jax.ShapeDtypeStruct((tip, tip), F32),
        ],
        in_specs=[vmem] * 2,
        out_specs=[vmem] * 2,
        scratch_shapes=[pltpu.VMEM((LANES, LANES), F32)],
        compiler_params=pltpu.CompilerParams(vmem_limit_bytes=24 * 2**20),
        cost_estimate=pl.CostEstimate(flops=10**10, bytes_accessed=10**7, transcendentals=0),
        name="factor",
    )(pivot, pivot_other)
    merged = pl.pallas_call(
        merge_kernel,
        out_shape=jax.ShapeDtypeStruct((half, front), F32),
        in_specs=[smem] + [vmem] * 7,
        out_specs=vmem,
        scratch_shapes=parts,
        compiler_params=pltpu.CompilerParams(vmem_limit_bytes=40 * 2**20),
        cost_estimate=pl.CostEstimate(flops=5 * 10**9, bytes_accessed=10**7, transcendentals=0),
        name="merge",
    )(side, inverse, tip_tip, pivot, pivot_other, pack, pack_other, outer)
    return merged, tip_block + sum_over_pairs(tip_tip, "tm")


def solution(mesh):
    placed = (P("tm", None, None), P("tm", None, None), P("tm", None, None), P())
    return jax.shard_map(
        local, mesh=mesh, in_specs=placed, out_specs=(P("tm", None), P()), check_vma=False
    )
```

```python
import functools

import jax
import jax.numpy as jnp
from jax import lax
from jax.experimental import pallas as pl
from jax.experimental.pallas import tpu as pltpu
from jax.sharding import PartitionSpec as P

F32 = jnp.float32
BF16 = jnp.bfloat16
SUB = 8
PAIR = 16
LANES = 128
HALF = 256
CHUNK = 576
SLICE = 80
NN = (((1,), (0,)), ((), ()))
NT = (((1,), (1,)), ((), ()))


def split(value):
    high = value.astype(BF16)
    return high, (value - high.astype(F32)).astype(BF16)


def dot3(left, right, dims=NN):
    one = functools.partial(lax.dot_general, dimension_numbers=dims, preferred_element_type=F32)
    count = left[0].shape[0]
    both = one(jnp.concatenate(left, axis=0), right[0])
    return both[:count] + (both[count:] + one(left[0], right[1]))


def row_of(value, index):
    return jnp.broadcast_to(value[index : index + 1, :], (SUB, LANES))


def column_of(value, index):
    return jnp.broadcast_to(value[:, index : index + 1], (SUB, LANES))


def total(terms):
    while len(terms) > 1:
        terms = [terms[k] + terms[k + 1] for k in range(0, len(terms), 2)]
    return terms[0]


def cleared(value, start, top):
    lane = lax.broadcasted_iota(jnp.int32, (SUB, LANES), 1)
    panel = (lane >= start) & (lane < start + len(top))
    terms = [column_of(value, start + k) * row for k, row in enumerate(top)]
    return jnp.where(panel, 0.0, value) - total(terms)


def late_update(work, step, top):
    value = work[...]
    right = tuple(
        jnp.concatenate(
            [jnp.where(step == k, part, jnp.zeros_like(part)) for k in range(8)], axis=0
        )
        for part in split(top)
    )
    lane = lax.broadcasted_iota(jnp.int32, (LANES, LANES), 1)
    panel = (lane >= PAIR * step) & (lane < PAIR * (step + 1))
    work[...] = jnp.where(panel, 0.0, value) - dot3(split(value), right)
    work[pl.ds(pl.multiple_of(PAIR * step, PAIR), PAIR), :] = top


def eliminated(value, pivot, first, second, corner, inverse):
    sub = lax.broadcasted_iota(jnp.int32, (SUB, LANES), 0)
    a, b, d = corner
    upper, lower = row_of(value, pivot), row_of(value, pivot + 1)
    upper, lower = d * upper - b * lower, a * lower - b * upper
    product = first * upper + second * lower
    rest = value - product * inverse
    return jnp.where(
        sub == pivot, upper * inverse, jnp.where(sub == pivot + 1, lower * inverse, rest)
    )


def turned(value, count):
    return pltpu.roll(value, (LANES - count) % LANES, 1)


def rows_of(value):
    return [row_of(value, k) for k in range(SUB)]


def columns_of(value, start):
    return [column_of(value, start + k) for k in range(SUB)]


def panel(row, columns, start):
    columns = list(columns)
    sub = lax.broadcasted_iota(jnp.int32, (SUB, LANES), 0)
    lane = lax.broadcasted_iota(jnp.int32, (SUB, LANES), 1) - start
    inside = (lane >= 0) & (lane < SUB)
    top = jnp.where(inside, jnp.where(lane == sub, 1.0, 0.0).astype(F32), row)
    for pivot in range(0, SUB, 2):
        a = row_of(columns[pivot], pivot)
        b = row_of(columns[pivot + 1], pivot)
        d = row_of(columns[pivot + 1], pivot + 1)
        inverse = pltpu.reciprocal(a * d - b * b)
        pair = (columns[pivot], columns[pivot + 1], (a, b, d), inverse)
        columns[pivot + 2 :] = [eliminated(value, pivot, *pair) for value in columns[pivot + 2 :]]
        top = eliminated(top, pivot, *pair)
    return top


def pair_step(work, step, state, late):
    first, second, columns, last = state[0], state[1], state[2:10], list(state[10:])
    following = work[pl.ds(pl.multiple_of((step + 1) % 8 * PAIR, PAIR), PAIR), :]
    following = [following[:SUB, :], following[SUB:, :]]
    if late:
        late_update(work, step - 1, pltpu.roll(jnp.concatenate(last, axis=0), PAIR * (step - 1), 1))
        rows = rows_of(last[0]) + rows_of(last[1])
        following = [turned(value, PAIR * (step - 1)) for value in following]
        following = [turned(cleared(value, 0, rows), PAIR) for value in following]
    top = panel(first, columns, 0)
    rows = rows_of(top)
    second = cleared(second, 0, rows)
    following = [cleared(value, 0, rows) for value in following]
    bottom = panel(second, columns_of(second, SUB), SUB)
    rows = rows_of(bottom)
    following = [cleared(value, SUB, rows) for value in following]
    top = cleared(top, SUB, rows)
    columns = columns_of(following[0], PAIR)
    return (*(turned(value, PAIR) for value in following), *columns, top, bottom)


def invert_128(blocks, works, beside, slot, unroll):
    beside(slot)
    states = []
    for block, work in zip(blocks, works):
        work[...] = block
        rows = [block[:SUB, :], block[SUB:PAIR, :]]
        state = (*rows, *columns_of(rows[0], 0), *rows)
        states.append(pair_step(work, 0, state, False))

    def step(index, carry):
        beside(slot + index)
        return tuple(pair_step(work, index, state, True) for work, state in zip(works, carry))

    states = lax.fori_loop(1, 8, step, tuple(states), unroll=unroll)
    for work, state in zip(works, states):
        late_update(work, 7, pltpu.roll(jnp.concatenate(state[10:], axis=0), 7 * PAIR, 1))
    return [work[...] for work in works]


def invert_256(blocks, works, beside=lambda slot: None, unroll=1):
    firsts = invert_128([block[0] for block in blocks], works, beside, 0, unroll)
    seconds, sides = [], []
    for first, (_, right, below, last) in zip(firsts, blocks):
        first, right, below = split(first), split(right), split(below)
        low = split(dot3(below, first))
        seconds.append(last - dot3(low, right))
        sides.append((low, split(dot3(first, right))))
    results = []
    for first, second, (low, high) in zip(firsts, invert_128(seconds, works, beside, 8, unroll), sides):
        corner = split(second)
        below = dot3(corner, low)
        top = jnp.concatenate([first + dot3(high, split(below)), -dot3(high, corner)], axis=1)
        bottom = jnp.concatenate([-below, second], axis=1)
        results.append(jnp.concatenate([top, bottom], axis=0))
    return results


def quarters(value):
    return (
        value[:LANES, :LANES],
        value[:LANES, LANES:],
        value[LANES:, :LANES],
        value[LANES:, LANES:],
    )


def chunks(count):
    parts = -(-count // CHUNK)
    return [(k * count // parts, count // parts) for k in range(parts)]


def equilibrate(pivot):
    width = pivot.shape[0]
    row = lax.broadcasted_iota(jnp.int32, (LANES, LANES), 0)
    lane = lax.broadcasted_iota(jnp.int32, (LANES, LANES), 1)
    scales = []
    for start in range(0, width, LANES):
        block = pivot[start : start + LANES, start : start + LANES]
        scales.append(lax.rsqrt(jnp.sum(jnp.where(row == lane, block, 0.0), axis=0, keepdims=True)))
    for index, scale in enumerate(scales):
        rows = pl.ds(index * LANES, LANES)
        down = jnp.broadcast_to(scale, (LANES, LANES)).T
        for other, across in enumerate(scales):
            lanes = pl.ds(other * LANES, LANES)
            pivot[rows, lanes] = pivot[rows, lanes] * down * across
    return jnp.concatenate(scales, axis=1)


def eliminate(systems, works, beside, prepare):
    scales = [equilibrate(system[0]) for system in systems]
    upper = invert_256([quarters(system[0][:HALF, :HALF]) for system in systems], works, beside)
    prepare()
    lower = []
    for system, inverse, scale in zip(systems, upper, scales):
        pivot, parts, row = system[0], system[6], system[7]
        inverse, right = split(inverse), split(pivot[:HALF, HALF:])
        parts[0], parts[1], parts[2], parts[3] = (*inverse, *right)
        row[...] = scale
        low = split(dot3(split(pivot[HALF:, :HALF]), inverse))
        lower.append(pivot[HALF:, HALF:] - dot3(low, right))

    def forward(slot):
        for _, g, gh, gl, zh, zl, parts, row in systems:
            start = jnp.minimum(slot * (SLICE // PAIR), (g.shape[0] - SLICE) // PAIR) * PAIR
            rows = pl.ds(pl.multiple_of(start, PAIR), SLICE)
            part = split(g[rows, :HALF] * row[:, :HALF])
            gh[rows, :HALF], gl[rows, :HALF] = part
            solved = split(dot3(part, (parts[0], parts[1])))
            zh[rows, :HALF], zl[rows, :HALF] = solved
            part = split(g[rows, HALF:] * row[:, HALF:] - dot3(solved, (parts[2], parts[3])))
            gh[rows, HALF:], gl[rows, HALF:] = part

    lower = [split(x) for x in invert_256([quarters(x) for x in lower], works, forward)]
    for (_, g, gh, gl, zh, zl, *_), inverse in zip(systems, lower):
        for start, size in chunks(g.shape[0]):
            rows = pl.ds(start, size)
            solved = split(dot3((gh[rows, HALF:], gl[rows, HALF:]), inverse))
            zh[rows, HALF:], zl[rows, HALF:] = solved


def update(system, row, rows, column, columns):
    gh, gl, zh, zl = system[2:6]
    row, column = pl.ds(row, rows), pl.ds(column, columns)
    return dot3((zh[row, :], zl[row, :]), (gh[column, :], gl[column, :]), NT)


def transpose_into(target, row, source):
    width = source.shape[1]
    for i in range(0, width, LANES):
        for j in range(0, source.shape[0], LANES):
            target[row + i : row + i + LANES, j : j + LANES] = source[
                j : j + LANES, i : i + LANES
            ].T


def front_kernel(
    side, diag, lower, arrow, pivot_out, pack_out, outer_out,
    dv, lv, av, ga, gb, gh, gl, zh, zl, pa, pb, ra, rb, pivot, terms, work, work_b, sems,
):
    width, tip = diag.shape[1], arrow.shape[1]
    two = 2 * width
    order = [
        (diag, dv, 1), (diag, dv, 3), (lower, lv, 0), (lower, lv, 1), (lower, lv, 2), (lower, lv, 3),
        (arrow, av, 1), (arrow, av, 3), (diag, dv, 2), (arrow, av, 2), (diag, dv, 0), (arrow, av, 0),
    ]
    copies = [
        pltpu.make_async_copy(source.at[k], target.at[k], sems.at[n])
        for n, (source, target, k) in enumerate(order)
    ]
    for copy in copies:
        copy.start()
    is_left = side[0] == 0
    first = (dv.at[1], ga, gh.at[0], gl.at[0], zh.at[0], zl.at[0], pa, ra)
    third = (dv.at[3], gb, gh.at[1], gl.at[1], zh.at[1], zl.at[1], pb, rb)
    for copy in copies[:2]:
        copy.wait()
    outer_out[...] = dv[3]

    def nothing(slot):
        pass

    def couplings():
        for copy in copies[2:]:
            copy.wait()
        transpose_into(ga, 0, lv.at[0])
        ga[width:two, :] = lv[1]
        ga[two:, :] = av[1]
        gb[:width, :] = lv[3]
        transpose_into(gb, width, lv.at[2])
        gb[two:, :] = av[3]

    eliminate([first, third], [work, work_b], nothing, couplings)

    def pick(left, right):
        return jnp.where(is_left, left, right)

    def drop(value):
        return jnp.where(is_left, value, jnp.zeros_like(value))

    e = (width, width, width, width)
    pivot[...] = dv[2] - update(first, *e) - drop(update(third, *e))

    def rest(slot):
        chain, piece, half = slot // 8, slot // 2 % 4, slot % 2
        lanes = pl.ds(pl.multiple_of(half * HALF, HALF), HALF)
        across = pl.ds(pl.multiple_of(piece * HALF, HALF), HALF)
        column = pl.ds(pl.multiple_of((width + piece * HALF) % two, HALF), HALF)
        right = (gh[chain, column, lanes], gl[chain, column, lanes])
        for row, size, target in ((0, width, 0), (two, tip, width)):
            rows, down = pl.ds(row, size), pl.ds(target, size)
            term = dot3((zh[chain, rows, lanes], zl[chain, rows, lanes]), right, NT)
            held = terms[chain, down, across]
            terms[chain, down, across] = jnp.where(half == 0, 0.0, held) + term

    tt = (two, tip, two, tip)

    def fronts():
        near, far = -terms[0, :width, :width], -terms[1, :width, :width]
        ga[:width, :] = pick(near, lv[2])
        ga[width:two, :] = pick(far, near)
        ga[two:, :] = av[2] - terms[0, width:, :width] - drop(terms[1, width:, :width])
        near, far = dv[0] - terms[0, :width, width:], -terms[1, :width, width:]
        pivot_out[:width, :] = pick(far, near)
        outer_out[...] = pick(near, outer_out[...])
        near, far = av[0] - terms[0, width:, width:], -terms[1, width:, width:]
        pivot_out[width : width + tip, :] = pick(far, near)
        pack_out[width : width + tip, :] = pick(near, av[3])
        pivot_out[width + tip :, :] = jnp.zeros((tip, width), F32)
        pivot_out[width + tip :, :tip] = -update(first, *tt) - drop(update(third, *tt))

    second = (pivot, ga, gh.at[0], gl.at[0], zh.at[0], zl.at[0], pa, ra)
    eliminate([second], [work], rest, fronts)
    pivot_out[:width, :] = pivot_out[:width, :] - update(second, width, width, width, width)
    pack_out[:width, :] = -update(second, 0, width, width, width)
    outer_out[...] = outer_out[...] - update(second, 0, width, 0, width)
    at = pl.ds(width, tip)
    pivot_out[at, :] = pivot_out[at, :] - update(second, two, tip, width, width)
    pack_out[at, :] = pack_out[at, :] - update(second, two, tip, 0, width)
    at = pl.ds(width + tip, tip)
    pivot_out[at, :tip] = pivot_out[at, :tip] - update(second, *tt)
    spill = pack_out.shape[0] - width - tip
    pack_out[width + tip :, :] = outer_out[:spill, :]


def invert_512(pivot, work):
    scale = equilibrate(pivot)
    (first,) = invert_256([quarters(pivot[:HALF, :HALF])], [work], unroll=7)
    right = split(pivot[:HALF, HALF:])
    below = split(pivot[HALF:, :HALF])
    upper = split(first)
    low = split(dot3(below, upper))
    high = split(dot3(upper, right))
    last = pivot[HALF:, HALF:] - dot3(low, right)
    (second,) = invert_256([quarters(last)], [work], unroll=7)
    corner = split(second)
    below = dot3(corner, low)
    pivot[:HALF, :HALF] = first + dot3(high, split(below))
    pivot[:HALF, HALF:] = -dot3(high, corner)
    pivot[HALF:, :HALF] = -below
    pivot[HALF:, HALF:] = second
    for start in range(0, pivot.shape[0], LANES):
        rows = pl.ds(start, LANES)
        down = jnp.broadcast_to(scale[:, start : start + LANES], (LANES, LANES)).T
        for lanes in range(0, pivot.shape[0], LANES):
            across = scale[:, lanes : lanes + LANES]
            lanes = pl.ds(lanes, LANES)
            pivot[rows, lanes] = pivot[rows, lanes] * down * across


def factor_kernel(mine, other, inverse, tip_out, work):
    width, tip = inverse.shape[0], tip_out.shape[0]
    inverse[...] = mine[:width, :] + other[:width, :]
    invert_512(inverse, work)
    at = pl.ds(width, tip)
    coupling = split(mine[at, :] + other[at, :])
    solved = split(dot3(coupling, split(inverse[...])))
    at = pl.ds(width + tip, tip)
    tip_out[...] = mine[at, :tip] + other[at, :tip] - dot3(solved, coupling, NT)


def merge_kernel(
    start, side, inverse, pivot_mine, pivot_other, pack_mine, pack_other, outer_mine, *refs
):
    merged, gh, gl, out, sem = refs[-5:]
    width = inverse.shape[0]
    tip = (pivot_mine.shape[0] - width) // 2
    two = 2 * width
    half = (two + tip) // 2
    spill = half - width
    count = out.shape[0]
    is_left = side[0] == 0
    for row, size in chunks(width):
        rows = pl.ds(row, size)
        mine, other = split(pack_mine[rows, :]), split(pack_other[rows, :])
        gh[rows, :] = jnp.where(is_left, mine[0], other[0])
        gl[rows, :] = jnp.where(is_left, mine[1], other[1])
        rows = pl.ds(width + row, size)
        gh[rows, :] = jnp.where(is_left, other[0], mine[0])
        gl[rows, :] = jnp.where(is_left, other[1], mine[1])
    at = pl.ds(width, tip)
    gh[two:, :], gl[two:, :] = split(pivot_mine[at, :] + pivot_other[at, :])
    outer_tip = pl.ds(width, tip)

    @pl.when(is_left)
    def _():
        size = min(count, width - start)
        out[:size, :width] = outer_mine[start : start + size, :]
        out[:size, width:two] = jnp.zeros((size, width), F32)
        out[:size, two:] = pack_mine[outer_tip, start : start + size].T
        if size < count:
            out[size:, :width] = jnp.zeros((spill, width), F32)
            out[size:, width:two] = pack_other[width + tip :, :]
            out[size:, two:] = pack_other[outer_tip, :LANES].T[:spill, :]

    @pl.when(jnp.logical_not(is_left))
    def _():
        size = min(count, half - tip - start)
        first = start + spill
        out[:size, :width] = jnp.zeros((size, width), F32)
        out[:size, width:two] = outer_mine[first : first + size, :]
        out[:size, two:] = pack_mine[outer_tip, :].T[first : first + size, :]
        if size < count:
            out[size:, :width] = pack_other[outer_tip, :]
            out[size:, width:two] = pack_mine[outer_tip, :]
            at = pl.ds(width + tip, tip)
            out[size:, two:] = pivot_mine[at, :tip] + pivot_other[at, :tip]

    rows = pl.ds(pl.multiple_of(side[0] * half + start, PAIR), count)
    solved = split(dot3((gh[rows, :], gl[rows, :]), split(inverse[...])))
    for lanes in (pl.ds(0, two), pl.ds(two, tip)):
        out[:, lanes] = out[:, lanes] - dot3(solved, (gh[lanes, :], gl[lanes, :]), NT)
    copy = pltpu.make_async_copy(out, merged.at[pl.ds(start, count), :], sem)
    copy.start()
    copy.wait()


def swapped(value, axis, mask):
    count = lax.axis_size(axis)
    return lax.ppermute(value, axis, [(k, k ^ mask) for k in range(count)])


def sum_over_pairs(value, axis):
    step = 2
    while step < lax.axis_size(axis):
        if 2 * step < lax.axis_size(axis):
            near, far, across = (swapped(value, axis, step * k) for k in (1, 2, 3))
            value = (value + near) + (far + across)
            step *= 4
        else:
            value = value + swapped(value, axis, step)
            step *= 2
    return value


def local(diag_blocks, lower_blocks, arrow_blocks, tip_block):
    count, width = diag_blocks.shape[:2]
    tip = arrow_blocks.shape[1]
    front = 2 * width + tip
    half = front // 2
    spill = half - width
    side = (lax.axis_index("tm") % 2).astype(jnp.int32).reshape(1)
    smem = pl.BlockSpec(memory_space=pltpu.SMEM)
    vmem = pl.BlockSpec(memory_space=pltpu.VMEM)
    parts = [pltpu.VMEM((front, width), BF16)] * 4
    params = pltpu.CompilerParams(vmem_limit_bytes=56 * 2**20)
    pivot, pack, outer = pl.pallas_call(
        front_kernel,
        out_shape=[
            jax.ShapeDtypeStruct((width + 2 * tip, width), F32),
            jax.ShapeDtypeStruct((width + tip + spill, width), F32),
            jax.ShapeDtypeStruct((width, width), F32),
        ],
        in_specs=[smem] + [pl.BlockSpec(memory_space=pl.ANY)] * 3,
        out_specs=[vmem] * 3,
        scratch_shapes=[
            pltpu.VMEM((count, width, width), F32),
            pltpu.VMEM((count, width, width), F32),
            pltpu.VMEM((count, tip, width), F32),
        ]
        + [pltpu.VMEM((front, width), F32)] * 2
        + [pltpu.VMEM((2, front, width), BF16)] * 4
        + [pltpu.VMEM((4, HALF, HALF), BF16)] * 2
        + [pltpu.VMEM((1, width), F32)] * 2
        + [pltpu.VMEM((width, width), F32), pltpu.VMEM((2, width + tip, 2 * width), F32)]
        + [pltpu.VMEM((LANES, LANES), F32)] * 2
        + [pltpu.SemaphoreType.DMA((3 * count,))],
        compiler_params=params,
        name="front",
    )(side, diag_blocks, lower_blocks, arrow_blocks)
    pivot_other = swapped(pivot, "tm", 1)
    pack_other = swapped(pack, "tm", 1)
    inverse, tip_tip = pl.pallas_call(
        factor_kernel,
        out_shape=[
            jax.ShapeDtypeStruct((width, width), F32),
            jax.ShapeDtypeStruct((tip, tip), F32),
        ],
        in_specs=[vmem] * 2,
        out_specs=[vmem] * 2,
        scratch_shapes=[pltpu.VMEM((LANES, LANES), F32)],
        compiler_params=pltpu.CompilerParams(vmem_limit_bytes=24 * 2**20),
        cost_estimate=pl.CostEstimate(flops=10**10, bytes_accessed=10**7, transcendentals=0),
        name="factor",
    )(pivot, pivot_other)
    operands = [side, inverse, pivot, pivot_other, pack, pack_other, outer]
    anywhere = pl.BlockSpec(memory_space=pl.ANY)
    for start, size in ((0, HALF), (HALF, half - HALF)):
        merged = pl.pallas_call(
            functools.partial(merge_kernel, start),
            out_shape=jax.ShapeDtypeStruct((half, front), F32),
            in_specs=[smem] + [vmem] * 6 + [anywhere] * (start > 0),
            out_specs=anywhere,
            scratch_shapes=parts[:2] + [pltpu.VMEM((size, front), F32), pltpu.SemaphoreType.DMA],
            input_output_aliases={7: 0} if start else {},
            compiler_params=pltpu.CompilerParams(vmem_limit_bytes=40 * 2**20),
            cost_estimate=pl.CostEstimate(flops=10**10, bytes_accessed=10**7, transcendentals=0),
            name="merge",
        )(*operands)
        operands.append(merged)
    return merged, tip_block + sum_over_pairs(tip_tip, "tm")


def solution(mesh):
    placed = (P("tm", None, None), P("tm", None, None), P("tm", None, None), P())
    return jax.shard_map(
        local, mesh=mesh, in_specs=placed, out_specs=(P("tm", None), P()), check_vma=False
    )
```
